32 devices in a mesh: grp: 8 (over z, y), seq: 4 (over x, core).
Axes of the slice: x: 2, y: 2, z: 4, core: 2. Of those that a mesh axis runs over, the one named last changes fastest.
Arguments:
- tokens_in: bfloat16 [24576, 768], P(('grp', 'seq')), may hold values from -6 to 6
- lengths: int32 [8], P('grp'), may hold values from 2305 to 3072, as said below
- ln1_gain: float32 [768], replicated, may hold values from 0.5 to 1.5
- ln1_bias: float32 [768], replicated, may hold values from -1.75 to 1.75
- w_qkv: bfloat16 [768, 2304], replicated, may hold values from -0.21875 to 0.21875
- bias_query: float32 [768], replicated, may hold values from -1.75 to 1.75
- bias_value: float32 [768], replicated, may hold values from -1.75 to 1.75
- w_out: bfloat16 [768, 768], replicated, may hold values from -0.875 to 0.875
- bias_out: float32 [768], replicated, may hold values from -1.75 to 1.75
- ln2_gain: float32 [768], replicated, may hold values from 0.5 to 1.5
- ln2_bias: float32 [768], replicated, may hold values from -1.75 to 1.75
- w_up: bfloat16 [768, 3072], replicated, may hold values from -0.21875 to 0.21875
- bias_up: float32 [3072], replicated, may hold values from -1.75 to 1.75
- w_down: bfloat16 [3072, 768], replicated, may hold values from -0.109375 to 0.109375
- bias_down: float32 [768], replicated, may hold values from -1.75 to 1.75
- proj_patch: bfloat16 [768, 768], replicated, may hold values from -0.21875 to 0.21875
- proj_class: bfloat16 [768, 768], replicated, may hold values from -0.21875 to 0.21875
- class_emb: bfloat16 [150, 768], replicated, may hold values from -6 to 6
- d_masks: bfloat16 [24576, 150], P(('grp', 'seq')), may hold values from -6 to 6
Outputs:
- masks: bfloat16 [24576, 150], P(('grp', 'seq'))
- grad_tokens: bfloat16 [24576, 768], P(('grp', 'seq'))
- grad_ln1_gain: float32 [768], P('grp')
- grad_ln1_bias: float32 [768], P('grp')
- grad_w_qkv: float32 [768, 2304], P('grp', 'seq')
- grad_bias_query: float32 [768], P('grp')
- grad_bias_value: float32 [768], P('grp')
- grad_w_out: float32 [768, 768], P('grp', 'seq')
- grad_bias_out: float32 [768], P('grp')
- grad_ln2_gain: float32 [768], P('grp')
- grad_ln2_bias: float32 [768], P('grp')
- grad_w_up: float32 [768, 3072], P('grp', 'seq')
- grad_bias_up: float32 [3072], P('grp')
- grad_w_down: float32 [3072, 768], P('grp', 'seq')
- grad_bias_down: float32 [768], P('grp')
- grad_proj_patch: float32 [768, 768], P('grp', 'seq')
- grad_proj_class: float32 [768, 768], P('grp', 'seq')
- grad_class_emb: float32 [150, 768], P(None, 'grp')
The draws below stay inside these ranges and needn't reach their ends.
Inputs may be any that keep to these rules, and one draw needn't show every extreme that they name: Image g fills the first lengths[g] rows of its 3072 rows, the rest is padding; in every draw some image has exactly 3072 rows.
All inputs are finite; a program needn't handle non-finite values.
Results may differ from the reference program's by a relative error of at most 0.015.
Values may be sent and summed in bfloat16 or wider, within the bound.
A program may use at most 256 MiB of HBM per device.

```python
import math
import jax
import jax.numpy as jnp
from jax import lax

D = 768
HEAD_DIM = 64
FF = 3072
NCLS = 150
TOK_DEV = 768
SEQ_LEN = 3072
IMAGES = 8
TOKENS = 24576


def draw_lengths(key, part):
    first_key = jax.random.fold_in(key, 11)
    second_key = jax.random.fold_in(key, 12)
    drawn_len = jax.random.randint(first_key, (IMAGES,), SEQ_LEN - TOK_DEV + 1, SEQ_LEN + 1, dtype=jnp.int32)
    full_index = jax.random.randint(second_key, (), 0, IMAGES, dtype=jnp.int32)
    positions = jnp.arange(IMAGES, dtype=jnp.int32)
    return jnp.where(positions == full_index, SEQ_LEN, drawn_len).astype(jnp.int32)


def steps_of(own_key, dims, split, smallest, high):
    def one(dim, parts):
        steps = jax.random.uniform(jax.random.fold_in(jax.random.fold_in(own_key, 6), dim), (parts,), jnp.float32, smallest / len(split), high / len(split))
        return jnp.repeat(jnp.exp(steps), dims[dim] // parts).reshape((-1,) + (1,) * (len(dims) - dim - 1))

    loudness = one(*split[0])
    for cut in split[1:]:
        loudness = loudness * one(*cut)
    return loudness


def noise(rng, dims, deviation, reach, shards=(), held_as=jnp.bfloat16):
    factor_of = steps_of(rng, dims, shards, -0.22, 0.18) if shards else 1.0
    values = jax.random.normal(rng, dims, jnp.float32) * deviation * factor_of
    return jnp.minimum(jnp.maximum(values, -reach), reach).astype(held_as)


def setup_inputs(seed: int = 0) -> dict:
    splits = jax.random.split(jax.random.key(seed), 20)
    tokens_in = noise(splits[0], (TOKENS, D), 1.0, 6.0, ((0, 32),))
    lengths = draw_lengths(jax.random.fold_in(splits[19], 71), 0)
    ln1_gain = jnp.clip(1.0 + 0.1 * jax.random.normal(splits[2], (D,), jnp.float32), 0.5, 1.5)
    ln1_bias = noise(splits[3], (D,), 0.3, 1.75, (), jnp.float32)
    w_qkv = noise(splits[4], (D, 3 * D), D ** -0.5, 0.21875)
    bias_query = noise(splits[5], (D,), 0.3, 1.75, (), jnp.float32)
    bias_value = noise(splits[6], (D,), 0.3, 1.75, (), jnp.float32)
    w_out = noise(splits[7], (D, D), (max(1, D // 16)) ** -0.5, 0.875)
    bias_out = noise(splits[8], (D,), 0.3, 1.75, (), jnp.float32)
    ln2_gain = jnp.clip(1.0 + 0.1 * jax.random.normal(splits[9], (D,), jnp.float32), 0.5, 1.5)
    ln2_bias = noise(splits[10], (D,), 0.3, 1.75, (), jnp.float32)
    w_up = noise(splits[11], (D, FF), D ** -0.5, 0.21875)
    bias_up = noise(splits[12], (FF,), 0.3, 1.75, (), jnp.float32)
    w_down = noise(splits[13], (FF, D), FF ** -0.5, 0.109375)
    bias_down = noise(splits[14], (D,), 0.3, 1.75, (), jnp.float32)
    proj_patch = noise(splits[15], (D, D), D ** -0.5, 0.21875)
    proj_class = noise(splits[16], (D, D), D ** -0.5, 0.21875)
    class_emb = noise(splits[17], (NCLS, D), 1.0, 6.0)
    d_masks = noise(splits[18], (TOKENS, NCLS), 1.0, 6.0, ((0, 32),))
    return dict(tokens_in=tokens_in, lengths=lengths, ln1_gain=ln1_gain, ln1_bias=ln1_bias, w_qkv=w_qkv, bias_query=bias_query, bias_value=bias_value, w_out=w_out, bias_out=bias_out, ln2_gain=ln2_gain, ln2_bias=ln2_bias, w_up=w_up, bias_up=bias_up, w_down=w_down, bias_down=bias_down, proj_patch=proj_patch, proj_class=proj_class, class_emb=class_emb, d_masks=d_masks)


EPS_NORM = 1e-06
EPS_UNIT = 1e-06

@jax.custom_vjp
def low(v):
    return lax.optimization_barrier(v.astype(jnp.bfloat16)).astype(jnp.float32)

@jax.custom_vjp
def low_back(v):
    return v

def low_keep(v):
    return (low(v), None)

def low_pass(kept, grad):
    return (grad,)

def back_keep(v):
    return (v, None)

def back_low(kept, grad):
    return (low(grad),)
low.defvjp(low_keep, low_pass)
low_back.defvjp(back_keep, back_low)

def matmul(left, right):
    return jnp.dot(left, right, precision=lax.Precision.HIGHEST, preferred_element_type=jnp.float32)

def layer_norm(matrix_rows, gain_vec, shift_vec):
    row_mean = lax.optimization_barrier(jnp.mean(matrix_rows, axis=-1, keepdims=True))
    centred = matrix_rows - row_mean
    row_var = lax.optimization_barrier(jnp.mean(centred * centred, axis=-1, keepdims=True))
    return centred * lax.rsqrt(row_var + EPS_NORM) * gain_vec + shift_vec

def unit_rows(matrix_rows):
    return matrix_rows * lax.rsqrt(lax.optimization_barrier(jnp.sum(matrix_rows * matrix_rows, axis=-1, keepdims=True)) + EPS_UNIT)

def attend(queries, key_rows, value_rows, lengths):
    images = lengths.shape[0]
    model_width = queries.shape[1]
    head_count = model_width // HEAD_DIM
    shaped = (images, SEQ_LEN, head_count, HEAD_DIM)
    score_scale = HEAD_DIM ** (-0.5)

    def one_image(pieces):
        query_all, key_all, value_all, length_now = pieces
        key_keep = jnp.arange(SEQ_LEN, dtype=jnp.int32) < length_now
        query_blocks = query_all.reshape(SEQ_LEN // TOK_DEV, TOK_DEV, head_count, HEAD_DIM)

        def one_block(query_block):
            scores = jnp.einsum('qhd,khd->hqk', query_block, key_all, precision=lax.Precision.HIGHEST) * score_scale
            scores = low_back(scores)
            scores = jnp.where(key_keep[None, None, :], scores, -1e+30)
            weights_p = low(jax.nn.softmax(scores, axis=-1))
            return jnp.einsum('hqk,khd->qhd', weights_p, value_all, precision=lax.Precision.HIGHEST)
        return lax.map(jax.checkpoint(one_block), query_blocks).reshape(SEQ_LEN, model_width)
    joined = lax.map(one_image, (queries.reshape(shaped), key_rows.reshape(shaped), value_rows.reshape(shaped), lengths))
    return joined.reshape(images * SEQ_LEN, model_width)

def forward(tokens, ln1_gain, ln1_bias, w_qkv, bias_query, bias_value, w_out, bias_out, ln2_gain, ln2_bias, w_up, bias_up, w_down, bias_down, proj_patch, proj_class, class_emb, lengths, valid_rows):
    model_width = tokens.shape[1]
    normed_one = low(layer_norm(tokens, ln1_gain, ln1_bias))
    zero_keys = jnp.zeros_like(bias_query)
    mixed = matmul(normed_one, w_qkv) + jnp.concatenate([bias_query, zero_keys, bias_value])
    mixed = low_back(low(mixed))
    queries = mixed[:, :model_width]
    key_rows = mixed[:, model_width:2 * model_width]
    value_rows = mixed[:, 2 * model_width:]
    attended = low_back(low(attend(queries, key_rows, value_rows, lengths)))
    branch = low_back(matmul(attended, w_out) + bias_out)
    middle = tokens + branch
    normed_two = low(layer_norm(middle, ln2_gain, ln2_bias))
    hidden = low_back(matmul(normed_two, w_up) + bias_up)
    active = low(jax.nn.gelu(hidden, approximate=False))
    feed = low_back(matmul(active, w_down) + bias_down)
    final = middle + feed
    patches = low_back(matmul(low(final), proj_patch))
    classes = low_back(matmul(class_emb, proj_class))
    patch_unit = low(unit_rows(patches))
    class_unit = low(unit_rows(classes))
    return matmul(patch_unit, class_unit.T) * math.sqrt(model_width) * valid_rows[:, None]

def reference(tokens_in, lengths, ln1_gain, ln1_bias, w_qkv, bias_query, bias_value, w_out, bias_out, ln2_gain, ln2_bias, w_up, bias_up, w_down, bias_down, proj_patch, proj_class, class_emb, d_masks):
    positions = jnp.arange(SEQ_LEN, dtype=jnp.int32)
    valid_rows = (positions[None, :] < lengths[:, None]).reshape(-1).astype(jnp.float32)
    params = (tokens_in, ln1_gain, ln1_bias, w_qkv, bias_query, bias_value, w_out, bias_out, ln2_gain, ln2_bias, w_up, bias_up, w_down, bias_down, proj_patch, proj_class, class_emb)
    params = tuple((item.astype(jnp.float32) for item in params))

    def forward_run(*inputs):
        return forward(*inputs, lengths, valid_rows)
    mask_out, pullback = jax.vjp(forward_run, *params)
    gradients = pullback(d_masks.astype(jnp.float32))
    return (mask_out.astype(jnp.bfloat16), gradients[0].astype(jnp.bfloat16), gradients[1], gradients[2], gradients[3], gradients[4], gradients[5], gradients[6], gradients[7], gradients[8], gradients[9], gradients[10], gradients[11], gradients[12], gradients[13], gradients[14], gradients[15], gradients[16])
```

```python
import functools
import math

import jax
import jax.numpy as jnp
from jax import lax
from jax.experimental import pallas as pl
from jax.experimental.pallas import tpu as pltpu
from jax.sharding import PartitionSpec as P

HEAD_DIM = 64
LANES = 128
EPS_NORM = 1e-06
EPS_UNIT = 1e-06
NEG_FILL = -1e30
LOG2E = math.log2(math.e)
F32 = jnp.float32
BF16 = jnp.bfloat16
MIB = 1 << 20


def dot_nn(a, b):
    return lax.dot_general(a, b, (((1,), (0,)), ((), ())), preferred_element_type=F32)


def dot_nt(a, b):
    return lax.dot_general(a, b, (((1,), (1,)), ((), ())), preferred_element_type=F32)


def dot_tn(a, b):
    return lax.dot_general(a, b, (((0,), (0,)), ((), ())), preferred_element_type=F32)


def attend_forward_kernel(q_ref, k_ref, v_ref, out_ref, mass_ref):
    scores = dot_nt(k_ref[...], q_ref[...])
    top = jnp.max(scores, axis=0, keepdims=True)
    prob = jnp.exp2((scores - top) * LOG2E).astype(BF16)
    summed = dot_tn(v_ref[...], prob)
    total = summed[HEAD_DIM : HEAD_DIM + 1]
    out_ref[...] = (summed[:HEAD_DIM] / total).astype(BF16)
    mass_ref[0] = top * LOG2E + jnp.log2(total)


def attend_forward(queries, keys, values):
    rows, width = queries.shape
    span = keys.shape[0]
    heads = width // LANES
    tile = rows // 2
    return pl.pallas_call(
        attend_forward_kernel,
        grid=(heads, 2),
        in_specs=[
            pl.BlockSpec((tile, LANES), lambda h, i: (i, h)),
            pl.BlockSpec((span, LANES), lambda h, i: (0, h)),
            pl.BlockSpec((span, LANES), lambda h, i: (0, h)),
        ],
        out_specs=[
            pl.BlockSpec((HEAD_DIM, tile), lambda h, i: (h, i)),
            pl.BlockSpec((1, 1, tile), lambda h, i: (h, 0, i)),
        ],
        out_shape=[
            jax.ShapeDtypeStruct((heads * HEAD_DIM, rows), BF16),
            jax.ShapeDtypeStruct((heads, 1, rows), F32),
        ],
        compiler_params=pltpu.CompilerParams(vmem_limit_bytes=50 * MIB),
        cost_estimate=pl.CostEstimate(
            flops=8 * heads * rows * span * LANES,
            bytes_accessed=(rows + 2 * span) * width * 2,
            transcendentals=heads * rows * span,
        ),
        name="attend_forward",
    )(queries, keys, values)


def attend_backward_kernel(
    q_ref,
    gout_ref,
    out_ref,
    mass_ref,
    k_ref,
    v_ref,
    gq_ref,
    gkv_ref,
    q_t,
    q_clean,
    gout_t,
    delta,
    gq_sum,
):
    step = pl.program_id(1)

    @pl.when(step == 0)
    def _():
        q_now = q_ref[...]
        column = lax.broadcasted_iota(jnp.int32, q_now.shape, 1)
        q_t[...] = q_now.T
        q_clean[...] = jnp.where(column < HEAD_DIM, jnp.zeros_like(q_now), q_now)
        turned = gout_ref[...].T
        gout_t[...] = turned
        delta[...] = jnp.sum(
            turned[:HEAD_DIM].astype(F32) * out_ref[...].astype(F32), axis=0, keepdims=True
        )

    key_now = k_ref[...]
    scores = dot_nn(key_now, q_t[...])
    prob = jnp.exp2(scores * LOG2E - mass_ref[0])
    gprob = dot_nn(v_ref[...], gout_t[...])
    gscore = (prob * (gprob - delta[...])).astype(BF16)
    gkv_ref[...] = (
        dot_nn(prob.astype(BF16), gout_ref[...]) + dot_nn(gscore, q_clean[...])
    ).astype(BF16)
    part = dot_tn(key_now, gscore)

    @pl.when(step == 0)
    def _():
        gq_sum[...] = part

    @pl.when(step > 0)
    def _():
        gq_sum[...] += part

    @pl.when(step == pl.num_programs(1) - 1)
    def _():
        gq_ref[...] = (gq_sum[HEAD_DIM:] * HEAD_DIM**-0.5).astype(BF16)


def attend_backward(queries, gouts, outs_t, mass, keys, values):
    rows, width = queries.shape
    span = keys.shape[0]
    heads = width // LANES
    tile = min(1024, span)
    return pl.pallas_call(
        attend_backward_kernel,
        grid=(heads, span // tile),
        in_specs=[
            pl.BlockSpec((rows, LANES), lambda h, j: (0, h)),
            pl.BlockSpec((rows, LANES), lambda h, j: (0, h)),
            pl.BlockSpec((HEAD_DIM, rows), lambda h, j: (h, 0)),
            pl.BlockSpec((1, 1, rows), lambda h, j: (h, 0, 0)),
            pl.BlockSpec((tile, LANES), lambda h, j: (j, h)),
            pl.BlockSpec((tile, LANES), lambda h, j: (j, h)),
        ],
        out_specs=[
            pl.BlockSpec((HEAD_DIM, rows), lambda h, j: (h, 0)),
            pl.BlockSpec((tile, LANES), lambda h, j: (j, h)),
        ],
        out_shape=[
            jax.ShapeDtypeStruct((heads * HEAD_DIM, rows), BF16),
            jax.ShapeDtypeStruct((span, width), BF16),
        ],
        scratch_shapes=[
            pltpu.VMEM((LANES, rows), BF16),
            pltpu.VMEM((rows, LANES), BF16),
            pltpu.VMEM((LANES, rows), BF16),
            pltpu.VMEM((1, rows), F32),
            pltpu.VMEM((LANES, rows), F32),
        ],
        compiler_params=pltpu.CompilerParams(vmem_limit_bytes=56 * MIB),
        cost_estimate=pl.CostEstimate(
            flops=20 * heads * rows * span * LANES,
            bytes_accessed=(2 * rows + 3 * span) * width * 2,
            transcendentals=heads * rows * span,
        ),
        name="attend_backward",
    )(queries, gouts, outs_t, mass, keys, values)


def layer_norm(matrix_rows, gain_vec, shift_vec):
    row_mean = jnp.mean(matrix_rows, axis=-1, keepdims=True)
    centred = matrix_rows - row_mean
    row_var = jnp.mean(centred * centred, axis=-1, keepdims=True)
    return centred * lax.rsqrt(row_var + EPS_NORM) * gain_vec + shift_vec


def unit_rows(matrix_rows):
    return matrix_rows * lax.rsqrt(
        jnp.sum(matrix_rows * matrix_rows, axis=-1, keepdims=True) + EPS_UNIT
    )


def gelu_exact(values_in):
    return jax.nn.gelu(values_in, approximate=False)


def column_sum(matrix_low):
    return jnp.sum(matrix_low.astype(F32), axis=0)


def swap(value, axis, bit):
    size = lax.axis_size(axis)
    return lax.ppermute(value, axis, [(i, i ^ bit) for i in range(size)])


def row_steps(part, names):
    groups = lax.axis_size("grp")
    bits = groups.bit_length() - 1
    here = lax.axis_index("grp")
    for name in names:
        axis = bits - 1 - name
        mine = (here >> name) & 1
        send = lax.dynamic_index_in_dim(part, 1 - mine, axis, keepdims=True)
        keep = lax.dynamic_index_in_dim(part, mine, axis, keepdims=True)
        got = swap(send, "grp", 1 << name)
        part = (keep.astype(F32) + got.astype(F32)).astype(BF16)
    return part


def split_rows(part):
    groups = lax.axis_size("grp")
    bits = groups.bit_length() - 1
    return part.reshape((2,) * bits + (part.shape[0] // groups, part.shape[1]))


def join_rows(part):
    return part.reshape(part.shape[-2], part.shape[-1])


def scatter_weight(keep, send, order):
    got = swap(send, "seq", 1)
    part = (keep.astype(F32) + got.astype(F32)).astype(BF16)
    half = part.shape[1] // 2
    return scatter_chip(part[:, :half], part[:, half:], order)


def scatter_chip(mine, other, order):
    mine, other = split_rows(mine), split_rows(other)
    for at, name in enumerate(order):
        if name == "x":
            got = swap(other, "seq", 2)
            mine = (mine.astype(F32) + got.astype(F32)).astype(BF16)
            other = None
        elif other is None:
            mine = row_steps(mine, [name])
        else:
            both = row_steps(jnp.concatenate([mine, other], axis=-1), [name])
            half = both.shape[-1] // 2
            mine, other = both[..., :half], both[..., half:]
    return join_rows(mine).astype(F32)


def column_blocks(matrix, seq_here):
    width = matrix.shape[1] // 4

    def block(index):
        return lax.dynamic_slice_in_dim(matrix, index * width, width, 1)

    keep = jnp.concatenate([block(seq_here), block(seq_here ^ 2)], axis=1)
    send = jnp.concatenate([block(seq_here ^ 1), block(seq_here ^ 3)], axis=1)
    return keep, send


def weight_grad(rows_left, rows_right, seq_here, order):
    keep, send = column_blocks(rows_right, seq_here)
    return scatter_weight(
        dot_tn(rows_left, keep).astype(BF16), dot_tn(rows_left, send).astype(BF16), order
    )


def body(
    tokens_in,
    lengths,
    ln1_gain,
    ln1_bias,
    w_qkv,
    bias_query,
    bias_value,
    w_out,
    bias_out,
    ln2_gain,
    ln2_bias,
    w_up,
    bias_up,
    w_down,
    bias_down,
    proj_patch,
    proj_class,
    class_emb,
    d_masks,
):
    row_count, model_width = tokens_in.shape
    head_count = model_width // HEAD_DIM
    heads_here = head_count // 2
    third = model_width // 4
    seq_devices = lax.axis_size("seq")
    grp_devices = lax.axis_size("grp")
    mask_scale = math.sqrt(model_width)
    seq_here = lax.axis_index("seq")
    grp_here = lax.axis_index("grp")
    core = seq_here & 1
    length_here = lengths[0]
    bits = grp_devices.bit_length() - 1
    order_a = ["x"] + list(range(bits))
    order_b = [0, "x"] + list(range(1, bits))
    order_c = list(range(1, bits)) + ["x", 0]

    tokens_x = swap(tokens_in, "seq", 2)
    tokens_c = swap(tokens_in, "seq", 1)
    tokens_xc = swap(tokens_x, "seq", 1)
    image_rows = jnp.concatenate([tokens_in, tokens_c, tokens_x, tokens_xc], axis=0)
    within = jnp.arange(row_count, dtype=jnp.int32)
    positions = jnp.concatenate(
        [(seq_here ^ block) * row_count + within for block in range(seq_devices)]
    )
    key_keep = positions < length_here
    valid_rows = key_keep[:row_count].astype(F32)

    tokens = tokens_in.astype(F32)
    normed_image = layer_norm(image_rows.astype(F32), ln1_gain, ln1_bias).astype(BF16)
    norm_one_back = jax.vjp(layer_norm, tokens, ln1_gain, ln1_bias)[1]

    def own_heads(matrix):
        parts = matrix.reshape(matrix.shape[:-1] + (2, 2, third))
        parts = lax.dynamic_index_in_dim(parts, core, parts.ndim - 2, keepdims=False)
        return parts.reshape(matrix.shape[:-1] + (heads_here, HEAD_DIM))

    def low_half(matrix):
        return jnp.concatenate([matrix, jnp.zeros_like(matrix)], axis=-1)

    def high_half(matrix):
        return jnp.concatenate([jnp.zeros_like(matrix), matrix], axis=-1)

    def flat(matrix):
        return matrix.reshape(matrix.shape[:-2] + (heads_here * LANES,))

    wq = own_heads(w_qkv[:, :model_width])
    wk = own_heads(w_qkv[:, model_width : 2 * model_width])
    wv = own_heads(w_qkv[:, 2 * model_width :])
    column = jnp.arange(heads_here * LANES, dtype=jnp.int32) % LANES
    query_rows = (
        dot_nn(normed_image[: 2 * row_count], flat(high_half(wq)))
        + flat(high_half(own_heads(bias_query)))
    ).astype(BF16)
    query_rows = jnp.where(column == 0, 1.0, query_rows * HEAD_DIM**-0.5).astype(BF16)
    key_rows = dot_nn(normed_image, flat(high_half(wk))).astype(BF16)
    key_rows = jnp.where(
        column == 0, jnp.where(key_keep, 0.0, NEG_FILL)[:, None], key_rows
    ).astype(BF16)
    value_rows = (
        dot_nn(normed_image, flat(low_half(wv)))
        + flat(low_half(own_heads(bias_value)))
        + (column == HEAD_DIM).astype(F32)
    ).astype(BF16)

    att_t, mass = attend_forward(query_rows, key_rows, value_rows)
    att_got = swap(att_t[:, row_count:], "seq", 1)
    att_own = att_t[:, :row_count].reshape(2, third, row_count)
    att_got = att_got.reshape(2, third, row_count)
    first = jnp.where(core == 0, att_own, att_got)
    second = jnp.where(core == 0, att_got, att_own)
    attended_t = jnp.stack([first, second], axis=1).reshape(model_width, row_count)

    branch = dot_tn(attended_t, w_out) + bias_out
    middle = tokens + branch
    normed_two, norm_two_back = jax.vjp(layer_norm, middle, ln2_gain, ln2_bias)
    normed_two_low = normed_two.astype(BF16)
    hidden = dot_nn(normed_two_low, w_up) + bias_up
    active, gelu_back = jax.vjp(gelu_exact, hidden)
    active_low = active.astype(BF16)
    final = middle + (dot_nn(active_low, w_down) + bias_down)
    final_low = final.astype(BF16)
    patches = dot_nn(final_low, proj_patch)
    patch_unit, patch_back = jax.vjp(unit_rows, patches)
    patch_low = patch_unit.astype(BF16)
    classes = dot_nn(class_emb, proj_class)
    class_unit, class_back = jax.vjp(unit_rows, classes)
    class_low = class_unit.astype(BF16)
    mask_out = (dot_nt(patch_low, class_low) * mask_scale * valid_rows[:, None]).astype(BF16)
    mask_grad = (d_masks.astype(F32) * valid_rows[:, None]).astype(BF16)
    grad_patch_unit = dot_nn(mask_grad, class_low) * mask_scale
    class_part = dot_tn(mask_grad, patch_low) * mask_scale
    class_total = lax.psum(class_part, ("grp", "seq"))
    grad_classes = class_back(class_total)[0].astype(BF16)
    grad_patches = patch_back(grad_patch_unit)[0].astype(BF16)
    grad_final = dot_nt(grad_patches, proj_patch)
    grad_feed = grad_final.astype(BF16)
    grad_bias_down = column_sum(grad_feed)
    out_w_down = weight_grad(active_low, grad_feed, seq_here, order_a)
    out_proj_patch = weight_grad(final_low, grad_patches, seq_here, order_c)
    grad_active = dot_nt(grad_feed, w_down)
    grad_hidden = gelu_back(grad_active)[0].astype(BF16)
    out_w_up = weight_grad(normed_two_low, grad_hidden, seq_here, order_b)
    grad_bias_up = column_sum(grad_hidden)
    grad_normed_two = dot_nt(grad_hidden, w_up)
    grad_middle_norm, grad_ln2_gain, grad_ln2_bias = norm_two_back(grad_normed_two)
    grad_middle = grad_final + grad_middle_norm
    grad_branch = grad_middle.astype(BF16)
    out_w_out = weight_grad(attended_t.T, grad_branch, seq_here, order_c)
    grad_bias_out = column_sum(grad_branch)

    branch_got = swap(grad_branch, "seq", 1)
    branch_rows = jnp.concatenate([grad_branch, branch_got], axis=0)
    wo = own_heads(w_out.T)
    gout_rows = dot_nn(branch_rows, flat(low_half(wo))).astype(BF16)
    gq_t, gkv = attend_backward(query_rows, gout_rows, att_t, mass, key_rows, value_rows)

    w_pairs = flat(jnp.concatenate([wv, wk], axis=-1))
    w_query = wq.reshape(model_width, heads_here * HEAD_DIM)
    gq = gq_t.T
    gn_far = dot_nt(gkv[2 * row_count :], w_pairs)
    gn_near = dot_nt(gkv[: 2 * row_count], w_pairs) + dot_nt(gq, w_query)
    far_got = swap(gn_far[row_count:].astype(BF16), "seq", 1)
    far_sum = (gn_far[:row_count] + far_got.astype(F32)).astype(BF16)
    near_got = swap(gn_near[row_count:].astype(BF16), "seq", 1)
    x_got = swap(far_sum, "seq", 2)
    grad_normed_one = gn_near[:row_count] + near_got.astype(F32) + x_got.astype(F32)
    grad_tokens_norm, grad_ln1_gain, grad_ln1_bias = norm_one_back(grad_normed_one)
    grad_tokens = (grad_middle + grad_tokens_norm).astype(BF16)

    dw_q = dot_tn(normed_image[: 2 * row_count], gq)
    dw_kv = dot_tn(normed_image, gkv).reshape(model_width, heads_here, 2, HEAD_DIM)
    dw_v = dw_kv[:, :, 0].reshape(model_width, heads_here * HEAD_DIM)
    dw_k = dw_kv[:, :, 1].reshape(model_width, heads_here * HEAD_DIM)
    part_zero = jnp.concatenate([dw_q, dw_k[:, :third]], axis=1).astype(BF16)
    part_one = jnp.concatenate([dw_k[:, third:], dw_v], axis=1).astype(BF16)
    at_zero = seq_here < 2
    qkv_mine = jnp.where(at_zero, part_zero, part_one)
    qkv_other = jnp.where(at_zero, part_one, part_zero)
    qkv_rows = scatter_chip(qkv_mine, qkv_other, order_a)
    pieces = [qkv_rows[:, i * third : (i + 1) * third] for i in range(3)]
    piece_got = swap(jnp.where(core == 0, pieces[2], pieces[0]), "seq", 1)
    out_w_qkv = jnp.concatenate(
        [
            jnp.where(core == 0, pieces[0], pieces[1]),
            piece_got,
            jnp.where(core == 0, pieces[1], pieces[2]),
        ],
        axis=1,
    )

    def place(vector):
        halves = vector.reshape(2, 1, third)
        zero = jnp.zeros_like(halves)
        both = jnp.where(
            core == 0,
            jnp.concatenate([halves, zero], axis=1),
            jnp.concatenate([zero, halves], axis=1),
        )
        return both.reshape(model_width)

    grad_bias_query = place(column_sum(gq))
    gkv_sums = column_sum(gkv).reshape(heads_here, 2, HEAD_DIM)
    grad_bias_value = place(gkv_sums[:, 0].reshape(heads_here * HEAD_DIM))

    early = lax.psum(
        jnp.concatenate(
            [grad_bias_down, grad_bias_out, grad_ln2_gain, grad_ln2_bias, grad_bias_up]
        ),
        ("grp", "seq"),
    )
    late = lax.psum(
        jnp.concatenate([grad_ln1_gain, grad_ln1_bias, grad_bias_query, grad_bias_value]),
        ("grp", "seq"),
    )
    rows_each = model_width // grp_devices
    cols_each = model_width // seq_devices

    def vector_rows(packed, index):
        return lax.dynamic_slice_in_dim(
            packed, index * model_width + grp_here * rows_each, rows_each, 0
        )

    ff_each = bias_up.shape[0] // grp_devices
    out_bias_up = lax.dynamic_slice_in_dim(
        early, 4 * model_width + grp_here * ff_each, ff_each, 0
    )
    emb_cols = lax.dynamic_slice_in_dim(class_emb, grp_here * rows_each, rows_each, 1)
    class_cols = lax.dynamic_slice_in_dim(grad_classes, seq_here * cols_each, cols_each, 1)
    grad_proj_class = dot_tn(emb_cols, class_cols)
    proj_rows = lax.dynamic_slice_in_dim(proj_class, grp_here * rows_each, rows_each, 0)
    grad_class_emb = dot_nt(grad_classes, proj_rows)
    return (
        mask_out,
        grad_tokens,
        vector_rows(late, 0),
        vector_rows(late, 1),
        out_w_qkv,
        vector_rows(late, 2),
        vector_rows(late, 3),
        out_w_out,
        vector_rows(early, 1),
        vector_rows(early, 2),
        vector_rows(early, 3),
        out_w_up,
        out_bias_up,
        out_w_down,
        vector_rows(early, 0),
        out_proj_patch,
        grad_proj_class,
        grad_class_emb,
    )


def solution(mesh):
    rows = P(("grp", "seq"), None)
    both = P("grp", "seq")
    return jax.shard_map(
        body,
        mesh=mesh,
        in_specs=(rows, P("grp")) + (P(),) * 16 + (rows,),
        out_specs=(
            rows,
            rows,
            P("grp"),
            P("grp"),
            both,
            P("grp"),
            P("grp"),
            both,
            P("grp"),
            P("grp"),
            P("grp"),
            both,
            P("grp"),
            both,
            P("grp"),
            both,
            both,
            P(None, "grp"),
        ),
        check_vma=False,
    )
```

```python
import functools
import math

import jax
import jax.numpy as jnp
from jax import lax
from jax.experimental import pallas as pl
from jax.experimental.pallas import tpu as pltpu
from jax.sharding import PartitionSpec as P

HEAD_DIM = 64
LANES = 128
EPS_NORM = 1e-06
EPS_UNIT = 1e-06
NEG_FILL = -1e30
LOG2E = math.log2(math.e)
F32 = jnp.float32
BF16 = jnp.bfloat16
MIB = 1 << 20
VMEM_LIMIT = 63 * MIB
MESH = pl.DeviceIdType.MESH


def dot_nn(a, b):
    return lax.dot_general(a, b, (((1,), (0,)), ((), ())), preferred_element_type=F32)


def dot_nt(a, b):
    return lax.dot_general(a, b, (((1,), (1,)), ((), ())), preferred_element_type=F32)


def dot_tn(a, b):
    return lax.dot_general(a, b, (((0,), (0,)), ((), ())), preferred_element_type=F32)


def swap_tokens(seq, src, dst, send, recv):
    return pltpu.make_async_remote_copy(
        src_ref=src,
        dst_ref=dst,
        send_sem=send,
        recv_sem=recv,
        device_id={"seq": seq + 1 - 2 * lax.rem(seq, 2)},
        device_id_type=MESH,
    )


def greet_core(seq):
    barrier = pltpu.get_barrier_semaphore()
    peer = {"seq": seq + 1 - 2 * lax.rem(seq, 2)}
    pl.semaphore_signal(barrier, inc=1, device_id=peer, device_id_type=MESH)
    pl.semaphore_wait(barrier, 1)


def normed_tile(step, per, own_ref, got, out_ref, gain_ref, shift_ref):
    tile = out_ref.shape[0]
    row = lax.rem(step, per) * tile

    @pl.when(step < per)
    def _():
        out_ref[...] = own_ref[pl.ds(pl.multiple_of(row, tile), tile), :]

    @pl.when(step >= per)
    def _():
        out_ref[...] = got[pl.ds(pl.multiple_of(row, tile), tile), :]

    rows = out_ref[...].astype(F32)
    centred = rows - jnp.mean(rows, axis=-1, keepdims=True)
    var = jnp.mean(centred * centred, axis=-1, keepdims=True)
    normed = centred * lax.rsqrt(var + EPS_NORM) * gain_ref[...] + shift_ref[...]
    normed = normed.astype(BF16)
    out_ref[...] = normed
    return normed, row


def key_mask(length, first_row, shape):
    where_row = lax.broadcasted_iota(jnp.int32, (shape[0], 1), 0) + first_row
    masked = jnp.where(where_row < length, 0.0, NEG_FILL)
    column = lax.broadcasted_iota(jnp.int32, (1, shape[1]), 1)
    return masked * jnp.where(lax.rem(column, LANES) == 0, 1.0, 0.0)


def project_near_kernel(
    lengths_ref,
    own_ref,
    gain_ref,
    shift_ref,
    w_ref,
    bias_query_ref,
    bias_value_ref,
    normed_ref,
    wkv_ref,
    vbias_ref,
    wpair_ref,
    wqt_ref,
    q_t_ref,
    gout_q_ref,
    k_ref,
    v_ref,
    wq,
    qbias,
    got,
    send,
    recv,
):
    step = pl.program_id(0)
    seq = lax.axis_index("seq")
    core = lax.rem(seq, 2)
    width = normed_ref.shape[1]
    tile = normed_ref.shape[0]
    rows = own_ref.shape[0]
    per = rows // tile

    @pl.when(step == 0)
    def _():
        greet_core(seq)
        swap_tokens(seq, own_ref, got, send, recv).start()
        zero = jnp.zeros((width, HEAD_DIM), BF16)
        zero_row = jnp.zeros((1, HEAD_DIM), F32)
        first = jnp.where(lax.broadcasted_iota(jnp.int32, (1, HEAD_DIM), 1) == 0, 1.0, 0.0)
        for which in range(2):

            @pl.when(core == which)
            def _():
                query_row, value_row = [], []
                for head in range(width // LANES):
                    within, group = divmod(head, 2)
                    at = (2 * group + which) * (width // 4) + within * HEAD_DIM
                    spot = slice(at, at + HEAD_DIM)
                    to = slice(head * LANES, (head + 1) * LANES)
                    query = w_ref[:, spot]
                    key = w_ref[:, width + at : width + at + HEAD_DIM]
                    value = w_ref[:, 2 * width + at : 2 * width + at + HEAD_DIM]
                    wq[:, to] = jnp.concatenate([zero, query], axis=1)
                    wkv_ref[:, to] = jnp.concatenate([zero, key], axis=1)
                    wkv_ref[:, width + head * LANES : width + (head + 1) * LANES] = (
                        jnp.concatenate([value, zero], axis=1)
                    )
                    wpair_ref[:, to] = jnp.concatenate([value, key], axis=1)
                    wqt_ref[head * HEAD_DIM : (head + 1) * HEAD_DIM, :] = query.T
                    query_row += [first * HEAD_DIM**0.5, bias_query_ref[:, spot]]
                    value_row += [bias_value_ref[:, spot], first]
                qbias[...] = jnp.concatenate(query_row, axis=1)
                vbias_ref[...] = jnp.concatenate(value_row, axis=1)

    @pl.when(step == per)
    def _():
        swap_tokens(seq, own_ref, got, send, recv).wait()

    normed, row = normed_tile(step, per, own_ref, got, normed_ref, gain_ref, shift_ref)
    block = step // per
    place = seq + block * (1 - 2 * core)
    mixed = (dot_nn(normed, wq[...]) + qbias[...]).astype(BF16).astype(F32)
    query = (mixed * HEAD_DIM**-0.5).astype(BF16)
    q_t_ref[...] = query.T
    column = lax.broadcasted_iota(jnp.int32, query.shape, 1)
    gout_q_ref[...] = jnp.where(lax.rem(column, LANES) == 0, jnp.zeros_like(query), query)
    mask = key_mask(lengths_ref[0], place * rows + row, k_ref.shape)
    k_ref[...] = (dot_nn(normed, wkv_ref[:, :width]) + mask).astype(BF16)
    v_ref[...] = (dot_nn(normed, wkv_ref[:, width:]) + vbias_ref[...]).astype(BF16)


def project_far_kernel(
    lengths_ref,
    own_ref,
    gain_ref,
    shift_ref,
    wkv_ref,
    vbias_ref,
    normed_in,
    k_in,
    v_in,
    normed_ref,
    k_ref,
    v_ref,
    got,
    send,
    recv,
):
    step = pl.program_id(0)
    seq = lax.axis_index("seq")
    core = lax.rem(seq, 2)
    width = normed_ref.shape[1]
    tile = normed_ref.shape[0]
    rows = own_ref.shape[0]
    per = rows // tile

    @pl.when(step == 0)
    def _():
        greet_core(seq)
        swap_tokens(seq, own_ref, got, send, recv).start()

    @pl.when(step == per)
    def _():
        swap_tokens(seq, own_ref, got, send, recv).wait()

    normed, row = normed_tile(step, per, own_ref, got, normed_ref, gain_ref, shift_ref)
    block = step // per
    place = seq + 2 - 4 * (seq // 2) + block * (1 - 2 * core)
    mask = key_mask(lengths_ref[0], place * rows + row, k_ref.shape)
    k_ref[...] = (dot_nn(normed, wkv_ref[:, :width]) + mask).astype(BF16)
    v_ref[...] = (dot_nn(normed, wkv_ref[:, width:]) + vbias_ref[...]).astype(BF16)


def whole(a):
    return pl.BlockSpec(a.shape, lambda *_: (0,) * len(a.shape))


def project_near(lengths, tokens, gain, shift, w_qkv, bias_query, bias_value):
    rows, width = tokens.shape
    tile = rows // 2
    shape = lambda *s: jax.ShapeDtypeStruct(s, BF16)
    tiled = pl.BlockSpec((tile, width), lambda i: (i, 0))
    image = shape(4 * rows, width)
    outs = [
        image,
        shape(width, 2 * width),
        jax.ShapeDtypeStruct((1, width), F32),
        shape(width, width),
        shape(width // 2, width),
        shape(width, 2 * rows),
        image,
        image,
        image,
    ]
    return pl.pallas_call(
        project_near_kernel,
        grid=(4,),
        in_specs=[pl.BlockSpec(memory_space=pltpu.SMEM)]
        + [whole(a) for a in (tokens, gain, shift, w_qkv, bias_query, bias_value)],
        out_specs=[
            tiled,
            whole(outs[1]),
            whole(outs[2]),
            whole(outs[3]),
            whole(outs[4]),
            pl.BlockSpec((width, tile), lambda i: (0, i)),
            pl.BlockSpec((tile, width), lambda i: (i + 4, 0)),
            tiled,
            tiled,
        ],
        out_shape=outs,
        scratch_shapes=[
            pltpu.VMEM((width, width), BF16),
            pltpu.VMEM((1, width), F32),
            pltpu.VMEM((rows, width), BF16),
            pltpu.SemaphoreType.DMA,
            pltpu.SemaphoreType.DMA,
        ],
        compiler_params=pltpu.CompilerParams(
            vmem_limit_bytes=VMEM_LIMIT, collective_id=2, has_side_effects=True
        ),
        cost_estimate=pl.CostEstimate(
            flops=12 * rows * width * width, bytes_accessed=20 * MIB, transcendentals=0
        ),
        name="project_near",
    )(lengths, tokens, gain, shift, w_qkv, bias_query, bias_value)


def project_far(lengths, tokens, gain, shift, wkv, vbias, images):
    rows, width = tokens.shape
    tile = rows // 2
    tiled = pl.BlockSpec((tile, width), lambda i: (i + 4, 0))
    return pl.pallas_call(
        project_far_kernel,
        grid=(4,),
        in_specs=[pl.BlockSpec(memory_space=pltpu.SMEM)]
        + [whole(a) for a in (tokens, gain, shift, wkv, vbias)]
        + [pl.BlockSpec(memory_space=pl.ANY)] * 3,
        out_specs=[tiled] * 3,
        out_shape=[jax.ShapeDtypeStruct(a.shape, a.dtype) for a in images],
        input_output_aliases={6: 0, 7: 1, 8: 2},
        scratch_shapes=[
            pltpu.VMEM((rows, width), BF16),
            pltpu.SemaphoreType.DMA,
            pltpu.SemaphoreType.DMA,
        ],
        compiler_params=pltpu.CompilerParams(
            vmem_limit_bytes=VMEM_LIMIT, collective_id=3, has_side_effects=True
        ),
        cost_estimate=pl.CostEstimate(
            flops=8 * rows * width * width, bytes_accessed=16 * MIB, transcendentals=0
        ),
        name="project_far",
    )(lengths, tokens, gain, shift, wkv, vbias, *images)


PART = 72


def attend_near_kernel(q_t_ref, k_ref, v_ref, part_ref, top_ref):
    scores = dot_nn(k_ref[...], q_t_ref[...])
    top = jnp.max(scores, axis=0, keepdims=True)
    prob = jnp.exp2((scores - top) * LOG2E).astype(BF16)
    part_ref[...] = dot_tn(v_ref[...], prob)[:PART]
    top_ref[0] = top


def attend_far_kernel(q_t_ref, k_ref, v_ref, part_ref, near_top_ref, own_ref, other_ref, mass_ref):
    scores = dot_nn(k_ref[...], q_t_ref[...])
    near_top = near_top_ref[0]
    top = jnp.maximum(jnp.max(scores, axis=0, keepdims=True), near_top)
    prob = jnp.exp2((scores - top) * LOG2E).astype(BF16)
    summed = dot_tn(v_ref[...], prob)[:PART]
    summed = summed + part_ref[...] * jnp.exp2((near_top - top) * LOG2E)
    total = summed[HEAD_DIM : HEAD_DIM + 1]
    mass_ref[0] = top * LOG2E + jnp.log2(total)
    out = (summed[:HEAD_DIM] / total).astype(BF16)

    @pl.when(pl.program_id(1) == 0)
    def _():
        own_ref[...] = out

    @pl.when(pl.program_id(1) == 1)
    def _():
        other_ref[...] = out


def attend_cost(heads, rows, span):
    return pl.CostEstimate(
        flops=8 * heads * rows * span * LANES,
        bytes_accessed=(rows + 2 * span) * heads * LANES * 2,
        transcendentals=heads * rows * span,
    )


def attend_forward(kernel, name, queries_t, keys, values, *partial):
    width, rows = queries_t.shape
    span = keys.shape[0] // 2
    heads = width // LANES
    tile = rows // 2
    at = 1 if partial else 0
    part_spec = pl.BlockSpec((PART, tile), lambda h, i: (h, i))
    row_spec = pl.BlockSpec((1, 1, tile), lambda h, i: (h, 0, i))
    row_shape = jax.ShapeDtypeStruct((heads, 1, rows), F32)
    if partial:
        out_specs = [pl.BlockSpec((HEAD_DIM, tile), lambda h, i: (h, 0))] * 2 + [row_spec]
        outs = [jax.ShapeDtypeStruct((heads * HEAD_DIM, tile), BF16)] * 2 + [row_shape]
    else:
        out_specs = [part_spec, row_spec]
        outs = [jax.ShapeDtypeStruct((heads * PART, rows), F32), row_shape]
    return pl.pallas_call(
        kernel,
        grid=(heads, 2),
        in_specs=[
            pl.BlockSpec((LANES, tile), lambda h, i: (h, i)),
            pl.BlockSpec((span, LANES), lambda h, i: (at, h)),
            pl.BlockSpec((span, LANES), lambda h, i: (at, h)),
        ]
        + [part_spec, row_spec][: len(partial)],
        out_specs=out_specs,
        out_shape=outs,
        compiler_params=pltpu.CompilerParams(vmem_limit_bytes=VMEM_LIMIT),
        cost_estimate=attend_cost(heads, rows, span),
        name=name,
    )(queries_t, keys, values, *partial)


def score_grads(q_t_ref, gout_t_ref, delta_ref, gout_q_ref, mass_ref, k_ref, v_ref):
    key_now = k_ref[...]
    scores = dot_nn(key_now, q_t_ref[...])
    prob = jnp.exp2(scores * LOG2E - mass_ref[0])
    gprob = dot_nn(v_ref[...], gout_t_ref[...])
    gscore = (prob * (gprob - delta_ref[0])).astype(BF16)
    gkv = dot_nn(jnp.concatenate([prob.astype(BF16), gscore], axis=1), gout_q_ref[...])
    return gkv.astype(BF16), dot_tn(key_now, gscore)[HEAD_DIM:]


def head_specs(rows, head_of):
    return [
        pl.BlockSpec((LANES, rows), lambda *n: (head_of(*n), 0)),
        pl.BlockSpec((LANES, rows), lambda *n: (head_of(*n), 0)),
        pl.BlockSpec((1, 1, rows), lambda *n: (head_of(*n), 0, 0)),
        pl.BlockSpec((2 * rows, LANES), lambda *n: (0, head_of(*n))),
        pl.BlockSpec((1, 1, rows), lambda *n: (head_of(*n), 0, 0)),
    ]


def attend_backward_kernel(q_t, gout_t, delta, gout_q, mass, k_ref, v_ref, gq_ref, gkv_ref, gq_sum):
    step = pl.program_id(1)
    gkv_ref[...], part = score_grads(q_t, gout_t, delta, gout_q, mass, k_ref, v_ref)

    @pl.when(step == 0)
    def _():
        gq_sum[...] = part

    @pl.when(step > 0)
    def _():
        gq_sum[...] += part

    @pl.when(step == pl.num_programs(1) - 1)
    def _():
        gq_ref[...] = (gq_sum[...] * HEAD_DIM**-0.5).astype(BF16)


def attend_backward(queries_t, gouts_t, delta, gout_q, mass, keys, values):
    width, rows = queries_t.shape
    span = keys.shape[0]
    heads = width // LANES
    tile = span // 4
    key_spec = pl.BlockSpec((tile, LANES), lambda h, j: (j, h))
    return pl.pallas_call(
        attend_backward_kernel,
        grid=(heads, span // tile),
        in_specs=head_specs(rows, lambda h, j: h) + [key_spec, key_spec],
        out_specs=[
            pl.BlockSpec((HEAD_DIM, rows), lambda h, j: (h, 0)),
            pl.BlockSpec((tile, LANES), lambda h, j: (j, h)),
        ],
        out_shape=[
            jax.ShapeDtypeStruct((heads * HEAD_DIM, rows), BF16),
            jax.ShapeDtypeStruct((span, width), BF16),
        ],
        scratch_shapes=[pltpu.VMEM((HEAD_DIM, rows), F32)],
        compiler_params=pltpu.CompilerParams(vmem_limit_bytes=VMEM_LIMIT),
        name="attend_backward",
    )(queries_t, gouts_t, delta, gout_q, mass, keys, values)


def erf_parts(u):
    size = jnp.abs(u)
    t = 1.0 / (1.0 + 0.2316418882 * size)
    bell = jnp.exp2(u * u * (-0.5 * LOG2E))
    poly = 0.5306027144 * t - 0.7265760135
    poly = poly * t + 0.7107068705
    poly = poly * t - 0.1422483683
    poly = poly * t + 0.1274147959
    tail = poly * t * bell
    return jnp.where(u < 0.0, tail, 1.0 - tail), bell * (2.0 * math.pi) ** -0.5


def core_order(matrix):
    width = matrix.shape[1] // 4
    return jnp.concatenate(
        [matrix[:, b * width : (b + 1) * width] for b in (0, 2, 1, 3)], axis=1
    )


def middle_kernel(
    lengths_ref,
    tok_ref,
    att_ref,
    got_ref,
    dmask_ref,
    w_out_ref,
    bias_out_ref,
    gain_ref,
    shift_ref,
    w_up_ref,
    bias_up_ref,
    w_down_ref,
    bias_down_ref,
    patch_w_ref,
    class_w_ref,
    class_ref,
    mask_ref,
    joined_ref,
    normed_ref,
    active_ref,
    ghid_ref,
    final_ref,
    gpatch_ref,
    gfeed_ref,
    gbranch_ref,
    gbranch_p_ref,
    gmid_ref,
    early_ref,
    classes_ref,
    slope,
    class_low,
    class_part_ref,
    gbias_down_ref,
    gbias_up_ref,
    gbias_out_ref,
    ggain_ref,
    gshift_ref,
):
    step = pl.program_id(0)
    seq = lax.axis_index("seq")
    core = lax.rem(seq, 2)
    tile, width = tok_ref.shape
    third = width // 4
    scale = math.sqrt(width)
    chunks = w_up_ref.shape[1] // width

    @pl.when(step == 0)
    def _():
        classes = dot_nn(class_ref[...], class_w_ref[...])
        classes_ref[...] = classes
        class_low[...] = (
            classes * lax.rsqrt(jnp.sum(classes * classes, axis=-1, keepdims=True) + EPS_UNIT)
        ).astype(BF16)
        for ref in (class_part_ref, gbias_down_ref, gbias_up_ref, gbias_out_ref, ggain_ref, gshift_ref):
            ref[...] = jnp.zeros_like(ref)

    for head in range(width // LANES):
        within, group = divmod(head, 2)
        at = 2 * group * third + within * HEAD_DIM
        own = slice(head * HEAD_DIM, (head + 1) * HEAD_DIM)
        joined_ref[pl.ds(at + core * third, HEAD_DIM), :] = att_ref[own, :]
        joined_ref[pl.ds(at + (1 - core) * third, HEAD_DIM), :] = got_ref[own, :]
    branch = dot_tn(joined_ref[...], w_out_ref[...]) + bias_out_ref[...]
    middle = tok_ref[...].astype(F32) + branch
    centred = middle - jnp.mean(middle, axis=-1, keepdims=True)
    inv = lax.rsqrt(jnp.mean(centred * centred, axis=-1, keepdims=True) + EPS_NORM)
    normal = centred * inv
    normed = (normal * gain_ref[...] + shift_ref[...]).astype(BF16)
    normed_ref[...] = normed
    final = middle + bias_down_ref[...]
    for chunk in range(chunks):
        cols = slice(chunk * width, (chunk + 1) * width)
        hidden = dot_nn(normed, w_up_ref[:, cols]) + bias_up_ref[:, cols]
        below, density = erf_parts(hidden)
        active = (hidden * below).astype(BF16)
        active_ref[:, cols] = active
        slope[:, cols] = below + hidden * density
        final = final + dot_nn(active, w_down_ref[cols, :])
    final_low = final.astype(BF16)
    final_ref[...] = final_low
    patches = dot_nn(final_low, patch_w_ref[...])
    unit_scale = lax.rsqrt(jnp.sum(patches * patches, axis=-1, keepdims=True) + EPS_UNIT)
    unit = patches * unit_scale
    unit_low = unit.astype(BF16)
    first_row = seq * (tile * pl.num_programs(0)) + step * tile
    where_row = lax.broadcasted_iota(jnp.int32, (tile, 1), 0) + first_row
    valid = jnp.where(where_row < lengths_ref[0], 1.0, 0.0)
    mask_ref[...] = (dot_nt(unit_low, class_low[...]) * (scale * valid)).astype(BF16)
    gmask = (dmask_ref[...].astype(F32) * valid).astype(BF16)
    class_part_ref[...] += dot_tn(gmask, unit_low) * scale
    gunit = dot_nn(gmask, class_low[...]) * scale
    gpatch = (
        unit_scale * (gunit - unit * jnp.sum(gunit * unit, axis=-1, keepdims=True))
    ).astype(BF16)
    gpatch_ref[...] = core_order(gpatch)
    gfinal = dot_nt(gpatch, patch_w_ref[...])
    gfeed = gfinal.astype(BF16)
    gfeed_ref[...] = core_order(gfeed)
    gbias_down_ref[...] += jnp.sum(gfeed.astype(F32), axis=0, keepdims=True)
    gnormed = jnp.zeros((tile, width), F32)
    for chunk in range(chunks):
        cols = slice(chunk * width, (chunk + 1) * width)
        ghidden = (dot_nt(gfeed, w_down_ref[cols, :]) * slope[:, cols]).astype(BF16)
        ghid_ref[:, cols] = ghidden
        gbias_up_ref[:, cols] += jnp.sum(ghidden.astype(F32), axis=0, keepdims=True)
        gnormed = gnormed + dot_nt(ghidden, w_up_ref[:, cols])
    ggain_ref[...] += jnp.sum(gnormed * normal, axis=0, keepdims=True)
    gshift_ref[...] += jnp.sum(gnormed, axis=0, keepdims=True)
    turned = gnormed * gain_ref[...]
    gmid = gfinal + inv * (
        turned
        - jnp.mean(turned, axis=-1, keepdims=True)
        - normal * jnp.mean(turned * normal, axis=-1, keepdims=True)
    )
    gmid_ref[...] = gmid
    gbranch = gmid.astype(BF16)
    gbranch_ref[...] = gbranch
    gbranch_p_ref[...] = core_order(gbranch)
    gbias_out_ref[...] += jnp.sum(gbranch.astype(F32), axis=0, keepdims=True)

    @pl.when(step == pl.num_programs(0) - 1)
    def _():
        class_rows = class_part_ref.shape[0]
        at = early_ref.shape[0] - 16
        early_ref[...] = jnp.zeros_like(early_ref)
        early_ref[:class_rows, :] = class_part_ref[...].astype(BF16)
        parts = [gbias_down_ref[...], gbias_out_ref[...], ggain_ref[...], gshift_ref[...]]
        parts += [gbias_up_ref[:, i * width : (i + 1) * width] for i in range(chunks)]
        parts += [jnp.zeros_like(gbias_down_ref)] * (16 - len(parts))
        early_ref[at:, :] = jnp.concatenate(parts, axis=0).astype(BF16)


def middle(lengths, tokens, att_own, att_got, d_masks, params):
    rows, width = tokens.shape
    tile = rows // 2
    classes = d_masks.shape[1]
    hidden = params[4].shape[1]
    full = lambda a: pl.BlockSpec(a.shape, lambda i, p: (0,) * len(a.shape))
    tiled = lambda n: pl.BlockSpec((tile, n), lambda i, p: (i, 0))
    turned = lambda n: pl.BlockSpec((n, tile), lambda i, p: (0, i))
    shape = jax.ShapeDtypeStruct
    low = lambda n: shape((rows, n), BF16)
    early_rows = (classes + 15) // 16 * 16 + 16
    sums = [shape((early_rows, width), BF16), shape((classes, width), F32)]
    return pl.pallas_call(
        middle_kernel,
        grid_spec=pltpu.PrefetchScalarGridSpec(
            num_scalar_prefetch=1,
            grid=(2,),
            in_specs=[tiled(width), turned(width // 2), turned(width // 2), tiled(classes)]
            + [pl.BlockSpec(a.shape, lambda i, p: (0, 0), pipeline_mode=pl.Buffered(1)) for a in params],
            out_specs=[
                tiled(classes),
                turned(width),
                tiled(width),
                tiled(hidden),
                tiled(hidden),
                tiled(width),
                tiled(width),
                tiled(width),
                tiled(width),
                tiled(width),
                tiled(width),
            ]
            + [full(a) for a in sums],
            scratch_shapes=[
                pltpu.VMEM((tile, hidden), F32),
                pltpu.VMEM((classes, width), BF16),
                pltpu.VMEM((classes, width), F32),
                pltpu.VMEM((1, width), F32),
                pltpu.VMEM((1, hidden), F32),
                pltpu.VMEM((1, width), F32),
                pltpu.VMEM((1, width), F32),
                pltpu.VMEM((1, width), F32),
            ],
        ),
        out_shape=[
            low(classes),
            shape((width, rows), BF16),
            low(width),
            low(hidden),
            low(hidden),
            low(width),
            low(width),
            low(width),
            low(width),
            low(width),
            shape((rows, width), F32),
        ]
        + sums,
        compiler_params=pltpu.CompilerParams(vmem_limit_bytes=VMEM_LIMIT),
        cost_estimate=pl.CostEstimate(
            flops=4 * rows * width * (2 * hidden + 2 * width),
            bytes_accessed=40 * MIB,
            transcendentals=2 * rows * hidden,
        ),
        name="middle",
    )(lengths, tokens, att_own, att_got, d_masks, *params)


def weights_kernel(
    normed_in,
    ghid_in,
    active_in,
    gfeed_in,
    joined_in,
    gbranch_in,
    gbranch_p_in,
    final_in,
    gpatch_in,
    w_out_in,
    att_own_in,
    att_other_in,
    gout_q_in,
    up_out,
    down_out,
    pair_out,
    gout_q_out,
    gout_t_out,
    delta_out,
    normed,
    ghid,
    active,
    gfeed,
    joined,
    gbranch,
    gbranch_p,
    final,
    gpatch,
    w_out,
    att_own,
    att_other,
    w_pad,
    up_send,
    down_send,
    pair_send,
    up_keep,
    down_keep,
    pair_keep,
    up_got,
    down_got,
    pair_got,
    branch_got,
    gout,
    gout_t,
    delta,
    send,
    recv,
    load,
    store,
):
    seq = lax.axis_index("seq")
    core = lax.rem(seq, 2)
    x = seq // 2
    rows, width = normed.shape
    half = width // 2
    heads = width // LANES
    third = width // 4
    tiles = active.shape[1] // width
    peer = {"seq": seq + 1 - 2 * core}

    barrier = pltpu.get_barrier_semaphore()
    pl.semaphore_signal(barrier, inc=1, device_id=peer, device_id_type=MESH)

    ins = (
        (joined_in, joined),
        (gbranch_p_in, gbranch_p),
        (final_in, final),
        (gpatch_in, gpatch),
        (gfeed_in, gfeed),
        (active_in, active),
        (normed_in, normed),
        (ghid_in, ghid),
        (w_out_in, w_out),
        (gbranch_in, gbranch),
        (att_own_in, att_own),
        (att_other_in, att_other),
    )
    loads = [pltpu.make_async_copy(a, b, load.at[i]) for i, (a, b) in enumerate(ins)]
    for copy in loads:
        copy.start()
    pl.semaphore_wait(barrier, 1)

    def far(at, src, dst):
        return pltpu.make_async_remote_copy(
            src_ref=src,
            dst_ref=dst,
            send_sem=send.at[at],
            recv_sem=recv.at[at],
            device_id=peer,
            device_id_type=MESH,
        )

    def far_branch():
        return far(0, gbranch_in, branch_got)

    def far_pair():
        return far(1, pair_send, pair_got)

    def far_down(i):
        return far(2 + i, down_send.at[i], down_got.at[i])

    def far_up(i):
        return far(2 + tiles + i, up_send.at[i], up_got.at[i])

    def lanes(index, size):
        return pl.ds(pl.multiple_of(index * size, size), size)

    def pair_of(which):
        spot = lanes(which, half)
        first = dot_nn(joined[...], gbranch_p[:, spot])
        second = dot_tn(final[...], gpatch[:, spot])
        return first, second

    def down_of(i, which):
        return dot_tn(active[:, lanes(i, width)], gfeed[:, lanes(which, half)])

    def up_of(block):
        return dot_tn(normed[...], ghid[:, lanes(block, width)])

    far_branch().start()
    for i in range(4):
        loads[i].wait()
    first, second = pair_of(1 - core)
    pair_send[:, :half] = first.astype(BF16)
    pair_send[:, half:] = second.astype(BF16)
    far_pair().start()
    loads[4].wait()
    loads[5].wait()

    def send_down(i, carry):
        down_send[i] = down_of(i, 1 - core).astype(BF16)
        far_down(i).start()
        return carry

    lax.fori_loop(0, tiles, send_down, 0)
    loads[6].wait()
    loads[7].wait()
    for i in range(2):
        block = 2 * (x + i - 2 * i * x) + 1 - core
        up_send[i] = up_of(block).astype(BF16)
        far_up(i).start()

    loads[8].wait()
    loads[9].wait()
    w_pad[...] = jnp.zeros_like(w_pad)
    for head in range(heads):
        within, group = divmod(head, 2)
        at = 2 * group * third + within * HEAD_DIM
        w_pad[head * LANES : head * LANES + HEAD_DIM, :] = w_out[
            pl.ds(pl.multiple_of(at + core * third, HEAD_DIM), HEAD_DIM), :
        ]
    loads[10].wait()
    loads[11].wait()
    for at, (rows_in, att) in enumerate(((gbranch, att_own), (branch_got, att_other))):
        if at == 1:
            far_branch().wait()
        spot = slice(at * rows, (at + 1) * rows)
        gout[spot, :] = dot_nt(rows_in[...], w_pad[...]).astype(BF16)
        turned = dot_nt(w_pad[...], rows_in[...]).astype(BF16)
        gout_t[:, spot] = turned
        for head in range(heads):
            low = turned[head * LANES : head * LANES + HEAD_DIM].astype(F32)
            own = att[head * HEAD_DIM : (head + 1) * HEAD_DIM, :].astype(F32)
            delta[head, :, spot] = jnp.sum(low * own, axis=0, keepdims=True)
    stores = [
        pltpu.make_async_copy(gout, gout_q_out.at[pl.ds(0, 2 * rows)], store.at[0]),
        pltpu.make_async_copy(gout_t, gout_t_out, store.at[4]),
        pltpu.make_async_copy(delta, delta_out, store.at[5]),
    ]
    for copy in stores:
        copy.start()

    first, second = pair_of(core)
    far_pair().wait()
    pair_keep[:, :half] = (first + pair_got[:, :half].astype(F32)).astype(BF16)
    pair_keep[:, half:] = (second + pair_got[:, half:].astype(F32)).astype(BF16)
    stores.append(pltpu.make_async_copy(pair_keep, pair_out, store.at[1]))
    stores[-1].start()

    def keep_down(i, carry):
        part = down_of(i, core)
        far_down(i).wait()
        down_keep[i] = (part + down_got[i].astype(F32)).astype(BF16)
        return carry

    lax.fori_loop(0, tiles, keep_down, 0)
    stores.append(pltpu.make_async_copy(down_keep, down_out, store.at[2]))
    stores[-1].start()
    for i in range(2):
        block = 2 * (x + i - 2 * i * x) + core
        part = up_of(block)
        far_up(i).wait()
        up_keep[i] = (part + up_got[i].astype(F32)).astype(BF16)
    stores.append(pltpu.make_async_copy(up_keep, up_out, store.at[3]))
    stores[-1].start()
    for copy in stores:
        copy.wait()


def weights(gout_q, *operands):
    rows, width = operands[0].shape
    hidden = operands[2].shape[1]
    tiles = hidden // width
    half = width // 2
    heads = width // LANES
    low = lambda *s: pltpu.VMEM(s, BF16)
    hbm = pl.BlockSpec(memory_space=pl.ANY)
    sets = [low(2, width, width), low(tiles, width, half), low(width, width)]
    shape = lambda *s: jax.ShapeDtypeStruct(s, BF16)
    outs = [
        shape(2, width, width),
        shape(tiles, width, half),
        shape(width, width),
        shape(*gout_q.shape),
        shape(width, 2 * rows),
        jax.ShapeDtypeStruct((heads, 1, 2 * rows), F32),
    ]
    return pl.pallas_call(
        weights_kernel,
        in_specs=[hbm] * (len(operands) + 1),
        out_specs=[hbm] * len(outs),
        out_shape=outs,
        input_output_aliases={len(operands): 3},
        scratch_shapes=[low(*a.shape) for a in operands]
        + [low(width, width)]
        + sets * 3
        + [
            low(rows, width),
            low(2 * rows, width),
            low(width, 2 * rows),
            pltpu.VMEM((heads, 1, 2 * rows), F32),
            pltpu.SemaphoreType.DMA((4 + tiles,)),
            pltpu.SemaphoreType.DMA((4 + tiles,)),
            pltpu.SemaphoreType.DMA((len(operands),)),
            pltpu.SemaphoreType.DMA((6,)),
        ],
        compiler_params=pltpu.CompilerParams(
            vmem_limit_bytes=VMEM_LIMIT, collective_id=1, has_side_effects=True
        ),
        cost_estimate=pl.CostEstimate(
            flops=4 * rows * width * (hidden + 2 * width),
            bytes_accessed=30 * MIB,
            transcendentals=0,
        ),
        name="weights",
    )(*operands, gout_q)


EXCHANGES = tuple(
    chain + way
    for chain, ways in (
        ("U", "XYZW"),
        ("D", "YZWX"),
        ("C", "ZWYX"),
        ("V", "CXYZW"),
        ("G", "CXN"),
        ("S", "W"),
        ("L", "CXYZW"),
        ("Q0", "YZWX"),
        ("Q1", "YZWX"),
        ("Q2", "YZWX"),
    )
    for way in ways
)


def backward_kernel(
    q_t,
    gout_t,
    delta,
    gout_q,
    mass,
    k_ref,
    v_ref,
    up_in,
    down_in,
    pair_in,
    early_in,
    normed_in,
    tokens_in,
    gmid_in,
    gain_ref,
    wpair_ref,
    wqt_ref,
    up_out,
    down_out,
    pair_out,
    early_out,
    qkv_out,
    swap_out,
    late_out,
    gtok_out,
    gq_all,
    gq_low,
    gkv_all,
    far_dw,
    normed,
    tokens,
    gmid,
    gn_far,
    gn_send,
    gn_own,
    gkv_sum,
    au,
    ad,
    ac,
    aq,
    ru0,
    ru1,
    ru2,
    ru3,
    rd0,
    rd1,
    rd2,
    rd3,
    rc0,
    rc1,
    rc2,
    rc3,
    rv,
    rq0,
    rq1,
    rq2,
    rq3,
    rg,
    rl,
    swap_send,
    swap_got,
    send,
    recv,
    local,
):
    step = pl.program_id(0)
    seq = lax.axis_index("seq")
    grp = lax.axis_index("grp")
    core = lax.rem(seq, 2)
    x = seq // 2
    y = lax.rem(grp, 2)
    z = lax.rem(grp // 2, 2)
    w = grp // 4
    peers = {
        "C": {"seq": seq + 1 - 2 * core},
        "X": {"seq": seq + 2 - 4 * x},
        "Y": {"grp": grp + 1 - 2 * y},
        "Z": {"grp": grp + 2 - 4 * z},
        "W": {"grp": grp + 4 - 8 * w},
    }
    tile = k_ref.shape[0]
    rows, heads = q_t.shape[1], gkv_all.shape[1] // LANES
    half = rows // 2
    width = wpair_ref.shape[1]
    tiles = half * 2 // tile
    per_phase = heads * tiles
    now = lax.rem(step, per_phase)
    head, block = now // tiles, lax.rem(now, tiles)

    def far(name, src, dst, way=None):
        at = EXCHANGES.index(name)
        return pltpu.make_async_remote_copy(
            src_ref=src,
            dst_ref=dst,
            send_sem=send.at[at],
            recv_sem=recv.at[at],
            device_id=peers[way or name[-1]],
            device_id_type=MESH,
        )

    def near(at, src, dst):
        return pltpu.make_async_copy(src, dst, local.at[at])

    def add(dst, src, count):
        if count is None:
            dst[...] = dst[...] + src[...]
            return
        for i in range(count):
            dst[i] = dst[i] + src[i]

    def exchange(name):
        if name == "UX":
            return far(name, up_in.at[1], ru0)
        if name == "UY":
            return far(name, au.at[:, :, 1 - y], ru1)
        if name == "UZ":
            return far(name, au.at[:, 1 - z, y], ru2)
        if name == "UW":
            return far(name, au.at[1 - w, z, y], ru3)
        if name == "DY":
            return far(name, down_in.at[:, :, 1 - y], rd0)
        if name == "DZ":
            return far(name, ad.at[:, 1 - z], rd1)
        if name == "DW":
            return far(name, ad.at[1 - w, z], rd2)
        if name == "DX":
            return far(name, ad.at[w, z], rd3)
        if name == "CZ":
            return far(name, pair_in.at[:, 1 - z], rc0)
        if name == "CW":
            return far(name, ac.at[1 - w], rc1)
        if name == "CY":
            return far(name, ac.at[w, 1 - y], rc2)
        if name == "CX":
            return far(name, ac.at[w, y], rc3)
        if name[0] == "V":
            return far(name, early_out, rv.at["CXYZW".index(name[1])])
        if name == "GC":
            return far(name, gn_far.at[1], rg.at[0])
        if name == "GX":
            return far(name, gn_far.at[0], rg.at[1])
        if name == "GN":
            return far(name, gn_send, rg.at[2], "C")
        if name == "SW":
            return far(name, swap_send, swap_got, "C")
        if name[0] == "L":
            return far(name, late_out, rl.at["CXYZW".index(name[1])])
        b = int(name[1])
        if name[2] == "Y":
            return far(name, aq.at[b, :, :, 1 - y], rq0.at[b])
        if name[2] == "Z":
            return far(name, aq.at[b, :, 1 - z, y], rq1.at[b])
        if name[2] == "W":
            return far(name, aq.at[b, 1 - w, z, y], rq2.at[b])
        return far(name, aq.at[b, w, z, y], rq3.at[b])

    def arrive(name):
        exchange(name).wait()
        if name == "UX":
            near(0, up_in.at[0], au).wait()
            for i in range(2):
                for j in range(2):
                    add(au.at[i, j], ru0.at[i, j], 2)
        elif name == "UY":
            for i in range(2):
                for j in range(2):
                    add(au.at[i, j, y], ru1.at[i, j], None)
        elif name == "UZ":
            for i in range(2):
                add(au.at[i, z, y], ru2.at[i], None)
        elif name == "UW":
            up_out[...] = au[w, z, y].astype(F32) + ru3[...].astype(F32)
        elif name == "DY":
            near(1, down_in.at[:, :, y], ad).wait()
            for i in range(2):
                add(ad.at[i], rd0.at[i], 2)
        elif name == "DZ":
            for i in range(2):
                add(ad.at[i, z], rd1.at[i], None)
        elif name == "DW":
            add(ad.at[w, z], rd2, None)
        elif name == "DX":
            down_out[...] = ad[w, z].astype(F32) + rd3[...].astype(F32)
        elif name == "CZ":
            near(2, pair_in.at[:, z], ac).wait()
            for i in range(2):
                add(ac.at[i], rc0.at[i], 2)
        elif name == "CW":
            add(ac.at[w], rc1, 2)
        elif name == "CY":
            add(ac.at[w, y], rc2, None)
        elif name == "CX":
            pair_out[...] = ac[w, y].astype(F32) + rc3[...].astype(F32)
        elif name[0] == "V":
            add(early_out, rv.at["CXYZW".index(name[1])], None)
        elif name == "GC":
            add(gn_far.at[0], rg.at[0], None)
        elif name[0] == "L":
            add(late_out, rl.at["CXYZW".index(name[1])], None)
        elif name[0] == "Q":
            b = int(name[1])
            if name[2] == "Y":
                for i in range(2):
                    for j in range(2):
                        add(aq.at[b, i, j, y], rq0.at[b, i, j], None)
            elif name[2] == "Z":
                for i in range(2):
                    add(aq.at[b, i, z, y], rq1.at[b, i], None)
            elif name[2] == "W":
                add(aq.at[b, w, z, y], rq2.at[b], None)
            else:
                qkv_out[b] = aq[b, w, z, y].astype(F32) + rq3[b].astype(F32)

    def start(*names):
        for name in names:
            exchange(name).start()

    def next_of(come, then):
        arrive(come)
        start(then)

    def at_step(number, action):
        @pl.when(step == number)
        def _():
            action()

    def weights_of(b):
        lanes = slice(2 * b * LANES, 2 * (b + 1) * LANES)
        both = dot_tn(gkv_all[:, lanes], normed[...]) + far_dw[lanes, :]
        low_rows = gq_all[2 * b : 2 * b + 2].reshape(LANES, rows) * HEAD_DIM**-0.5
        low_rows = low_rows.astype(BF16)
        gq_low[b * LANES : (b + 1) * LANES, :] = low_rows
        query = dot_nn(low_rows, normed[...])
        size = HEAD_DIM
        stacked = jnp.concatenate(
            [
                query,
                both[size : 2 * size],
                both[3 * size :],
                both[:size],
                both[2 * size : 3 * size],
            ],
            axis=0,
        )
        aq[b] = stacked.T.astype(BF16).reshape(aq.shape[1:])
        start("Q%dY" % b)

    def first_step():
        barrier = pltpu.get_barrier_semaphore()
        for peer in peers.values():
            pl.semaphore_signal(barrier, inc=1, device_id=peer, device_id_type=MESH)
        pl.semaphore_wait(barrier, len(peers))
        near(0, up_in.at[0], au).start()
        near(1, down_in.at[:, :, y], ad).start()
        near(2, pair_in.at[:, z], ac).start()
        near(3, early_in, early_out).start()
        start("UX", "DY", "CZ")
        near(4, normed_in.at[pl.ds(rows, rows)], normed).start()
        near(3, early_in, early_out).wait()
        start("VC")

    def far_post():
        near(4, normed_in.at[pl.ds(rows, rows)], normed).wait()
        gkv_sum[...] = jnp.sum(gkv_all[...].astype(F32), axis=0, keepdims=True)
        for i in (1, 0):
            gn_far[i] = dot_nt(gkv_all[i * half : (i + 1) * half, :], wpair_ref[...]).astype(BF16)
            if i == 1:
                start("GC")
        far_dw[...] = dot_tn(gkv_all[...], normed[...])
        near(5, normed_in.at[pl.ds(0, rows)], normed).start()

    at_step(0, first_step)
    at_step(5, lambda: next_of("CZ", "CW"))
    at_step(9, lambda: next_of("CW", "CY"))
    at_step(10, lambda: next_of("VC", "VX"))
    at_step(10, lambda: next_of("UX", "UY"))
    at_step(11, lambda: next_of("DY", "DZ"))
    at_step(12, far_post)
    at_step(13, lambda: next_of("VX", "VY"))
    at_step(13, lambda: next_of("GC", "GX"))
    at_step(14, lambda: next_of("CY", "CX"))
    at_step(15, lambda: next_of("UY", "UZ"))
    at_step(16, lambda: near(5, normed_in.at[pl.ds(0, rows)], normed).wait())
    at_step(16, lambda: weights_of(0))
    at_step(16, lambda: next_of("DZ", "DW"))
    at_step(17, lambda: next_of("VY", "VZ"))
    at_step(18, lambda: next_of("UZ", "UW"))
    at_step(19, lambda: next_of("Q0Y", "Q0Z"))
    at_step(20, lambda: weights_of(1))
    at_step(20, lambda: arrive("CX"))
    at_step(20, lambda: near(6, tokens_in, tokens).start())
    at_step(20, lambda: near(7, gmid_in, gmid).start())
    at_step(21, lambda: next_of("DW", "DX"))
    at_step(21, lambda: next_of("Q0Z", "Q0W"))
    at_step(22, lambda: next_of("VZ", "VW"))
    at_step(22, lambda: arrive("UW"))
    at_step(23, lambda: next_of("Q1Y", "Q1Z"))
    at_step(23, lambda: next_of("Q0W", "Q0X"))

    gkv, part = score_grads(q_t, gout_t, delta, gout_q, mass, k_ref, v_ref)
    lanes = pl.ds(pl.multiple_of(head * LANES, LANES), LANES)
    gkv_all[pl.ds(pl.multiple_of(block * tile, tile), tile), lanes] = gkv

    @pl.when(step < per_phase)
    def _():
        @pl.when(block == 0)
        def _():
            gq_all[head] = part

        @pl.when(block != 0)
        def _():
            gq_all[head] += part

    @pl.when(step >= per_phase)
    def _():
        gq_all[head] += part

    @pl.when(step == 2 * per_phase - 1)
    def _():
        weights_of(2)

        def gn_of(at):
            spot = slice(at * half, (at + 1) * half)
            return dot_nt(gkv_all[spot, :], wpair_ref[...]) + dot_tn(gq_low[:, spot], wqt_ref[...])

        gn_send[...] = gn_of(1).astype(BF16)
        start("GN")
        gn_own[...] = gn_of(0)
        gkv_now = gkv_sum[...] + jnp.sum(gkv_all[...].astype(F32), axis=0, keepdims=True)
        ones = jnp.ones((8, rows), BF16)
        gq_now = dot_nt(ones, gq_low[...])[:1]
        gq_now = jnp.concatenate([gq_now, jnp.zeros_like(gq_now)], axis=1)
        next_of("Q1Z", "Q1W")
        arrive("GN")
        exchange("GX").wait()
        near(6, tokens_in, tokens).wait()
        rows_now = tokens[...].astype(F32)
        centred = rows_now - jnp.mean(rows_now, axis=-1, keepdims=True)
        inv = lax.rsqrt(jnp.mean(centred * centred, axis=-1, keepdims=True) + EPS_NORM)
        normal = centred * inv
        gn = gn_own[...] + rg[1].astype(F32) + rg[2].astype(F32)
        zero = jnp.zeros((1, width), F32)
        mine = core == 0
        late_out[...] = jnp.concatenate(
            [
                jnp.sum(gn * normal, axis=0, keepdims=True),
                jnp.sum(gn, axis=0, keepdims=True),
                zero,
                zero,
                jnp.where(mine, gq_now, zero),
                jnp.where(mine, zero, gq_now),
                jnp.where(mine, gkv_now, zero),
                jnp.where(mine, zero, gkv_now),
            ],
            axis=0,
        )
        start("LC")
        next_of("Q2Y", "Q2Z")
        next_of("Q1W", "Q1X")
        next_of("LC", "LX")
        near(7, gmid_in, gmid).wait()
        turned = gn * gain_ref[...]
        gtok_out[...] = (
            gmid[...]
            + inv
            * (
                turned
                - jnp.mean(turned, axis=-1, keepdims=True)
                - normal * jnp.mean(turned * normal, axis=-1, keepdims=True)
            )
        ).astype(BF16)
        next_of("Q2Z", "Q2W")
        next_of("LX", "LY")
        arrive("Q0X")
        arrive("Q1X")
        arrive("DX")
        next_of("Q2W", "Q2X")
        next_of("LY", "LZ")
        arrive("Q2X")
        size = HEAD_DIM

        def pick(b, group):
            low = qkv_out[b, :, group * size : (group + 1) * size]
            high = qkv_out[b, :, (group + 3) * size : (group + 4) * size]
            return jnp.where(x == 0, low, high)

        pieces = [jnp.where(mine, pick(b, 2), pick(b, 0)) for b in range(3)]
        pieces.append(jnp.zeros_like(pieces[0]))
        swap_send[...] = jnp.concatenate(pieces, axis=1)
        start("SW")
        next_of("LZ", "LW")
        arrive("VW")
        arrive("SW")
        swap_out[...] = swap_got[...]
        arrive("LW")


def backward(head_arrays, keys, values, sums, early, normed, tokens, gmid, gain, wpair, wqt):
    width, rows = head_arrays[0].shape
    heads = width // LANES
    half = rows // 2
    tile = half
    up, down, pair = sums
    each = up.shape[4]
    down_each, down_width = down.shape[3:]
    grid = 4 * heads
    head_of = lambda n: lax.rem(n, 2 * heads) // 2
    key_spec = pl.BlockSpec(
        (tile, LANES), lambda n: ((1 - n // (2 * heads)) * 2 + lax.rem(n, 2), head_of(n))
    )
    hbm = pl.BlockSpec(memory_space=pl.ANY)
    vmem = pl.BlockSpec(memory_space=pltpu.VMEM)
    low = lambda *s: pltpu.VMEM(s, BF16)
    full = lambda *s: pltpu.VMEM(s, F32)
    qkv_width = width // 2
    outs = [
        jax.ShapeDtypeStruct((each, width), F32),
        jax.ShapeDtypeStruct((down_each, down_width), F32),
        jax.ShapeDtypeStruct((each, width), F32),
        jax.ShapeDtypeStruct(early.shape, BF16),
        jax.ShapeDtypeStruct((3, each, qkv_width), F32),
        jax.ShapeDtypeStruct((each, 256), F32),
        jax.ShapeDtypeStruct((8, width), F32),
        jax.ShapeDtypeStruct((half, width), BF16),
    ]
    return pl.pallas_call(
        backward_kernel,
        grid=(grid,),
        in_specs=head_specs(rows, head_of) + [key_spec, key_spec] + [hbm] * 7
        + [vmem] * 3,
        out_specs=[vmem] * len(outs),
        out_shape=outs,
        scratch_shapes=[
            full(heads, HEAD_DIM, rows),
            low(heads * HEAD_DIM, rows),
            low(rows, width),
            full(width, width),
            low(rows, width),
            low(half, width),
            full(half, width),
            low(2, half, width),
            low(half, width),
            full(half, width),
            full(1, width),
            low(2, 2, 2, each, width),
            low(2, 2, down_each, down_width),
            low(2, 2, each, width),
            low(3, 2, 2, 2, each, qkv_width),
            low(2, 2, 2, each, width),
            low(2, 2, each, width),
            low(2, each, width),
            low(each, width),
            low(2, 2, down_each, down_width),
            low(2, down_each, down_width),
            low(down_each, down_width),
            low(down_each, down_width),
            low(2, 2, each, width),
            low(2, each, width),
            low(each, width),
            low(each, width),
            low(5, *early.shape),
            low(3, 2, 2, each, qkv_width),
            low(3, 2, each, qkv_width),
            low(3, each, qkv_width),
            low(3, each, qkv_width),
            low(3, half, width),
            full(5, 8, width),
            full(each, 256),
            full(each, 256),
            pltpu.SemaphoreType.DMA((len(EXCHANGES),)),
            pltpu.SemaphoreType.DMA((len(EXCHANGES),)),
            pltpu.SemaphoreType.DMA((8,)),
        ],
        compiler_params=pltpu.CompilerParams(
            vmem_limit_bytes=VMEM_LIMIT, collective_id=0, has_side_effects=True
        ),
        cost_estimate=pl.CostEstimate(
            flops=40 * heads * rows * rows * LANES,
            bytes_accessed=40 * MIB,
            transcendentals=2 * heads * rows * rows,
        ),
        name="backward",
    )(*head_arrays, keys, values, up, down, pair, early, normed, tokens, gmid, gain, wpair, wqt)


def finish_kernel(
    up_ref,
    down_ref,
    pair_ref,
    early_ref,
    qkv_ref,
    swap_ref,
    late_ref,
    gtok_ref,
    classes_ref,
    class_ref,
    class_w_ref,
    up_out,
    down_out,
    wout_out,
    patch_out,
    qkv_out,
    class_w_out,
    class_out,
    gtok_out,
    gbias_up_out,
    *rest,
):
    vector_outs, product = rest[:-1], rest[-1]
    seq, grp = lax.axis_index("seq"), lax.axis_index("grp")
    core, x = lax.rem(seq, 2), seq // 2
    gtok_out[...] = gtok_ref[...]
    width = up_ref.shape[1]
    third = width // 4
    each = up_ref.shape[0]
    size = HEAD_DIM
    up_out[...] = up_ref[...]
    down_out[...] = jnp.where(x == 0, down_ref[:, :third], down_ref[:, third:])
    wout_out[...] = jnp.where(x == 0, pair_ref[:, :third], pair_ref[:, third : 2 * third])
    patch_out[...] = jnp.where(x == 0, pair_ref[:, 2 * third : 3 * third], pair_ref[:, 3 * third :])

    def group(j):
        parts = []
        for b in range(3):
            low = qkv_ref[b, :, j * size : (j + 1) * size]
            high = qkv_ref[b, :, (j + 3) * size : (j + 4) * size]
            parts.append(jnp.where(x == 0, low, high))
        return jnp.concatenate(parts, axis=1)

    first, second, last = group(0), group(1), group(2)
    got = swap_ref[:, :third]
    qkv_out[...] = jnp.concatenate(
        [jnp.where(core == 0, first, second), got, jnp.where(core == 0, second, last)], axis=1
    )

    classes = classes_ref[...]
    count = classes.shape[0]
    scale = lax.rsqrt(jnp.sum(classes * classes, axis=-1, keepdims=True) + EPS_UNIT)
    unit = classes * scale
    gunit = early_ref[:count, :].astype(F32)
    gclass = (scale * (gunit - unit * jnp.sum(gunit * unit, axis=-1, keepdims=True))).astype(BF16)
    product[...] = dot_tn(class_ref[...], gclass)
    block = product[pl.ds(grp * each, each), :]
    mine = block[:, :third]
    for s in range(1, 4):
        mine = jnp.where(seq == s, block[:, s * third : (s + 1) * third], mine)
    class_w_out[...] = mine

    def own_lanes(matrix, each):
        total = matrix.shape[1]
        return pltpu.roll(matrix, lax.rem(total - grp * each, total), 1)[:, :each]

    class_out[...] = own_lanes(dot_nt(gclass, class_w_ref[...]), each)
    at = early_ref.shape[0] - 16
    vectors = early_ref[at:, :].astype(F32)
    late = late_ref[...]

    def all_heads(first, second):
        parts = []
        for g in range(2):
            for vector in (first, second):
                parts += [vector[i * 2 + g] for i in range(3)]
        return jnp.concatenate(parts, axis=1)

    def lanes_of(matrix, row, stride, count):
        return [matrix[row : row + 1, i * stride : i * stride + size] for i in range(count)]

    gquery = all_heads(lanes_of(late, 4, size, 6), lanes_of(late, 5, size, 6))
    gvalue = all_heads(lanes_of(late, 6, 2 * size, 6), lanes_of(late, 7, 2 * size, 6))
    packed = jnp.concatenate(
        [vectors[:4], late[:2], gquery, gvalue], axis=0
    )
    mine = own_lanes(packed, each)
    for i, ref in enumerate(vector_outs):
        ref[...] = mine[i : i + 1]
    chunks = gbias_up_out.shape[1] // each
    flat = jnp.concatenate([vectors[4 + i : 5 + i] for i in range(chunks)], axis=1)
    flat = jnp.concatenate([flat] * 8, axis=0)
    gbias_up_out[...] = own_lanes(flat, chunks * each)[:1]


def finish(*operands):
    up, down, pair, early, qkv, _, late, gtok, classes, class_emb, class_w = operands
    each, width = up.shape
    third = width // 4
    hidden_each = down.shape[0]
    shapes = [
        (each, width),
        (hidden_each, third),
        (each, third),
        (each, third),
        (each, 3 * third),
        (each, third),
        (classes.shape[0], each),
        gtok.shape,
        (1, hidden_each),
    ] + [(1, each)] * 8
    vmem = pl.BlockSpec(memory_space=pltpu.VMEM)
    return pl.pallas_call(
        finish_kernel,
        in_specs=[vmem] * len(operands),
        out_specs=[vmem] * len(shapes),
        out_shape=[jax.ShapeDtypeStruct(s, BF16 if s == gtok.shape else F32) for s in shapes],
        scratch_shapes=[pltpu.VMEM((width, width), F32)],
        compiler_params=pltpu.CompilerParams(vmem_limit_bytes=VMEM_LIMIT),
        name="finish",
    )(*operands)


def layer_norm(matrix_rows, gain_vec, shift_vec):
    row_mean = jnp.mean(matrix_rows, axis=-1, keepdims=True)
    centred = matrix_rows - row_mean
    row_var = jnp.mean(centred * centred, axis=-1, keepdims=True)
    return centred * lax.rsqrt(row_var + EPS_NORM) * gain_vec + shift_vec


def unit_rows(matrix_rows):
    return matrix_rows * lax.rsqrt(
        jnp.sum(matrix_rows * matrix_rows, axis=-1, keepdims=True) + EPS_UNIT
    )


def column_sum(matrix_low):
    return jnp.sum(matrix_low.astype(F32), axis=0)


def swap(value, axis, bit):
    size = lax.axis_size(axis)
    return lax.ppermute(value, axis, [(i, i ^ bit) for i in range(size)])


def add_low(first, second):
    return (first.astype(F32) + second.astype(F32)).astype(BF16)


def sum_rows(part):
    groups = lax.axis_size("grp")
    bits = groups.bit_length() - 1
    here = lax.axis_index("grp")
    each = part.shape[0] // groups
    width = part.shape[1]
    part = part.reshape((2,) * bits + (each, width))
    for name in range(bits):
        axis = bits - 1 - name
        mine = (here >> name) & 1
        send = lax.dynamic_index_in_dim(part, 1 - mine, axis, keepdims=True)
        keep = lax.dynamic_index_in_dim(part, mine, axis, keepdims=True)
        part = add_low(keep, swap(send, "grp", 1 << name))
    return part.reshape(each, width)


def sum_x(part, x_here):
    half = part.shape[1] // 2
    low, high = part[:, :half], part[:, half:]
    mine = jnp.where(x_here == 0, low, high)
    other = jnp.where(x_here == 0, high, low)
    return mine.astype(F32) + swap(other, "seq", 2).astype(F32)


def body(
    tokens_in,
    lengths,
    ln1_gain,
    ln1_bias,
    w_qkv,
    bias_query,
    bias_value,
    w_out,
    bias_out,
    ln2_gain,
    ln2_bias,
    w_up,
    bias_up,
    w_down,
    bias_down,
    proj_patch,
    proj_class,
    class_emb,
    d_masks,
):
    row_count, model_width = tokens_in.shape
    head_count = model_width // HEAD_DIM
    heads_here = head_count // 2
    third = model_width // 4
    seq_devices = lax.axis_size("seq")
    grp_devices = lax.axis_size("grp")
    seq_here = lax.axis_index("seq")
    grp_here = lax.axis_index("grp")
    core = seq_here & 1
    x_here = seq_here >> 1
    row = lambda vector: vector.reshape(1, -1)

    tokens_x = swap(tokens_in, "seq", 2)
    normed_image, w_kv, value_bias, w_pairs, w_query_t, queries_t, gout_q, keys, values = project_near(
        lengths, tokens_in, row(ln1_gain), row(ln1_bias), w_qkv, row(bias_query), row(bias_value)
    )
    partial, near_top = attend_forward(attend_near_kernel, "attend_near", queries_t, keys, values)
    tokens_x, partial = lax.optimization_barrier((tokens_x, partial))
    normed_image, keys, values = project_far(
        lengths,
        tokens_x,
        row(ln1_gain),
        row(ln1_bias),
        w_kv,
        value_bias,
        (normed_image, keys, values),
    )
    att_own, att_other, mass = attend_forward(
        attend_far_kernel, "attend_far", queries_t, keys, values, partial, near_top
    )
    att_got = swap(att_other, "seq", 1)
    (
        mask_out,
        joined,
        normed_two,
        active,
        grad_hidden,
        final_low,
        grad_patches,
        grad_feed,
        grad_branch,
        grad_branch_p,
        grad_middle,
        early,
        classes,
    ) = middle(
        lengths,
        tokens_in,
        att_own,
        att_got,
        d_masks,
        (
            w_out,
            row(bias_out),
            row(ln2_gain),
            row(ln2_bias),
            w_up,
            row(bias_up),
            w_down,
            row(bias_down),
            proj_patch,
            proj_class,
            class_emb,
        ),
    )
    up_sum, down_sum, pair_sum, gout_q, gouts_t, delta = weights(
        gout_q,
        normed_two,
        grad_hidden,
        active,
        grad_feed,
        joined,
        grad_branch,
        grad_branch_p,
        final_low,
        grad_patches,
        w_out,
        att_own,
        att_other,
    )
    head_arrays = (queries_t, gouts_t, delta, gout_q, mass)
    down_sum = down_sum.reshape(bias_up.shape[0], model_width // 2)
    rows_each = model_width // grp_devices
    ff_each = bias_up.shape[0] // grp_devices
    cols_each = model_width // seq_devices

    if grp_devices == 8 and rows_each % 16 == 0:
        sums = (
            up_sum.reshape(2, 2, 2, 2, rows_each, -1),
            down_sum.reshape(2, 2, 2, ff_each, -1),
            pair_sum.reshape(2, 2, 2, rows_each, -1),
        )
        raw = backward(
            head_arrays,
            keys,
            values,
            sums,
            early,
            normed_image,
            tokens_in,
            grad_middle,
            row(ln1_gain),
            w_pairs,
            w_query_t,
        )
        (
            out_w_up,
            out_w_down,
            out_w_out,
            out_proj_patch,
            out_w_qkv,
            grad_proj_class,
            grad_class_emb,
            grad_tokens,
            out_bias_up,
            *vectors,
        ) = finish(*raw, classes, class_emb, proj_class)
        vectors = [vector[0] for vector in vectors]
        return (
            mask_out,
            grad_tokens,
            vectors[4],
            vectors[5],
            out_w_qkv,
            vectors[6],
            vectors[7],
            out_w_out,
            vectors[1],
            vectors[2],
            vectors[3],
            out_w_up,
            out_bias_up[0],
            out_w_down,
            vectors[0],
            out_proj_patch,
            grad_proj_class,
            grad_class_emb,
        )

    out_w_down = sum_x(sum_rows(down_sum), x_here)
    out_w_up = sum_rows(add_low(up_sum[0], swap(up_sum[1], "seq", 2))).astype(F32)
    pair_rows = sum_rows(pair_sum)
    out_w_out = sum_x(pair_rows[:, : 2 * third], x_here)
    out_proj_patch = sum_x(pair_rows[:, 2 * third :], x_here)
    early = lax.psum(early.astype(F32), ("grp", "seq"))
    class_total = early[: class_emb.shape[0]]
    vectors = early[-16:]
    gq_t, gkv = attend_backward(*head_arrays, keys, values)

    gq = gq_t.T
    gn_far = dot_nt(gkv[2 * row_count :], w_pairs)
    gn_near = dot_nt(gkv[: 2 * row_count], w_pairs) + dot_nn(gq, w_query_t)
    far_got = swap(gn_far[row_count:].astype(BF16), "seq", 1)
    far_sum = (gn_far[:row_count] + far_got.astype(F32)).astype(BF16)
    near_got = swap(gn_near[row_count:].astype(BF16), "seq", 1)
    x_got = swap(far_sum, "seq", 2)
    grad_normed_one = gn_near[:row_count] + near_got.astype(F32) + x_got.astype(F32)
    norm_one_back = jax.vjp(layer_norm, tokens_in.astype(F32), ln1_gain, ln1_bias)[1]
    grad_tokens_norm, grad_ln1_gain, grad_ln1_bias = norm_one_back(grad_normed_one)
    grad_tokens = (grad_middle + grad_tokens_norm).astype(BF16)

    dw_q = dot_tn(normed_image[: 2 * row_count], gq).reshape(model_width, 3, 2, HEAD_DIM)
    dw_kv = dot_tn(normed_image, gkv).reshape(model_width, 3, 2, 2, HEAD_DIM)
    three = lambda matrix: matrix.reshape(model_width, third)
    part_zero = [three(dw_q[:, :, 0]), three(dw_q[:, :, 1]), three(dw_kv[:, :, 0, 1])]
    part_one = [three(dw_kv[:, :, 1, 1]), three(dw_kv[:, :, 0, 0]), three(dw_kv[:, :, 1, 0])]
    part_zero = jnp.concatenate(part_zero, axis=1).astype(BF16)
    part_one = jnp.concatenate(part_one, axis=1).astype(BF16)
    qkv_mine = jnp.where(x_here == 0, part_zero, part_one)
    qkv_other = jnp.where(x_here == 0, part_one, part_zero)
    qkv_rows = sum_rows(add_low(qkv_mine, swap(qkv_other, "seq", 2))).astype(F32)
    pieces = [qkv_rows[:, i * third : (i + 1) * third] for i in range(3)]
    piece_got = swap(jnp.where(core == 0, pieces[2], pieces[0]), "seq", 1)
    out_w_qkv = jnp.concatenate(
        [
            jnp.where(core == 0, pieces[0], pieces[1]),
            piece_got,
            jnp.where(core == 0, pieces[1], pieces[2]),
        ],
        axis=1,
    )

    def put_back(vector):
        halves = vector.reshape(3, 2, HEAD_DIM).swapaxes(0, 1).reshape(2, 1, third)
        zero = jnp.zeros_like(halves)
        both = jnp.where(
            core == 0,
            jnp.concatenate([halves, zero], axis=1),
            jnp.concatenate([zero, halves], axis=1),
        )
        return both.reshape(model_width)

    grad_bias_query = put_back(column_sum(gq))
    gkv_sums = column_sum(gkv).reshape(heads_here, 2, HEAD_DIM)
    grad_bias_value = put_back(gkv_sums[:, 0].reshape(heads_here * HEAD_DIM))
    late = jnp.stack([grad_ln1_gain, grad_ln1_bias, grad_bias_query, grad_bias_value], axis=1)
    late = jnp.concatenate([late, jnp.zeros((model_width, LANES - 4), F32)], axis=1).astype(BF16)
    late = add_low(late, swap(late, "seq", 1))
    late = sum_rows(add_low(late, swap(late, "seq", 2))).astype(F32)

    class_back = jax.vjp(unit_rows, classes)[1]
    grad_classes = class_back(class_total)[0].astype(BF16)

    def vector_rows(index):
        return lax.dynamic_slice_in_dim(vectors[index], grp_here * rows_each, rows_each, 0)

    out_bias_up = lax.dynamic_slice_in_dim(
        vectors[4 : 4 + bias_up.shape[0] // model_width].reshape(-1), grp_here * ff_each, ff_each, 0
    )
    emb_cols = lax.dynamic_slice_in_dim(class_emb, grp_here * rows_each, rows_each, 1)
    class_cols = lax.dynamic_slice_in_dim(grad_classes, seq_here * cols_each, cols_each, 1)
    grad_proj_class = dot_tn(emb_cols, class_cols)
    proj_rows = lax.dynamic_slice_in_dim(proj_class, grp_here * rows_each, rows_each, 0)
    grad_class_emb = dot_nt(grad_classes, proj_rows)
    return (
        mask_out,
        grad_tokens,
        late[:, 0],
        late[:, 1],
        out_w_qkv,
        late[:, 2],
        late[:, 3],
        out_w_out,
        vector_rows(1),
        vector_rows(2),
        vector_rows(3),
        out_w_up,
        out_bias_up,
        out_w_down,
        vector_rows(0),
        out_proj_patch,
        grad_proj_class,
        grad_class_emb,
    )


def solution(mesh):
    rows = P(("grp", "seq"), None)
    both = P("grp", "seq")
    return jax.shard_map(
        body,
        mesh=mesh,
        in_specs=(rows, P("grp")) + (P(),) * 16 + (rows,),
        out_specs=(
            rows,
            rows,
            P("grp"),
            P("grp"),
            both,
            P("grp"),
            P("grp"),
            both,
            P("grp"),
            P("grp"),
            P("grp"),
            both,
            P("grp"),
            both,
            P("grp"),
            both,
            both,
            P(None, "grp"),
        ),
        check_vma=False,
    )
```

```python
import functools
import math

import jax
import jax.numpy as jnp
from jax import lax
from jax.experimental import pallas as pl
from jax.experimental.pallas import tpu as pltpu
from jax.sharding import PartitionSpec as P

HEAD_DIM = 64
LANES = 128
EPS_NORM = 1e-06
EPS_UNIT = 1e-06
NEG_FILL = -1e30
LOG2E = math.log2(math.e)
F32 = jnp.float32
BF16 = jnp.bfloat16
MIB = 1 << 20
VMEM_LIMIT = 63 * MIB
MESH = pl.DeviceIdType.MESH


def dot_nn(a, b):
    return lax.dot_general(a, b, (((1,), (0,)), ((), ())), preferred_element_type=F32)


def dot_nt(a, b):
    return lax.dot_general(a, b, (((1,), (1,)), ((), ())), preferred_element_type=F32)


def dot_tn(a, b):
    return lax.dot_general(a, b, (((0,), (0,)), ((), ())), preferred_element_type=F32)


def swap_tokens(seq, src, dst, send, recv):
    return pltpu.make_async_remote_copy(
        src_ref=src,
        dst_ref=dst,
        send_sem=send,
        recv_sem=recv,
        device_id={"seq": seq + 1 - 2 * lax.rem(seq, 2)},
        device_id_type=MESH,
    )


def greet_core(seq):
    peer = {"seq": seq + 1 - 2 * lax.rem(seq, 2)}
    pl.semaphore_signal(
        pltpu.get_barrier_semaphore(), inc=1, device_id=peer, device_id_type=MESH
    )


def await_core():
    pl.semaphore_wait(pltpu.get_barrier_semaphore(), 1)


def normed_tile(step, per, own_ref, got, out_ref, gain_ref, shift_ref):
    tile = out_ref.shape[0]
    row = lax.rem(step, per) * tile

    @pl.when(step < per)
    def _():
        out_ref[...] = own_ref[pl.ds(pl.multiple_of(row, tile), tile), :]

    @pl.when(step >= per)
    def _():
        out_ref[...] = got[pl.ds(pl.multiple_of(row, tile), tile), :]

    rows = out_ref[...].astype(F32)
    centred = rows - jnp.mean(rows, axis=-1, keepdims=True)
    var = jnp.mean(centred * centred, axis=-1, keepdims=True)
    normed = centred * lax.rsqrt(var + EPS_NORM) * as_row(gain_ref) + as_row(shift_ref)
    normed = normed.astype(BF16)
    out_ref[...] = normed
    return normed, row


def spread(matrix, upper):
    zero = jnp.zeros((matrix.shape[0], HEAD_DIM), matrix.dtype)
    parts = []
    for at in range(0, matrix.shape[1], HEAD_DIM):
        piece = matrix[:, at : at + HEAD_DIM]
        parts += [zero, piece] if upper else [piece, zero]
    return jnp.concatenate(parts, axis=1)


def column_is(column, width):
    at = lax.broadcasted_iota(jnp.int32, (1, width), 1)
    return jnp.where(lax.rem(at, LANES) == column, 1.0, 0.0)


def key_mask(length, first_row, shape):
    where_row = lax.broadcasted_iota(jnp.int32, (shape[0], 1), 0) + first_row
    masked = jnp.where(where_row < length, 0.0, NEG_FILL)
    return masked * column_is(0, shape[1])


def keys_values(normed, mask, wkv_ref, vbias_ref, k_ref, v_ref):
    width = k_ref.shape[1]
    both = dot_nn(normed, wkv_ref[...])
    k_ref[...] = (spread(both[:, : width // 2], True) + mask).astype(BF16)
    value = spread(both[:, width // 2 :] + vbias_ref[...], False)
    v_ref[...] = (value + column_is(HEAD_DIM, width)).astype(BF16)


def project_near_kernel(
    lengths_ref,
    own_ref,
    gain_ref,
    shift_ref,
    w_ref,
    bias_query_ref,
    bias_value_ref,
    normed_ref,
    wkv_ref,
    vbias_ref,
    wpair_ref,
    wqt_ref,
    q_t_ref,
    gout_q_ref,
    k_ref,
    v_ref,
    wq,
    qbias,
    got,
    send,
    recv,
):
    step = pl.program_id(0)
    seq = lax.axis_index("seq")
    core = lax.rem(seq, 2)
    width = normed_ref.shape[1]
    tile = normed_ref.shape[0]
    rows = own_ref.shape[0]
    per = rows // tile

    @pl.when(step == 0)
    def _():
        greet_core(seq)
        bias_query, bias_value = as_row(bias_query_ref), as_row(bias_value_ref)
        for which in range(2):

            @pl.when(core == which)
            def _():
                rows_q, rows_v, queries, keys, values, pairs = [], [], [], [], [], []
                for head in range(width // LANES):
                    within, group = divmod(head, 2)
                    at = (2 * group + which) * (width // 4) + within * HEAD_DIM
                    spot = slice(at, at + HEAD_DIM)
                    queries.append(w_ref[:, spot])
                    keys.append(w_ref[:, width + at : width + at + HEAD_DIM])
                    values.append(w_ref[:, 2 * width + at : 2 * width + at + HEAD_DIM])
                    pairs += [values[-1], keys[-1]]
                    rows_q.append(bias_query[:, spot])
                    rows_v.append(bias_value[:, spot])
                together = jnp.concatenate(queries, axis=1)
                wq[...] = together
                wqt_ref[...] = together.T
                wkv_ref[...] = jnp.concatenate(keys + values, axis=1)
                wpair_ref[...] = jnp.concatenate(pairs, axis=1)
                qbias[...] = jnp.concatenate(rows_q, axis=1)
                vbias_ref[...] = jnp.concatenate(rows_v, axis=1)

        await_core()
        swap_tokens(seq, own_ref, got, send, recv).start()

    @pl.when(step == per)
    def _():
        swap_tokens(seq, own_ref, got, send, recv).wait()

    normed, row = normed_tile(step, per, own_ref, got, normed_ref, gain_ref, shift_ref)
    block = step // per
    place = seq + block * (1 - 2 * core)
    mixed = (dot_nn(normed, wq[...]) + qbias[...]).astype(BF16).astype(F32)
    query = spread(mixed * HEAD_DIM**-0.5, True)
    gout_q_ref[...] = query.astype(BF16)
    q_t_ref[...] = (query + column_is(0, width)).astype(BF16).T
    mask = key_mask(lengths_ref[0], place * rows + row, k_ref.shape)
    keys_values(normed, mask, wkv_ref, vbias_ref, k_ref, v_ref)


def project_far_kernel(
    lengths_ref,
    own_ref,
    gain_ref,
    shift_ref,
    wkv_ref,
    vbias_ref,
    normed_in,
    k_in,
    v_in,
    normed_ref,
    k_ref,
    v_ref,
    got,
    send,
    recv,
):
    step = pl.program_id(0)
    seq = lax.axis_index("seq")
    core = lax.rem(seq, 2)
    width = normed_ref.shape[1]
    tile = normed_ref.shape[0]
    rows = own_ref.shape[0]
    per = rows // tile

    @pl.when(step == 0)
    def _():
        greet_core(seq)
        await_core()
        swap_tokens(seq, own_ref, got, send, recv).start()

    @pl.when(step == per)
    def _():
        swap_tokens(seq, own_ref, got, send, recv).wait()

    normed, row = normed_tile(step, per, own_ref, got, normed_ref, gain_ref, shift_ref)
    block = step // per
    place = seq + 2 - 4 * (seq // 2) + block * (1 - 2 * core)
    mask = key_mask(lengths_ref[0], place * rows + row, k_ref.shape)
    keys_values(normed, mask, wkv_ref, vbias_ref, k_ref, v_ref)


def as_row(ref):
    return ref[...].reshape(1, -1)


def whole(a):
    return pl.BlockSpec(a.shape, lambda *_: (0,) * len(a.shape))


def project_near(lengths, tokens, gain, shift, w_qkv, bias_query, bias_value):
    rows, width = tokens.shape
    tile = rows // 2
    shape = lambda *s: jax.ShapeDtypeStruct(s, BF16)
    tiled = pl.BlockSpec((tile, width), lambda i: (i, 0))
    image = shape(4 * rows, width)
    outs = [
        image,
        shape(width, width),
        jax.ShapeDtypeStruct((1, width // 2), F32),
        shape(width, width),
        shape(width // 2, width),
        shape(width, 2 * rows),
        image,
        image,
        image,
    ]
    return pl.pallas_call(
        project_near_kernel,
        grid=(4,),
        in_specs=[pl.BlockSpec(memory_space=pltpu.SMEM)]
        + [whole(a) for a in (tokens, gain, shift, w_qkv, bias_query, bias_value)],
        out_specs=[
            tiled,
            whole(outs[1]),
            whole(outs[2]),
            whole(outs[3]),
            whole(outs[4]),
            pl.BlockSpec((width, tile), lambda i: (0, i)),
            pl.BlockSpec((tile, width), lambda i: (i + 4, 0)),
            tiled,
            tiled,
        ],
        out_shape=outs,
        scratch_shapes=[
            pltpu.VMEM((width, width // 2), BF16),
            pltpu.VMEM((1, width // 2), F32),
            pltpu.VMEM((rows, width), BF16),
            pltpu.SemaphoreType.DMA,
            pltpu.SemaphoreType.DMA,
        ],
        compiler_params=pltpu.CompilerParams(
            vmem_limit_bytes=VMEM_LIMIT, collective_id=2, has_side_effects=True
        ),
        cost_estimate=pl.CostEstimate(
            flops=12 * rows * width * width, bytes_accessed=20 * MIB, transcendentals=0
        ),
        name="project_near",
    )(lengths, tokens, gain, shift, w_qkv, bias_query, bias_value)


def project_far(lengths, tokens, gain, shift, wkv, vbias, images):
    rows, width = tokens.shape
    tile = rows // 2
    tiled = pl.BlockSpec((tile, width), lambda i: (i + 4, 0))
    return pl.pallas_call(
        project_far_kernel,
        grid=(4,),
        in_specs=[pl.BlockSpec(memory_space=pltpu.SMEM)]
        + [whole(a) for a in (tokens, gain, shift, wkv, vbias)]
        + [pl.BlockSpec(memory_space=pl.ANY)] * 3,
        out_specs=[tiled] * 3,
        out_shape=[jax.ShapeDtypeStruct(a.shape, a.dtype) for a in images],
        input_output_aliases={6: 0, 7: 1, 8: 2},
        scratch_shapes=[
            pltpu.VMEM((rows, width), BF16),
            pltpu.SemaphoreType.DMA,
            pltpu.SemaphoreType.DMA,
        ],
        compiler_params=pltpu.CompilerParams(
            vmem_limit_bytes=VMEM_LIMIT, collective_id=3, has_side_effects=True
        ),
        cost_estimate=pl.CostEstimate(
            flops=8 * rows * width * width, bytes_accessed=16 * MIB, transcendentals=0
        ),
        name="project_far",
    )(lengths, tokens, gain, shift, wkv, vbias, *images)


PART = 72


def attend_near_kernel(q_t_ref, k_ref, v_ref, part_ref, top_ref):
    scores = dot_nn(k_ref[...], q_t_ref[...])
    top = jnp.max(scores, axis=0, keepdims=True)
    prob = jnp.exp2((scores - top) * LOG2E).astype(BF16)
    part_ref[...] = dot_tn(v_ref[...], prob)[:PART]
    top_ref[0] = top


def attend_far_kernel(q_t_ref, k_ref, v_ref, part_ref, near_top_ref, own_ref, other_ref, mass_ref):
    scores = dot_nn(k_ref[...], q_t_ref[...])
    near_top = near_top_ref[0]
    top = jnp.maximum(jnp.max(scores, axis=0, keepdims=True), near_top)
    prob = jnp.exp2((scores - top) * LOG2E).astype(BF16)
    summed = dot_tn(v_ref[...], prob)[:PART]
    summed = summed + part_ref[...] * jnp.exp2((near_top - top) * LOG2E)
    total = summed[HEAD_DIM : HEAD_DIM + 1]
    mass_ref[0] = top * LOG2E + jnp.log2(total)
    out = (summed[:HEAD_DIM] / total).astype(BF16)
    half = own_ref.shape[1]
    own_ref[...] = out[:, :half]
    other_ref[...] = out[:, half:]


def attend_cost(heads, rows, span):
    return pl.CostEstimate(
        flops=8 * heads * rows * span * LANES,
        bytes_accessed=(rows + 2 * span) * heads * LANES * 2,
        transcendentals=heads * rows * span,
    )


def attend_forward(kernel, name, queries_t, keys, values, *partial):
    width, rows = queries_t.shape
    span = keys.shape[0] // 2
    heads = width // LANES
    at = 1 if partial else 0
    part_spec = pl.BlockSpec((PART, rows), lambda h: (h, 0))
    row_spec = pl.BlockSpec((1, 1, rows), lambda h: (h, 0, 0))
    row_shape = jax.ShapeDtypeStruct((heads, 1, rows), F32)
    if partial:
        out_specs = [pl.BlockSpec((HEAD_DIM, rows // 2), lambda h: (h, 0))] * 2 + [row_spec]
        outs = [jax.ShapeDtypeStruct((heads * HEAD_DIM, rows // 2), BF16)] * 2 + [row_shape]
    else:
        out_specs = [part_spec, row_spec]
        outs = [jax.ShapeDtypeStruct((heads * PART, rows), F32), row_shape]
    return pl.pallas_call(
        kernel,
        grid=(heads,),
        in_specs=[
            pl.BlockSpec((LANES, rows), lambda h: (h, 0)),
            pl.BlockSpec((span, LANES), lambda h: (at, h)),
            pl.BlockSpec((span, LANES), lambda h: (at, h)),
        ]
        + [part_spec, row_spec][: len(partial)],
        out_specs=out_specs,
        out_shape=outs,
        compiler_params=pltpu.CompilerParams(vmem_limit_bytes=VMEM_LIMIT),
        cost_estimate=attend_cost(heads, rows, span),
        name=name,
    )(queries_t, keys, values, *partial)


def score_grads(q_t_ref, gout_t_ref, delta_ref, gout_q_ref, mass_ref, k_ref, v_ref):
    key_now = k_ref[...]
    scores = dot_nn(key_now, q_t_ref[...])
    prob = jnp.exp2(scores * LOG2E - mass_ref[0])
    gprob = dot_nn(v_ref[...], gout_t_ref[...])
    gscore = (prob * (gprob - delta_ref[0])).astype(BF16)
    gkv = dot_nn(jnp.concatenate([prob.astype(BF16), gscore], axis=1), gout_q_ref[...])
    return gkv.astype(BF16), dot_tn(key_now, gscore)[HEAD_DIM:]


def head_specs(rows, head_of):
    return [
        pl.BlockSpec((LANES, rows), lambda *n: (head_of(*n), 0)),
        pl.BlockSpec((LANES, rows), lambda *n: (head_of(*n), 0)),
        pl.BlockSpec((1, 1, rows), lambda *n: (head_of(*n), 0, 0)),
        pl.BlockSpec((2 * rows, LANES), lambda *n: (0, head_of(*n))),
        pl.BlockSpec((1, 1, rows), lambda *n: (head_of(*n), 0, 0)),
    ]


def attend_backward_kernel(q_t, gout_t, delta, gout_q, mass, k_ref, v_ref, gq_ref, gkv_ref, gq_sum):
    step = pl.program_id(1)
    gkv_ref[...], part = score_grads(q_t, gout_t, delta, gout_q, mass, k_ref, v_ref)

    @pl.when(step == 0)
    def _():
        gq_sum[...] = part

    @pl.when(step > 0)
    def _():
        gq_sum[...] += part

    @pl.when(step == pl.num_programs(1) - 1)
    def _():
        gq_ref[...] = (gq_sum[...] * HEAD_DIM**-0.5).astype(BF16)


def attend_backward(queries_t, gouts_t, delta, gout_q, mass, keys, values):
    width, rows = queries_t.shape
    span = keys.shape[0]
    heads = width // LANES
    tile = span // 4
    key_spec = pl.BlockSpec((tile, LANES), lambda h, j: (j, h))
    return pl.pallas_call(
        attend_backward_kernel,
        grid=(heads, span // tile),
        in_specs=head_specs(rows, lambda h, j: h) + [key_spec, key_spec],
        out_specs=[
            pl.BlockSpec((HEAD_DIM, rows), lambda h, j: (h, 0)),
            pl.BlockSpec((tile, LANES), lambda h, j: (j, h)),
        ],
        out_shape=[
            jax.ShapeDtypeStruct((heads * HEAD_DIM, rows), BF16),
            jax.ShapeDtypeStruct((span, width), BF16),
        ],
        scratch_shapes=[pltpu.VMEM((HEAD_DIM, rows), F32)],
        compiler_params=pltpu.CompilerParams(vmem_limit_bytes=VMEM_LIMIT),
        name="attend_backward",
    )(queries_t, gouts_t, delta, gout_q, mass, keys, values)


def erf_parts(u):
    size = jnp.abs(u)
    t = 1.0 / (1.0 + 0.2316418882 * size)
    bell = jnp.exp2(u * u * (-0.5 * LOG2E))
    poly = 0.5306027144 * t - 0.7265760135
    poly = poly * t + 0.7107068705
    poly = poly * t - 0.1422483683
    poly = poly * t + 0.1274147959
    tail = poly * t * bell
    return jnp.where(u < 0.0, tail, 1.0 - tail), bell * (2.0 * math.pi) ** -0.5


def core_order(matrix):
    width = matrix.shape[1] // 4
    return jnp.concatenate(
        [matrix[:, b * width : (b + 1) * width] for b in (0, 2, 1, 3)], axis=1
    )


def middle_kernel(
    lengths_ref,
    tok_ref,
    att_ref,
    other_in,
    dmask_ref,
    w_out_ref,
    bias_out_ref,
    gain_ref,
    shift_ref,
    w_up_in,
    bias_up_ref,
    w_down_in,
    bias_down_ref,
    patch_w_in,
    class_w_ref,
    class_ref,
    mask_ref,
    joined_ref,
    normed_ref,
    active_ref,
    ghid_ref,
    final_ref,
    gpatch_ref,
    gfeed_ref,
    gbranch_ref,
    gbranch_p_ref,
    gmid_ref,
    early_ref,
    classes_ref,
    slope,
    class_low,
    class_part_ref,
    gbias_down_ref,
    gbias_up_ref,
    gbias_out_ref,
    ggain_ref,
    gshift_ref,
    w_up_ref,
    w_down_ref,
    patch_w_ref,
    got_ref,
    load,
    send,
    recv,
):
    step = pl.program_id(0)
    seq = lax.axis_index("seq")
    moves = ((w_up_in, w_up_ref), (w_down_in, w_down_ref), (patch_w_in, patch_w_ref))
    loads = [pltpu.make_async_copy(a, b, load.at[i]) for i, (a, b) in enumerate(moves)]
    core = lax.rem(seq, 2)
    tile, width = tok_ref.shape
    third = width // 4
    scale = math.sqrt(width)
    chunks = w_up_ref.shape[1] // width

    @pl.when(step == 0)
    def _():
        greet_core(seq)
        for copy in loads:
            copy.start()
        await_core()
        swap_tokens(seq, other_in, got_ref, send, recv).start()
        classes = dot_nn(class_ref[...], class_w_ref[...])
        classes_ref[...] = classes
        class_low[...] = (
            classes * lax.rsqrt(jnp.sum(classes * classes, axis=-1, keepdims=True) + EPS_UNIT)
        ).astype(BF16)
        for ref in (class_part_ref, gbias_down_ref, gbias_up_ref, gbias_out_ref, ggain_ref, gshift_ref):
            ref[...] = jnp.zeros_like(ref)

    @pl.when(step == 0)
    def _():
        swap_tokens(seq, other_in, got_ref, send, recv).wait()

    here = pl.ds(pl.multiple_of(step * tile, tile), tile)
    for head in range(width // LANES):
        within, group = divmod(head, 2)
        at = 2 * group * third + within * HEAD_DIM
        own = slice(head * HEAD_DIM, (head + 1) * HEAD_DIM)
        joined_ref[pl.ds(at + core * third, HEAD_DIM), :] = att_ref[own, :]
        joined_ref[pl.ds(at + (1 - core) * third, HEAD_DIM), :] = got_ref[own, here]
    branch = dot_tn(joined_ref[...], w_out_ref[...]) + as_row(bias_out_ref)
    middle = tok_ref[...].astype(F32) + branch
    centred = middle - jnp.mean(middle, axis=-1, keepdims=True)
    inv = lax.rsqrt(jnp.mean(centred * centred, axis=-1, keepdims=True) + EPS_NORM)
    normal = centred * inv
    normed = (normal * as_row(gain_ref) + as_row(shift_ref)).astype(BF16)
    normed_ref[...] = normed
    bias_up = as_row(bias_up_ref)

    def ready(at):
        @pl.when(step == 0)
        def _():
            loads[at].wait()

    ready(0)
    final = middle + as_row(bias_down_ref)
    for chunk in range(chunks):
        cols = slice(chunk * width, (chunk + 1) * width)
        hidden = dot_nn(normed, w_up_ref[:, cols]) + bias_up[:, cols]
        below, density = erf_parts(hidden)
        active = (hidden * below).astype(BF16)
        active_ref[:, cols] = active
        slope[:, cols] = below + hidden * density
        if chunk == 0:
            ready(1)
        final = final + dot_nn(active, w_down_ref[cols, :])
    final_low = final.astype(BF16)
    final_ref[...] = final_low
    ready(2)
    patches = dot_nn(final_low, patch_w_ref[...])
    unit_scale = lax.rsqrt(jnp.sum(patches * patches, axis=-1, keepdims=True) + EPS_UNIT)
    unit = patches * unit_scale
    unit_low = unit.astype(BF16)
    first_row = seq * (tile * pl.num_programs(0)) + step * tile
    where_lane = lax.broadcasted_iota(jnp.int32, (1, tile), 1) + first_row
    valid = jnp.where(where_lane < lengths_ref[0], 1.0, 0.0)
    mask_ref[...] = (dot_nt(class_low[...], unit_low) * (scale * valid)).astype(BF16)
    gmask = (dmask_ref[...].astype(F32) * valid).astype(BF16)
    class_part_ref[...] += dot_nn(gmask, unit_low) * scale
    gunit = dot_tn(gmask, class_low[...]) * scale
    gpatch = (
        unit_scale * (gunit - unit * jnp.sum(gunit * unit, axis=-1, keepdims=True))
    ).astype(BF16)
    gpatch_ref[...] = core_order(gpatch)
    gfinal = dot_nt(gpatch, patch_w_ref[...])
    gfeed = gfinal.astype(BF16)
    gfeed_ref[...] = core_order(gfeed)
    gbias_down_ref[...] += jnp.sum(gfeed.astype(F32), axis=0, keepdims=True)
    gnormed = jnp.zeros((tile, width), F32)
    for chunk in range(chunks):
        cols = slice(chunk * width, (chunk + 1) * width)
        ghidden = (dot_nt(gfeed, w_down_ref[cols, :]) * slope[:, cols]).astype(BF16)
        ghid_ref[:, cols] = ghidden
        gbias_up_ref[:, cols] += jnp.sum(ghidden.astype(F32), axis=0, keepdims=True)
        gnormed = gnormed + dot_nt(ghidden, w_up_ref[:, cols])
    ggain_ref[...] += jnp.sum(gnormed * normal, axis=0, keepdims=True)
    gshift_ref[...] += jnp.sum(gnormed, axis=0, keepdims=True)
    turned = gnormed * as_row(gain_ref)
    gmid = gfinal + inv * (
        turned
        - jnp.mean(turned, axis=-1, keepdims=True)
        - normal * jnp.mean(turned * normal, axis=-1, keepdims=True)
    )
    gmid_ref[...] = gmid
    gbranch = gmid.astype(BF16)
    gbranch_ref[...] = gbranch
    gbranch_p_ref[...] = core_order(gbranch)
    gbias_out_ref[...] += jnp.sum(gbranch.astype(F32), axis=0, keepdims=True)

    @pl.when(step == pl.num_programs(0) - 1)
    def _():
        class_rows = class_part_ref.shape[0]
        at = early_ref.shape[0] - 16
        early_ref[...] = jnp.zeros_like(early_ref)
        early_ref[:class_rows, :] = class_part_ref[...].astype(BF16)
        parts = [gbias_down_ref[...], gbias_out_ref[...], ggain_ref[...], gshift_ref[...]]
        parts += [gbias_up_ref[:, i * width : (i + 1) * width] for i in range(chunks)]
        parts += [jnp.zeros_like(gbias_down_ref)] * (16 - len(parts))
        early_ref[at:, :] = jnp.concatenate(parts, axis=0).astype(BF16)


def middle(lengths, tokens, att_own, att_other, d_masks, params):
    rows, width = tokens.shape
    tile = rows // 2
    classes = d_masks.shape[0]
    hidden = params[4].shape[1]
    full = lambda a: pl.BlockSpec(a.shape, lambda i: (0,) * len(a.shape))
    tiled = lambda n: pl.BlockSpec((tile, n), lambda i: (i, 0))
    turned = lambda n: pl.BlockSpec((n, tile), lambda i: (0, i))
    shape = jax.ShapeDtypeStruct
    low = lambda n: shape((rows, n), BF16)
    early_rows = (classes + 15) // 16 * 16 + 16
    sums = [shape((early_rows, width), BF16), shape((classes, width), F32)]
    return pl.pallas_call(
        middle_kernel,
        grid_spec=pl.GridSpec(
            grid=(2,),
            in_specs=[
                pl.BlockSpec(memory_space=pltpu.SMEM),
                tiled(width),
                turned(width // 2),
                pl.BlockSpec(memory_space=pl.ANY),
                turned(classes),
            ]
            + [
                pl.BlockSpec(memory_space=pl.ANY)
                if at in (4, 6, 8)
                else pl.BlockSpec(
                    a.shape, lambda i, n=a.ndim: (0,) * n, pipeline_mode=pl.Buffered(1)
                )
                for at, a in enumerate(params)
            ],
            out_specs=[
                turned(classes),
                turned(width),
                tiled(width),
                tiled(hidden),
                tiled(hidden),
                tiled(width),
                tiled(width),
                tiled(width),
                tiled(width),
                tiled(width),
                tiled(width),
            ]
            + [full(a) for a in sums],
            scratch_shapes=[
                pltpu.VMEM((tile, hidden), F32),
                pltpu.VMEM((classes, width), BF16),
                pltpu.VMEM((classes, width), F32),
                pltpu.VMEM((1, width), F32),
                pltpu.VMEM((1, hidden), F32),
                pltpu.VMEM((1, width), F32),
                pltpu.VMEM((1, width), F32),
                pltpu.VMEM((1, width), F32),
                pltpu.VMEM(params[4].shape, BF16),
                pltpu.VMEM(params[6].shape, BF16),
                pltpu.VMEM(params[8].shape, BF16),
                pltpu.VMEM((width // 2, rows), BF16),
                pltpu.SemaphoreType.DMA((3,)),
                pltpu.SemaphoreType.DMA,
                pltpu.SemaphoreType.DMA,
            ],
        ),
        out_shape=[
            shape((classes, rows), BF16),
            shape((width, rows), BF16),
            low(width),
            low(hidden),
            low(hidden),
            low(width),
            low(width),
            low(width),
            low(width),
            low(width),
            shape((rows, width), F32),
        ]
        + sums,
        compiler_params=pltpu.CompilerParams(
            vmem_limit_bytes=VMEM_LIMIT, collective_id=4, has_side_effects=True
        ),
        cost_estimate=pl.CostEstimate(
            flops=4 * rows * width * (2 * hidden + 2 * width),
            bytes_accessed=40 * MIB,
            transcendentals=2 * rows * hidden,
        ),
        name="middle",
    )(lengths, tokens, att_own, att_other, d_masks, *params)


def weights_kernel(
    normed_in,
    ghid_in,
    active_in,
    gfeed_in,
    joined_in,
    gbranch_in,
    gbranch_p_in,
    final_in,
    gpatch_in,
    w_out_in,
    att_own_in,
    att_other_in,
    early_in,
    gout_q_in,
    up_out,
    down_out,
    pair_out,
    early_out,
    gout_q_out,
    gout_t_out,
    delta_out,
    normed,
    ghid,
    active,
    gfeed,
    joined,
    gbranch,
    gbranch_p,
    final,
    gpatch,
    w_out,
    att_own,
    att_other,
    early,
    w_pad,
    up_part,
    down_part,
    pair_part,
    up_got,
    down_got,
    pair_got,
    branch_got,
    gout,
    gout_t,
    delta,
    early_got,
    pair_sum,
    pair_far,
    send,
    recv,
    load,
    store,
):
    seq = lax.axis_index("seq")
    grp = lax.axis_index("grp")
    core = lax.rem(seq, 2)
    x = seq // 2
    y = lax.rem(grp, 2)
    z = lax.rem(grp // 2, 2)
    rows, width = normed.shape
    half = width // 2
    heads = width // LANES
    third = width // 4
    tiles = active.shape[1] // width
    peer = {"seq": seq + 1 - 2 * core}

    peer_x = {"seq": seq + 2 - 4 * x}
    peer_y = {"grp": grp + 1 - 2 * y}
    peer_z = {"grp": grp + 2 - 4 * z}
    peers = (peer, peer_x, peer_y, peer_z)

    barrier = pltpu.get_barrier_semaphore()
    for other in peers:
        pl.semaphore_signal(barrier, inc=1, device_id=other, device_id_type=MESH)

    ins = (
        (joined_in, joined),
        (gbranch_p_in, gbranch_p),
        (final_in, final),
        (gpatch_in, gpatch),
        (gfeed_in, gfeed),
        (active_in, active),
        (normed_in, normed),
        (ghid_in, ghid),
        (w_out_in, w_out),
        (gbranch_in, gbranch),
        (att_own_in, att_own),
        (att_other_in, att_other),
        (early_in, early),
    )
    loads = [pltpu.make_async_copy(a, b, load.at[i]) for i, (a, b) in enumerate(ins)]
    for copy in loads:
        copy.start()
    pl.semaphore_wait(barrier, len(peers))

    def far(at, src, dst, to=peer):
        return pltpu.make_async_remote_copy(
            src_ref=src,
            dst_ref=dst,
            send_sem=send.at[at],
            recv_sem=recv.at[at],
            device_id=to,
            device_id_type=MESH,
        )

    def far_early(i):
        return far(4 + tiles + i, early, early_got.at[i], (peer, peer_y, peer_x)[i])

    def early_step(i):
        far_early(i).wait()
        early[...] = early[...] + early_got[i]

    def far_z():
        return far(7 + tiles, pair_sum.at[:, 1 - z], pair_far, peer_z)

    def far_branch():
        return far(0, gbranch_in, branch_got)

    def far_pair():
        return far(1, pair_part.at[1 - core], pair_got)

    def far_down(i):
        return far(2 + i, down_part.at[1 - core, i], down_got.at[i])

    def far_up(i):
        return far(2 + tiles + i, up_part.at[1 - core, i], up_got.at[i])

    def lanes(index, size):
        return pl.ds(pl.multiple_of(index * size, size), size)

    stores = []

    def gouts():
        loads[8].wait()
        loads[9].wait()
        w_pad[...] = jnp.zeros_like(w_pad)
        for head in range(heads):
            within, group = divmod(head, 2)
            at = 2 * group * third + within * HEAD_DIM
            w_pad[head * LANES : head * LANES + HEAD_DIM, :] = w_out[
                pl.ds(pl.multiple_of(at + core * third, HEAD_DIM), HEAD_DIM), :
            ]
        loads[10].wait()
        loads[11].wait()
        for at, (rows_in, att) in enumerate(((gbranch, att_own), (branch_got, att_other))):
            if at == 1:
                far_branch().wait()
            spot = slice(at * rows, (at + 1) * rows)
            gout[spot, :] = dot_nt(rows_in[...], w_pad[...]).astype(BF16)
            turned = gout[spot, :].T
            gout_t[:, spot] = turned
            for head in range(heads):
                low = turned[head * LANES : head * LANES + HEAD_DIM].astype(F32)
                own = att[head * HEAD_DIM : (head + 1) * HEAD_DIM, :].astype(F32)
                delta[head, :, spot] = jnp.sum(low * own, axis=0, keepdims=True)
        stores.extend([
            pltpu.make_async_copy(gout, gout_q_out.at[pl.ds(0, 2 * rows)], store.at[0]),
            pltpu.make_async_copy(gout_t, gout_t_out, store.at[4]),
            pltpu.make_async_copy(delta, delta_out, store.at[5]),
        ])
        for copy in stores:
            copy.start()

    far_branch().start()
    for i in range(4):
        loads[i].wait()
    first = dot_nn(joined[...], gbranch_p[...]).astype(BF16)
    second = dot_tn(final[...], gpatch[...]).astype(BF16)
    for i in range(2):
        pair_part[i, :, :half] = first[:, i * half : (i + 1) * half]
        pair_part[i, :, half:] = second[:, i * half : (i + 1) * half]
    far_pair().start()
    loads[12].wait()
    far_early(0).start()
    gouts()
    early_step(0)
    far_early(1).start()
    far_pair().wait()
    pair_sum[...] = (pair_part[core] + pair_got[...]).reshape(pair_sum.shape)
    far_z().start()
    loads[4].wait()
    loads[5].wait()

    def down_tile(i, carry):
        part = dot_tn(active[:, lanes(i, width)], gfeed[...]).astype(BF16)
        down_part[0, i] = part[:, :half]
        down_part[1, i] = part[:, half:]
        far_down(i).start()
        return carry

    lax.fori_loop(0, tiles, down_tile, 0)
    early_step(1)
    far_early(2).start()
    loads[6].wait()
    loads[7].wait()

    def up_of(which, i):
        block = 2 * (x + i - 2 * i * x) + which
        up_part[which, i] = dot_tn(normed[...], ghid[:, lanes(block, width)]).astype(BF16)

    for i in range(2):
        up_of(1 - core, i)
        far_up(i).start()
    for i in range(2):
        up_of(core, i)

    def keep(at, part, out):
        copy = pltpu.make_async_copy(part, out, store.at[at])
        copy.start()
        stores.append(copy)

    def keep_down(i, carry):
        far_down(i).wait()
        down_part[core, i] = down_part[core, i] + down_got[i]
        return carry

    lax.fori_loop(0, tiles, keep_down, 0)
    keep(2, down_part.at[core], down_out)
    for i in range(2):
        far_up(i).wait()
        up_part[core, i] = up_part[core, i] + up_got[i]
    keep(3, up_part.at[core], up_out)
    far_z().wait()
    for i in range(2):
        pair_sum[i, z] = pair_sum[i, z] + pair_far[i]
    keep(1, pair_sum.at[:, z], pair_out)
    early_step(2)
    keep(6, early, early_out)
    for copy in stores:
        copy.wait()


def weights(gout_q, *operands):
    rows, width = operands[0].shape
    hidden = operands[2].shape[1]
    tiles = hidden // width
    half = width // 2
    heads = width // LANES
    low = lambda *s: pltpu.VMEM(s, BF16)
    hbm = pl.BlockSpec(memory_space=pl.ANY)
    sets = [low(2, 2, width, width), low(2, tiles, width, half), low(2, width, width)]
    sets += [low(2, width, width), low(tiles, width, half), low(width, width)]
    shape = lambda *s: jax.ShapeDtypeStruct(s, BF16)
    early = operands[-1].shape
    each = width // 8
    outs = [
        shape(2, width, width),
        shape(tiles, width, half),
        shape(2, 2, each, width),
        shape(*early),
        shape(*gout_q.shape),
        shape(width, 2 * rows),
        jax.ShapeDtypeStruct((heads, 1, 2 * rows), F32),
    ]
    return pl.pallas_call(
        weights_kernel,
        in_specs=[hbm] * (len(operands) + 1),
        out_specs=[hbm] * len(outs),
        out_shape=outs,
        input_output_aliases={len(operands): 4},
        scratch_shapes=[low(*a.shape) for a in operands]
        + [low(width, width)]
        + sets
        + [
            low(rows, width),
            low(2 * rows, width),
            low(width, 2 * rows),
            pltpu.VMEM((heads, 1, 2 * rows), F32),
            low(3, *early),
            low(2, 2, 2, each, width),
            low(2, 2, each, width),
            pltpu.SemaphoreType.DMA((8 + tiles,)),
            pltpu.SemaphoreType.DMA((8 + tiles,)),
            pltpu.SemaphoreType.DMA((len(operands),)),
            pltpu.SemaphoreType.DMA((7,)),
        ],
        compiler_params=pltpu.CompilerParams(
            vmem_limit_bytes=VMEM_LIMIT, collective_id=1, has_side_effects=True
        ),
        cost_estimate=pl.CostEstimate(
            flops=4 * rows * width * (hidden + 2 * width),
            bytes_accessed=30 * MIB,
            transcendentals=0,
        ),
        name="weights",
    )(*operands, gout_q)


def weights_plain(
    gout_q,
    normed,
    ghid,
    active,
    gfeed,
    joined,
    gbranch,
    gbranch_p,
    final,
    gpatch,
    w_out,
    att_own,
    att_other,
    early,
):
    rows, width = normed.shape
    half = width // 2
    heads = width // LANES
    third = width // 4
    seq = lax.axis_index("seq")
    core = seq & 1

    def both_cores(matrix):
        mine = lax.dynamic_index_in_dim(matrix, core, 0, keepdims=False)
        other = lax.dynamic_index_in_dim(matrix, 1 - core, 0, keepdims=False)
        return (mine + swap(other, "seq", 1).astype(F32)).astype(BF16)

    up = dot_tn(normed, ghid).reshape(width, 2, 2, -1).transpose(2, 1, 0, 3)
    up = jnp.where(seq < 2, up, up[:, ::-1])
    down = dot_tn(active, gfeed).reshape(active.shape[1], 2, half).transpose(1, 0, 2)
    first = dot_nn(joined, gbranch_p).reshape(width, 2, half)
    second = dot_tn(final, gpatch).reshape(width, 2, half)
    pair = jnp.concatenate([first, second], axis=2).transpose(1, 0, 2)
    w_heads = w_out.reshape(2, 2, heads // 2, HEAD_DIM, width)
    w_heads = lax.dynamic_index_in_dim(w_heads, core, 1, keepdims=False)
    w_heads = w_heads.swapaxes(0, 1).reshape(heads, HEAD_DIM, width)
    w_pad = jnp.concatenate([w_heads, jnp.zeros_like(w_heads)], axis=1).reshape(width, width)
    branch = jnp.concatenate([gbranch, swap(gbranch, "seq", 1)])
    gout = dot_nt(branch, w_pad).astype(BF16)
    gout_t = gout.T
    att = jnp.concatenate([att_own, att_other], axis=1).reshape(heads, HEAD_DIM, 2 * rows)
    low = gout_t.reshape(heads, 2, HEAD_DIM, 2 * rows)[:, 0]
    delta = jnp.sum(low.astype(F32) * att.astype(F32), axis=1, keepdims=True)
    gout_q = jnp.concatenate([gout, gout_q[2 * rows :]])
    return (
        both_cores(up),
        both_cores(down),
        both_cores(pair),
        lax.psum(early.astype(F32), ("grp", "seq")),
        gout_q,
        gout_t,
        delta,
    )


EXCHANGES = tuple(
    chain + way
    for chain, ways in (
        ("U", "XYZW"),
        ("D", "YZWX"),
        ("C", "WYX"),
        ("V", "ZW"),
        ("G", "CXN"),
        ("L", "CXYZWD"),
        ("Q0", "YZWXCR"),
        ("Q1", "YZWXCR"),
        ("Q2", "YZWDyzwdXCR"),
    )
    for way in ways
)


def backward_kernel(
    q_t,
    gout_t,
    delta,
    gout_q,
    mass,
    k_ref,
    v_ref,
    up_in,
    down_in,
    pair_in,
    early_in,
    normed_in,
    tokens_in,
    gmid_in,
    gain_ref,
    wpair_ref,
    wqt_ref,
    up_out,
    down_out,
    pair_out,
    early_out,
    qkv_out,
    swap_out,
    late_out,
    gtok_out,
    gq_all,
    gq_low,
    gkv_all,
    far_dw,
    normed,
    tokens,
    gmid,
    gn_far,
    gn_send,
    gn_own,
    gkv_sum,
    au,
    ad,
    ac,
    wq,
    aq,
    bq,
    fin,
    piece,
    ru0,
    ru1,
    ru2,
    ru3,
    rd0,
    rd1,
    rd2,
    rd3,
    rc1,
    rc2,
    rc3,
    rv,
    rwy,
    rwz,
    rww,
    rqy,
    rqz,
    sqy,
    sqz,
    rqx,
    rqp,
    rg,
    rl,
    send,
    recv,
    local,
):
    step = pl.program_id(0)
    seq = lax.axis_index("seq")
    grp = lax.axis_index("grp")
    core = lax.rem(seq, 2)
    x = seq // 2
    y = lax.rem(grp, 2)
    z = lax.rem(grp // 2, 2)
    w = grp // 4
    peers = {
        "C": {"seq": seq + 1 - 2 * core},
        "X": {"seq": seq + 2 - 4 * x},
        "Y": {"grp": grp + 1 - 2 * y},
        "Z": {"grp": grp + 2 - 4 * z},
        "W": {"grp": grp + 4 - 8 * w},
        "D": {"grp": grp + 4 - 8 * w + 2 - 4 * z},
        "R": {"seq": seq + 2 - 4 * x + 1 - 2 * core},
    }
    tile = k_ref.shape[0]
    rows, heads = q_t.shape[1], gkv_all.shape[1] // LANES
    half = rows // 2
    width = wpair_ref.shape[1]
    tiles = half * 2 // tile
    per_phase = heads * tiles
    now = lax.rem(step, per_phase)
    head, block = now // tiles, lax.rem(now, tiles)

    def far(name, src, dst, way=None):
        at = EXCHANGES.index(name)
        return pltpu.make_async_remote_copy(
            src_ref=src,
            dst_ref=dst,
            send_sem=send.at[at],
            recv_sem=recv.at[at],
            device_id=peers[way or name[-1].upper()],
            device_id_type=MESH,
        )

    def near(at, src, dst):
        return pltpu.make_async_copy(src, dst, local.at[at])

    def add(dst, src, count):
        if count is None:
            dst[...] = dst[...] + src[...]
            return
        for i in range(count):
            dst[i] = dst[i] + src[i]

    def exchange(name):
        if name == "UX":
            return far(name, up_in.at[1], ru0)
        if name == "UY":
            return far(name, au.at[:, :, 1 - y], ru1)
        if name == "UZ":
            return far(name, au.at[:, 1 - z, y], ru2)
        if name == "UW":
            return far(name, au.at[1 - w, z, y], ru3)
        if name == "DY":
            return far(name, down_in.at[:, :, 1 - y], rd0)
        if name == "DZ":
            return far(name, ad.at[:, 1 - z], rd1)
        if name == "DW":
            return far(name, ad.at[1 - w, z], rd2)
        if name == "DX":
            return far(name, ad.at[w, z], rd3)
        if name == "CW":
            return far(name, pair_in.at[1 - w], rc1)
        if name == "CY":
            return far(name, ac.at[w, 1 - y], rc2)
        if name == "CX":
            return far(name, ac.at[w, y], rc3)
        if name[0] == "V":
            return far(name, early_out, rv.at["ZW".index(name[1])])
        if name == "GC":
            return far(name, gn_far.at[1], rg.at[0])
        if name == "GX":
            return far(name, gn_far.at[0], rg.at[1])
        if name == "GN":
            return far(name, gn_send, rg.at[2], "C")
        if name[0] == "L":
            return far(name, late_out, rl.at["CXYZWD".index(name[1])])
        b, way = int(name[1]), name[2]
        spots = {"Z": (w, 1 - z), "W": (1 - w, z), "D": (1 - w, 1 - z)}
        if way == "X":
            return far(name, fin.at[b], rqx.at[b])
        if way in "CR":
            return far(name, piece.at[b, "CR".index(way)], rqp.at[b, "CR".index(way)])
        if b < 2:
            if way == "Y":
                return far(name, wq.at[b, :, :, 1 - y], rwy.at[b])
            if way == "Z":
                return far(name, wq.at[b, :, 1 - z, y], rwz.at[b])
            return far(name, wq.at[b, 1 - w, z, y], rww.at[b])
        if way == "Y":
            return far(name, aq.at[:, :, 1 - y], rqy)
        if way in spots:
            return far(name, aq.at[*spots[way], y], rqz.at["ZWD".index(way)])
        if way == "y":
            return far(name, bq.at[w, z, 1 - y], sqy)
        return far(name, bq.at[*spots[way.upper()]], sqz.at["zwd".index(way)])

    def arrive(name):
        exchange(name).wait()
        if name == "UX":
            near(0, up_in.at[0], au).wait()
            for i in range(2):
                for j in range(2):
                    add(au.at[i, j], ru0.at[i, j], 2)
        elif name == "UY":
            for i in range(2):
                for j in range(2):
                    add(au.at[i, j, y], ru1.at[i, j], None)
        elif name == "UZ":
            for i in range(2):
                add(au.at[i, z, y], ru2.at[i], None)
        elif name == "UW":
            up_out[...] = au[w, z, y].astype(F32) + ru3[...].astype(F32)
        elif name == "DY":
            near(1, down_in.at[:, :, y], ad).wait()
            for i in range(2):
                add(ad.at[i], rd0.at[i], 2)
        elif name == "DZ":
            for i in range(2):
                add(ad.at[i, z], rd1.at[i], None)
        elif name == "DW":
            add(ad.at[w, z], rd2, None)
        elif name == "DX":
            down_out[...] = ad[w, z].astype(F32) + rd3[...].astype(F32)
        elif name == "CW":
            near(2, pair_in, ac).wait()
            add(ac.at[w], rc1, 2)
        elif name == "CY":
            add(ac.at[w, y], rc2, None)
        elif name == "CX":
            pair_out[...] = ac[w, y].astype(F32) + rc3[...].astype(F32)
        elif name[0] == "V":
            add(early_out, rv.at["ZW".index(name[1])], None)
        elif name == "GC":
            add(gn_far.at[0], rg.at[0], None)
        elif name[0] == "L":
            add(late_out, rl.at["CXYZWD".index(name[1])], None)
        elif name[0] != "Q":
            pass
        elif name[1] != "2":
            b = int(name[1])
            if name[2] == "Y":
                for i in range(2):
                    for j in range(2):
                        add(wq.at[b, i, j, y], rwy.at[b, i, j], None)
            elif name[2] == "Z":
                for i in range(2):
                    add(wq.at[b, i, z, y], rwz.at[b, i], None)
            elif name[2] == "W":
                add(wq.at[b, w, z, y], rww.at[b], None)
        elif name[2] == "Y":
            for i in range(2):
                for j in range(2):
                    add(aq.at[i, j, y], rqy.at[i, j], None)
        elif name[2] in "ZWD":
            add(aq.at[w, z, y], rqz.at["ZWD".index(name[2])], None)
        elif name[2] == "y":
            add(bq.at[w, z, y], sqy, None)
        elif name[2] in "zwd":
            add(bq.at[w, z], sqz.at["zwd".index(name[2])], 2)

    def start(*names):
        for name in names:
            exchange(name).start()

    def next_of(come, *then):
        for name in come.split():
            arrive(name)
        start(*then)

    def round_one():
        arrive("Q2Y")
        start("Q2Z", "Q2W", "Q2D")
        for way in "zwd":
            arrive("Q2" + way)
        start("Q2y")

    def pick(matrix, at, group):
        size = HEAD_DIM
        low = matrix[:, group * size : (group + 1) * size]
        high = matrix[:, (group + 3) * size : (group + 4) * size]
        return jnp.where(at == 0, low, high)

    def round_two(b):
        for way in "ZWDy" if b == 2 else "W":
            arrive("Q%d%s" % (b, way))
        if b == 2:
            whole = jnp.concatenate([aq[w, z, y], bq[w, z, y]], axis=1)
        else:
            whole = wq[b, w, z, y]
        fin[b] = whole
        for i, at in enumerate((x, 1 - x)):
            part = jnp.where(core == 0, pick(whole, at, 2), pick(whole, at, 0))
            piece[b, i] = jnp.concatenate([part, jnp.zeros_like(part)], axis=1)
        start("Q%dX" % b, "Q%dC" % b, "Q%dR" % b)

    def round_three(b):
        for way in "XCR":
            arrive("Q%d%s" % (b, way))
        qkv_out[b] = fin[b].astype(F32) + rqx[b].astype(F32)
        swap_out[b] = rqp[b, 0].astype(F32) + rqp[b, 1].astype(F32)

    def at_step(number, action):
        @pl.when(step == number)
        def _():
            action()

    def weights_of(b):
        lanes = slice(2 * b * LANES, 2 * (b + 1) * LANES)
        both = dot_tn(gkv_all[:, lanes], normed[...]) + far_dw[lanes, :]
        low_rows = gq_all[2 * b : 2 * b + 2].reshape(LANES, rows) * HEAD_DIM**-0.5
        low_rows = low_rows.astype(BF16)
        gq_low[b * LANES : (b + 1) * LANES, :] = low_rows
        query = dot_nn(low_rows, normed[...])
        size = HEAD_DIM
        stacked = jnp.concatenate(
            [
                query,
                both[size : 2 * size],
                both[3 * size :],
                both[:size],
                both[2 * size : 3 * size],
            ],
            axis=0,
        )
        turned = stacked.T.astype(BF16)
        if b < 2:
            wq[b] = turned.reshape(wq.shape[1:])
            start("Q%dY" % b)
        else:
            cut = aq.shape[-1]
            aq[...] = turned[:, :cut].reshape(aq.shape)
            bq[...] = turned[:, cut:].reshape(bq.shape)
            start("Q2Y", "Q2z", "Q2w", "Q2d")

    def first_step():
        barrier = pltpu.get_barrier_semaphore()
        for peer in peers.values():
            pl.semaphore_signal(barrier, inc=1, device_id=peer, device_id_type=MESH)
        pl.semaphore_wait(barrier, len(peers))
        near(0, up_in.at[0], au).start()
        near(1, down_in.at[:, :, y], ad).start()
        near(2, pair_in, ac).start()
        near(3, early_in, early_out).start()
        start("UX", "DY", "CW")
        near(4, normed_in.at[pl.ds(rows, rows)], normed).start()
        near(3, early_in, early_out).wait()

    def far_post():
        near(4, normed_in.at[pl.ds(rows, rows)], normed).wait()
        gkv_sum[...] = jnp.sum(gkv_all[...].astype(F32), axis=0, keepdims=True)
        for i in (1, 0):
            gn_far[i] = dot_nt(gkv_all[i * half : (i + 1) * half, :], wpair_ref[...]).astype(BF16)
            if i == 1:
                start("GC")
        far_dw[...] = dot_tn(gkv_all[...], normed[...])
        near(5, normed_in.at[pl.ds(0, rows)], normed).start()

    at_step(0, first_step)
    at_step(5, lambda: next_of("CW", "CY"))
    at_step(5, lambda: start("VZ"))
    at_step(7, lambda: next_of("VZ", "VW"))
    at_step(8, lambda: next_of("CY", "CX"))
    at_step(9, lambda: next_of("UX", "UY"))
    at_step(9, lambda: next_of("DY", "DZ"))
    at_step(11, lambda: arrive("CX"))
    at_step(12, far_post)
    at_step(13, lambda: next_of("GC", "GX"))
    at_step(13, lambda: arrive("VW"))
    at_step(14, lambda: next_of("UY", "UZ"))
    at_step(14, lambda: next_of("DZ", "DW"))
    at_step(16, lambda: near(5, normed_in.at[pl.ds(0, rows)], normed).wait())
    at_step(16, lambda: weights_of(0))
    at_step(17, lambda: next_of("UZ", "UW"))
    at_step(18, lambda: next_of("Q0Y", "Q0Z"))
    at_step(19, lambda: next_of("DW", "DX"))
    at_step(20, lambda: weights_of(1))
    at_step(20, lambda: arrive("UW"))
    at_step(20, lambda: next_of("Q0Z", "Q0W"))
    at_step(20, lambda: near(6, tokens_in, tokens).start())
    at_step(20, lambda: near(7, gmid_in, gmid).start())
    at_step(22, lambda: round_two(0))
    at_step(22, lambda: next_of("Q1Y", "Q1Z"))
    at_step(23, lambda: next_of("Q1Z", "Q1W"))

    gkv, part = score_grads(q_t, gout_t, delta, gout_q, mass, k_ref, v_ref)
    lanes = pl.ds(pl.multiple_of(head * LANES, LANES), LANES)
    gkv_all[pl.ds(pl.multiple_of(block * tile, tile), tile), lanes] = gkv

    @pl.when(step < per_phase)
    def _():
        @pl.when(block == 0)
        def _():
            gq_all[head] = part

        @pl.when(block != 0)
        def _():
            gq_all[head] += part

    @pl.when(step >= per_phase)
    def _():
        gq_all[head] += part

    @pl.when(step == 2 * per_phase - 1)
    def _():
        weights_of(2)

        def gn_of(at):
            spot = slice(at * half, (at + 1) * half)
            return dot_nt(gkv_all[spot, :], wpair_ref[...]) + dot_tn(gq_low[:, spot], wqt_ref[...])

        gn_send[...] = gn_of(1).astype(BF16)
        start("GN")
        gn_own[...] = gn_of(0)
        gkv_now = gkv_sum[...] + jnp.sum(gkv_all[...].astype(F32), axis=0, keepdims=True)
        ones = jnp.ones((8, rows), BF16)
        gq_now = dot_nt(ones, gq_low[...])[:1]
        gq_now = jnp.concatenate([gq_now, jnp.zeros_like(gq_now)], axis=1)
        arrive("GN")
        exchange("GX").wait()
        near(6, tokens_in, tokens).wait()
        rows_now = tokens[...].astype(F32)
        centred = rows_now - jnp.mean(rows_now, axis=-1, keepdims=True)
        inv = lax.rsqrt(jnp.mean(centred * centred, axis=-1, keepdims=True) + EPS_NORM)
        normal = centred * inv
        gn = gn_own[...] + rg[1].astype(F32) + rg[2].astype(F32)
        zero = jnp.zeros((1, width), F32)
        mine = core == 0
        late_out[...] = jnp.concatenate(
            [
                jnp.sum(gn * normal, axis=0, keepdims=True),
                jnp.sum(gn, axis=0, keepdims=True),
                zero,
                zero,
                jnp.where(mine, gq_now, zero),
                jnp.where(mine, zero, gq_now),
                jnp.where(mine, gkv_now, zero),
                jnp.where(mine, zero, gkv_now),
            ],
            axis=0,
        )
        start("LC")
        round_two(1)
        next_of("LC", "LX")
        round_one()
        near(7, gmid_in, gmid).wait()
        turned = gn * as_row(gain_ref)
        gtok_out[...] = (
            gmid[...]
            + inv
            * (
                turned
                - jnp.mean(turned, axis=-1, keepdims=True)
                - normal * jnp.mean(turned * normal, axis=-1, keepdims=True)
            )
        ).astype(BF16)
        next_of("LX", "LY")
        round_three(0)
        round_three(1)
        arrive("DX")
        round_two(2)
        next_of("LY", "LZ", "LW", "LD")
        round_three(2)
        for name in ("LZ", "LW", "LD"):
            exchange(name).wait()
        for at in range(3, 6):
            late_out[...] = late_out[...] + rl[at]


def backward(head_arrays, keys, values, sums, early, normed, tokens, gmid, gain, wpair, wqt):
    width, rows = head_arrays[0].shape
    heads = width // LANES
    half = rows // 2
    tile = half
    up, down, pair = sums
    each = up.shape[4]
    down_each, down_width = down.shape[3:]
    grid = 4 * heads
    head_of = lambda n: lax.rem(n, 2 * heads) // 2
    key_spec = pl.BlockSpec(
        (tile, LANES), lambda n: ((1 - n // (2 * heads)) * 2 + lax.rem(n, 2), head_of(n))
    )
    hbm = pl.BlockSpec(memory_space=pl.ANY)
    vmem = pl.BlockSpec(memory_space=pltpu.VMEM)
    low = lambda *s: pltpu.VMEM(s, BF16)
    full = lambda *s: pltpu.VMEM(s, F32)
    qkv_width = width // 2
    wide = qkv_width - LANES
    outs = [
        jax.ShapeDtypeStruct((each, width), F32),
        jax.ShapeDtypeStruct((down_each, down_width), F32),
        jax.ShapeDtypeStruct((each, width), F32),
        jax.ShapeDtypeStruct(early.shape, BF16),
        jax.ShapeDtypeStruct((3, each, qkv_width), F32),
        jax.ShapeDtypeStruct((3, each, LANES), F32),
        jax.ShapeDtypeStruct((8, width), F32),
        jax.ShapeDtypeStruct((half, width), BF16),
    ]
    return pl.pallas_call(
        backward_kernel,
        grid=(grid,),
        in_specs=head_specs(rows, head_of) + [key_spec, key_spec] + [hbm] * 7
        + [vmem] * 3,
        out_specs=[vmem] * len(outs),
        out_shape=outs,
        scratch_shapes=[
            full(heads, HEAD_DIM, rows),
            low(heads * HEAD_DIM, rows),
            low(rows, width),
            full(width, width),
            low(rows, width),
            low(half, width),
            full(half, width),
            low(2, half, width),
            low(half, width),
            full(half, width),
            full(1, width),
            low(2, 2, 2, each, width),
            low(2, 2, down_each, down_width),
            low(2, 2, each, width),
            low(2, 2, 2, 2, each, qkv_width),
            low(2, 2, 2, each, wide),
            low(2, 2, 2, each, LANES),
            low(3, each, qkv_width),
            low(3, 2, each, LANES),
            low(2, 2, 2, each, width),
            low(2, 2, each, width),
            low(2, each, width),
            low(each, width),
            low(2, 2, down_each, down_width),
            low(2, down_each, down_width),
            low(down_each, down_width),
            low(down_each, down_width),
            low(2, each, width),
            low(each, width),
            low(each, width),
            low(2, *early.shape),
            low(2, 2, 2, each, qkv_width),
            low(2, 2, each, qkv_width),
            low(2, each, qkv_width),
            low(2, 2, each, wide),
            low(3, each, wide),
            low(each, LANES),
            low(3, 2, each, LANES),
            low(3, each, qkv_width),
            low(3, 2, each, LANES),
            low(3, half, width),
            full(6, 8, width),
            pltpu.SemaphoreType.DMA((len(EXCHANGES),)),
            pltpu.SemaphoreType.DMA((len(EXCHANGES),)),
            pltpu.SemaphoreType.DMA((8,)),
        ],
        compiler_params=pltpu.CompilerParams(
            vmem_limit_bytes=VMEM_LIMIT, collective_id=0, has_side_effects=True
        ),
        cost_estimate=pl.CostEstimate(
            flops=40 * heads * rows * rows * LANES,
            bytes_accessed=40 * MIB,
            transcendentals=2 * heads * rows * rows,
        ),
        name="backward",
    )(*head_arrays, keys, values, up, down, pair, early, normed, tokens, gmid, gain, wpair, wqt)


def finish_kernel(
    up_ref,
    down_ref,
    pair_ref,
    early_ref,
    qkv_ref,
    swap_ref,
    late_ref,
    gtok_ref,
    classes_ref,
    class_ref,
    class_w_ref,
    up_out,
    down_out,
    wout_out,
    patch_out,
    qkv_out,
    class_w_out,
    class_out,
    gtok_out,
    gbias_up_out,
    *rest,
):
    vector_outs, product = rest[:-1], rest[-1]
    seq, grp = lax.axis_index("seq"), lax.axis_index("grp")
    core, x = lax.rem(seq, 2), seq // 2
    gtok_out[...] = gtok_ref[...]
    width = up_ref.shape[1]
    third = width // 4
    each = up_ref.shape[0]
    size = HEAD_DIM
    up_out[...] = up_ref[...]
    down_out[...] = jnp.where(x == 0, down_ref[:, :third], down_ref[:, third:]).T
    wout_out[...] = jnp.where(x == 0, pair_ref[:, :third], pair_ref[:, third : 2 * third])
    patch_out[...] = jnp.where(x == 0, pair_ref[:, 2 * third : 3 * third], pair_ref[:, 3 * third :])

    def group(j):
        parts = []
        for b in range(3):
            low = qkv_ref[b, :, j * size : (j + 1) * size]
            high = qkv_ref[b, :, (j + 3) * size : (j + 4) * size]
            parts.append(jnp.where(x == 0, low, high))
        return jnp.concatenate(parts, axis=1)

    first, second, last = group(0), group(1), group(2)
    got = jnp.concatenate([swap_ref[b, :, :size] for b in range(3)], axis=1)
    qkv_out[...] = jnp.concatenate(
        [jnp.where(core == 0, first, second), got, jnp.where(core == 0, second, last)], axis=1
    )

    classes = classes_ref[...]
    count = classes.shape[0]
    scale = lax.rsqrt(jnp.sum(classes * classes, axis=-1, keepdims=True) + EPS_UNIT)
    unit = classes * scale
    gunit = early_ref[:count, :].astype(F32)
    gclass = (scale * (gunit - unit * jnp.sum(gunit * unit, axis=-1, keepdims=True))).astype(BF16)
    product[...] = dot_tn(class_ref[...], gclass)
    block = product[pl.ds(grp * each, each), :]
    mine = block[:, :third]
    for s in range(1, 4):
        mine = jnp.where(seq == s, block[:, s * third : (s + 1) * third], mine)
    class_w_out[...] = mine

    def own_lanes(matrix, each):
        total = matrix.shape[1]
        return pltpu.roll(matrix, lax.rem(total - grp * each, total), 1)[:, :each]

    class_out[...] = own_lanes(dot_nt(gclass, class_w_ref[...]), each)
    at = early_ref.shape[0] - 16
    vectors = early_ref[at:, :].astype(F32)
    late = late_ref[...]

    def all_heads(first, second):
        parts = []
        for g in range(2):
            for vector in (first, second):
                parts += [vector[i * 2 + g] for i in range(3)]
        return jnp.concatenate(parts, axis=1)

    def lanes_of(matrix, row, stride, count):
        return [matrix[row : row + 1, i * stride : i * stride + size] for i in range(count)]

    gquery = all_heads(lanes_of(late, 4, size, 6), lanes_of(late, 5, size, 6))
    gvalue = all_heads(lanes_of(late, 6, 2 * size, 6), lanes_of(late, 7, 2 * size, 6))
    packed = jnp.concatenate(
        [vectors[:4], late[:2], gquery, gvalue], axis=0
    )
    mine = own_lanes(packed, each)
    for i, ref in enumerate(vector_outs):
        ref[...] = mine[i]
    chunks = gbias_up_out.shape[0] // each
    flat = jnp.concatenate([vectors[4 + i : 5 + i] for i in range(chunks)], axis=1)
    flat = jnp.concatenate([flat] * 8, axis=0)
    gbias_up_out[...] = own_lanes(flat, chunks * each)[0]


def finish(*operands):
    up, down, pair, early, qkv, _, late, gtok, classes, class_emb, class_w = operands
    each, width = up.shape
    third = width // 4
    hidden_each = down.shape[0]
    shapes = [
        (each, width),
        (third, hidden_each),
        (each, third),
        (each, third),
        (each, 3 * third),
        (each, third),
        (classes.shape[0], each),
        gtok.shape,
        (hidden_each,),
    ] + [(each,)] * 8
    vmem = pl.BlockSpec(memory_space=pltpu.VMEM)
    return pl.pallas_call(
        finish_kernel,
        in_specs=[vmem] * len(operands),
        out_specs=[vmem] * len(shapes),
        out_shape=[jax.ShapeDtypeStruct(s, BF16 if s == gtok.shape else F32) for s in shapes],
        scratch_shapes=[pltpu.VMEM((width, width), F32)],
        compiler_params=pltpu.CompilerParams(vmem_limit_bytes=VMEM_LIMIT),
        name="finish",
    )(*operands)


def layer_norm(matrix_rows, gain_vec, shift_vec):
    row_mean = jnp.mean(matrix_rows, axis=-1, keepdims=True)
    centred = matrix_rows - row_mean
    row_var = jnp.mean(centred * centred, axis=-1, keepdims=True)
    return centred * lax.rsqrt(row_var + EPS_NORM) * gain_vec + shift_vec


def unit_rows(matrix_rows):
    return matrix_rows * lax.rsqrt(
        jnp.sum(matrix_rows * matrix_rows, axis=-1, keepdims=True) + EPS_UNIT
    )


def column_sum(matrix_low):
    return jnp.sum(matrix_low.astype(F32), axis=0)


def swap(value, axis, bit):
    size = lax.axis_size(axis)
    return lax.ppermute(value, axis, [(i, i ^ bit) for i in range(size)])


def add_low(first, second):
    return (first.astype(F32) + second.astype(F32)).astype(BF16)


def sum_rows(part):
    groups = lax.axis_size("grp")
    bits = groups.bit_length() - 1
    here = lax.axis_index("grp")
    each = part.shape[0] // groups
    width = part.shape[1]
    part = part.reshape((2,) * bits + (each, width))
    for name in range(bits):
        axis = bits - 1 - name
        mine = (here >> name) & 1
        send = lax.dynamic_index_in_dim(part, 1 - mine, axis, keepdims=True)
        keep = lax.dynamic_index_in_dim(part, mine, axis, keepdims=True)
        part = add_low(keep, swap(send, "grp", 1 << name))
    return part.reshape(each, width)


def sum_x(part, x_here):
    half = part.shape[1] // 2
    low, high = part[:, :half], part[:, half:]
    mine = jnp.where(x_here == 0, low, high)
    other = jnp.where(x_here == 0, high, low)
    return mine.astype(F32) + swap(other, "seq", 2).astype(F32)


def body(
    tokens_in,
    lengths,
    ln1_gain,
    ln1_bias,
    w_qkv,
    bias_query,
    bias_value,
    w_out,
    bias_out,
    ln2_gain,
    ln2_bias,
    w_up,
    bias_up,
    w_down,
    bias_down,
    proj_patch,
    proj_class,
    class_emb,
    d_masks,
):
    row_count, model_width = tokens_in.shape
    head_count = model_width // HEAD_DIM
    heads_here = head_count // 2
    third = model_width // 4
    seq_devices = lax.axis_size("seq")
    grp_devices = lax.axis_size("grp")
    seq_here = lax.axis_index("seq")
    grp_here = lax.axis_index("grp")
    core = seq_here & 1
    x_here = seq_here >> 1

    tokens_x = swap(tokens_in, "seq", 2)
    normed_image, w_kv, value_bias, w_pairs, w_query_t, queries_t, gout_q, keys, values = project_near(
        lengths, tokens_in, ln1_gain, ln1_bias, w_qkv, bias_query, bias_value
    )
    partial, near_top = attend_forward(attend_near_kernel, "attend_near", queries_t, keys, values)
    tokens_x, partial = lax.optimization_barrier((tokens_x, partial))
    normed_image, keys, values = project_far(
        lengths,
        tokens_x,
        ln1_gain,
        ln1_bias,
        w_kv,
        value_bias,
        (normed_image, keys, values),
    )
    att_own, att_other, mass = attend_forward(
        attend_far_kernel, "attend_far", queries_t, keys, values, partial, near_top
    )
    (
        mask_out,
        joined,
        normed_two,
        active,
        grad_hidden,
        final_low,
        grad_patches,
        grad_feed,
        grad_branch,
        grad_branch_p,
        grad_middle,
        early,
        classes,
    ) = middle(
        lengths,
        tokens_in,
        att_own,
        att_other,
        d_masks.T,
        (
            w_out,
            bias_out,
            ln2_gain,
            ln2_bias,
            w_up,
            bias_up,
            w_down,
            bias_down,
            proj_patch,
            proj_class,
            class_emb,
        ),
    )
    fused = grp_devices == 8 and model_width % (16 * grp_devices) == 0
    up_sum, down_sum, pair_sum, early, gout_q, gouts_t, delta = (weights if fused else weights_plain)(
        gout_q,
        normed_two,
        grad_hidden,
        active,
        grad_feed,
        joined,
        grad_branch,
        grad_branch_p,
        final_low,
        grad_patches,
        w_out,
        att_own,
        att_other,
        early,
    )
    head_arrays = (queries_t, gouts_t, delta, gout_q, mass)
    down_sum = down_sum.reshape(bias_up.shape[0], model_width // 2)
    rows_each = model_width // grp_devices
    ff_each = bias_up.shape[0] // grp_devices
    cols_each = model_width // seq_devices

    if fused:
        sums = (
            up_sum.reshape(2, 2, 2, 2, rows_each, -1),
            down_sum.reshape(2, 2, 2, ff_each, -1),
            pair_sum,
        )
        raw = backward(
            head_arrays,
            keys,
            values,
            sums,
            early,
            normed_image,
            tokens_in,
            grad_middle,
            ln1_gain,
            w_pairs,
            w_query_t,
        )
        (
            out_w_up,
            out_w_down,
            out_w_out,
            out_proj_patch,
            out_w_qkv,
            grad_proj_class,
            grad_class_emb,
            grad_tokens,
            out_bias_up,
            *vectors,
        ) = finish(*raw, classes, class_emb, proj_class)
        return (
            mask_out.T,
            grad_tokens,
            vectors[4],
            vectors[5],
            out_w_qkv,
            vectors[6],
            vectors[7],
            out_w_out,
            vectors[1],
            vectors[2],
            vectors[3],
            out_w_up,
            out_bias_up,
            out_w_down.T,
            vectors[0],
            out_proj_patch,
            grad_proj_class,
            grad_class_emb,
        )

    out_w_down = sum_x(sum_rows(down_sum), x_here)
    out_w_up = sum_rows(add_low(up_sum[0], swap(up_sum[1], "seq", 2))).astype(F32)
    pair_rows = sum_rows(pair_sum)
    out_w_out = sum_x(pair_rows[:, : 2 * third], x_here)
    out_proj_patch = sum_x(pair_rows[:, 2 * third :], x_here)
    class_total = early[: class_emb.shape[0]]
    vectors = early[-16:]
    gq_t, gkv = attend_backward(*head_arrays, keys, values)

    gq = gq_t.T
    gn_far = dot_nt(gkv[2 * row_count :], w_pairs)
    gn_near = dot_nt(gkv[: 2 * row_count], w_pairs) + dot_nn(gq, w_query_t)
    far_got = swap(gn_far[row_count:].astype(BF16), "seq", 1)
    far_sum = (gn_far[:row_count] + far_got.astype(F32)).astype(BF16)
    near_got = swap(gn_near[row_count:].astype(BF16), "seq", 1)
    x_got = swap(far_sum, "seq", 2)
    grad_normed_one = gn_near[:row_count] + near_got.astype(F32) + x_got.astype(F32)
    norm_one_back = jax.vjp(layer_norm, tokens_in.astype(F32), ln1_gain, ln1_bias)[1]
    grad_tokens_norm, grad_ln1_gain, grad_ln1_bias = norm_one_back(grad_normed_one)
    grad_tokens = (grad_middle + grad_tokens_norm).astype(BF16)

    dw_q = dot_tn(normed_image[: 2 * row_count], gq).reshape(model_width, 3, 2, HEAD_DIM)
    dw_kv = dot_tn(normed_image, gkv).reshape(model_width, 3, 2, 2, HEAD_DIM)
    three = lambda matrix: matrix.reshape(model_width, third)
    part_zero = [three(dw_q[:, :, 0]), three(dw_q[:, :, 1]), three(dw_kv[:, :, 0, 1])]
    part_one = [three(dw_kv[:, :, 1, 1]), three(dw_kv[:, :, 0, 0]), three(dw_kv[:, :, 1, 0])]
    part_zero = jnp.concatenate(part_zero, axis=1).astype(BF16)
    part_one = jnp.concatenate(part_one, axis=1).astype(BF16)
    qkv_mine = jnp.where(x_here == 0, part_zero, part_one)
    qkv_other = jnp.where(x_here == 0, part_one, part_zero)
    qkv_rows = sum_rows(add_low(qkv_mine, swap(qkv_other, "seq", 2))).astype(F32)
    pieces = [qkv_rows[:, i * third : (i + 1) * third] for i in range(3)]
    piece_got = swap(jnp.where(core == 0, pieces[2], pieces[0]), "seq", 1)
    out_w_qkv = jnp.concatenate(
        [
            jnp.where(core == 0, pieces[0], pieces[1]),
            piece_got,
            jnp.where(core == 0, pieces[1], pieces[2]),
        ],
        axis=1,
    )

    def put_back(vector):
        halves = vector.reshape(3, 2, HEAD_DIM).swapaxes(0, 1).reshape(2, 1, third)
        zero = jnp.zeros_like(halves)
        both = jnp.where(
            core == 0,
            jnp.concatenate([halves, zero], axis=1),
            jnp.concatenate([zero, halves], axis=1),
        )
        return both.reshape(model_width)

    grad_bias_query = put_back(column_sum(gq))
    gkv_sums = column_sum(gkv).reshape(heads_here, 2, HEAD_DIM)
    grad_bias_value = put_back(gkv_sums[:, 0].reshape(heads_here * HEAD_DIM))
    late = jnp.stack([grad_ln1_gain, grad_ln1_bias, grad_bias_query, grad_bias_value], axis=1)
    late = jnp.concatenate([late, jnp.zeros((model_width, LANES - 4), F32)], axis=1).astype(BF16)
    late = add_low(late, swap(late, "seq", 1))
    late = sum_rows(add_low(late, swap(late, "seq", 2))).astype(F32)

    class_back = jax.vjp(unit_rows, classes)[1]
    grad_classes = class_back(class_total)[0].astype(BF16)

    def vector_rows(index):
        return lax.dynamic_slice_in_dim(vectors[index], grp_here * rows_each, rows_each, 0)

    out_bias_up = lax.dynamic_slice_in_dim(
        vectors[4 : 4 + bias_up.shape[0] // model_width].reshape(-1), grp_here * ff_each, ff_each, 0
    )
    emb_cols = lax.dynamic_slice_in_dim(class_emb, grp_here * rows_each, rows_each, 1)
    class_cols = lax.dynamic_slice_in_dim(grad_classes, seq_here * cols_each, cols_each, 1)
    grad_proj_class = dot_tn(emb_cols, class_cols)
    proj_rows = lax.dynamic_slice_in_dim(proj_class, grp_here * rows_each, rows_each, 0)
    grad_class_emb = dot_nt(grad_classes, proj_rows)
    return (
        mask_out.T,
        grad_tokens,
        late[:, 0],
        late[:, 1],
        out_w_qkv,
        late[:, 2],
        late[:, 3],
        out_w_out,
        vector_rows(1),
        vector_rows(2),
        vector_rows(3),
        out_w_up,
        out_bias_up,
        out_w_down,
        vector_rows(0),
        out_proj_patch,
        grad_proj_class,
        grad_class_emb,
    )


def solution(mesh):
    rows = P(("grp", "seq"), None)
    both = P("grp", "seq")
    return jax.shard_map(
        body,
        mesh=mesh,
        in_specs=(rows, P("grp")) + (P(),) * 16 + (rows,),
        out_specs=(
            rows,
            rows,
            P("grp"),
            P("grp"),
            both,
            P("grp"),
            P("grp"),
            both,
            P("grp"),
            P("grp"),
            P("grp"),
            both,
            P("grp"),
            both,
            P("grp"),
            both,
            both,
            P(None, "grp"),
        ),
        check_vma=False,
    )
```

```python
import functools
import math

import jax
import jax.numpy as jnp
from jax import lax
from jax.experimental import pallas as pl
from jax.experimental.pallas import tpu as pltpu
from jax.sharding import PartitionSpec as P

HEAD_DIM = 64
LANES = 128
EPS_NORM = 1e-06
EPS_UNIT = 1e-06
NEG_FILL = -1e30
LOG2E = math.log2(math.e)
F32 = jnp.float32
BF16 = jnp.bfloat16
MIB = 1 << 20
VMEM_LIMIT = 63 * MIB
MESH = pl.DeviceIdType.MESH


def dot_nn(a, b):
    return lax.dot_general(a, b, (((1,), (0,)), ((), ())), preferred_element_type=F32)


def dot_nt(a, b):
    return lax.dot_general(a, b, (((1,), (1,)), ((), ())), preferred_element_type=F32)


def dot_tn(a, b):
    return lax.dot_general(a, b, (((0,), (0,)), ((), ())), preferred_element_type=F32)


def swap_tokens(seq, src, dst, send, recv):
    return pltpu.make_async_remote_copy(
        src_ref=src,
        dst_ref=dst,
        send_sem=send,
        recv_sem=recv,
        device_id={"seq": seq + 1 - 2 * lax.rem(seq, 2)},
        device_id_type=MESH,
    )


def greet_core(seq):
    peer = {"seq": seq + 1 - 2 * lax.rem(seq, 2)}
    pl.semaphore_signal(
        pltpu.get_barrier_semaphore(), inc=1, device_id=peer, device_id_type=MESH
    )


def await_core():
    pl.semaphore_wait(pltpu.get_barrier_semaphore(), 1)


def normed_tile(step, per, own_ref, got, out_ref, gain_ref, shift_ref):
    tile = out_ref.shape[0]
    row = lax.rem(step, per) * tile

    @pl.when(step < per)
    def _():
        out_ref[...] = own_ref[pl.ds(pl.multiple_of(row, tile), tile), :]

    @pl.when(step >= per)
    def _():
        out_ref[...] = got[pl.ds(pl.multiple_of(row, tile), tile), :]

    rows = out_ref[...].astype(F32)
    centred = rows - jnp.mean(rows, axis=-1, keepdims=True)
    var = jnp.mean(centred * centred, axis=-1, keepdims=True)
    normed = centred * lax.rsqrt(var + EPS_NORM) * as_row(gain_ref) + as_row(shift_ref)
    normed = normed.astype(BF16)
    out_ref[...] = normed
    return normed, row


def spread(matrix, upper):
    zero = jnp.zeros((matrix.shape[0], HEAD_DIM), matrix.dtype)
    parts = []
    for at in range(0, matrix.shape[1], HEAD_DIM):
        piece = matrix[:, at : at + HEAD_DIM]
        parts += [zero, piece] if upper else [piece, zero]
    return jnp.concatenate(parts, axis=1)


def column_is(column, width):
    at = lax.broadcasted_iota(jnp.int32, (1, width), 1)
    return jnp.where(lax.rem(at, LANES) == column, 1.0, 0.0)


def key_mask(length, first_row, shape):
    where_row = lax.broadcasted_iota(jnp.int32, (shape[0], 1), 0) + first_row
    masked = jnp.where(where_row < length, 0.0, NEG_FILL)
    return masked * column_is(0, shape[1])


def keys_values(normed, mask, wkv_ref, vbias_ref, k_ref, v_ref):
    width = k_ref.shape[1]
    both = dot_nn(normed, wkv_ref[...])
    k_ref[...] = (spread(both[:, : width // 2], True) + mask).astype(BF16)
    value = spread(both[:, width // 2 :] + vbias_ref[...], False)
    v_ref[...] = (value + column_is(HEAD_DIM, width)).astype(BF16)


def project_near_kernel(
    lengths_ref,
    own_ref,
    gain_ref,
    shift_ref,
    w_ref,
    bias_query_ref,
    bias_value_ref,
    normed_ref,
    wkv_ref,
    vbias_ref,
    wpair_ref,
    wqt_ref,
    q_t_ref,
    gout_q_ref,
    k_ref,
    v_ref,
    wq,
    qbias,
    got,
    send,
    recv,
):
    step = pl.program_id(0)
    seq = lax.axis_index("seq")
    core = lax.rem(seq, 2)
    width = normed_ref.shape[1]
    tile = normed_ref.shape[0]
    rows = own_ref.shape[0]
    per = rows // tile

    @pl.when(step == 0)
    def _():
        greet_core(seq)
        bias_query, bias_value = as_row(bias_query_ref), as_row(bias_value_ref)
        for which in range(2):

            @pl.when(core == which)
            def _():
                rows_q, rows_v, queries, keys, values, pairs = [], [], [], [], [], []
                for head in range(width // LANES):
                    within, group = divmod(head, 2)
                    at = (2 * group + which) * (width // 4) + within * HEAD_DIM
                    spot = slice(at, at + HEAD_DIM)
                    queries.append(w_ref[:, spot])
                    keys.append(w_ref[:, width + at : width + at + HEAD_DIM])
                    values.append(w_ref[:, 2 * width + at : 2 * width + at + HEAD_DIM])
                    pairs += [values[-1], keys[-1]]
                    rows_q.append(bias_query[:, spot])
                    rows_v.append(bias_value[:, spot])
                together = jnp.concatenate(queries, axis=1)
                wq[...] = together
                wqt_ref[...] = together.T
                wkv_ref[...] = jnp.concatenate(keys + values, axis=1)
                wpair_ref[...] = jnp.concatenate(pairs, axis=1)
                qbias[...] = jnp.concatenate(rows_q, axis=1)
                vbias_ref[...] = jnp.concatenate(rows_v, axis=1)

        await_core()
        swap_tokens(seq, own_ref, got, send, recv).start()

    @pl.when(step == per)
    def _():
        swap_tokens(seq, own_ref, got, send, recv).wait()

    normed, row = normed_tile(step, per, own_ref, got, normed_ref, gain_ref, shift_ref)
    block = step // per
    place = seq + block * (1 - 2 * core)
    mixed = (dot_nn(normed, wq[...]) + qbias[...]).astype(BF16).astype(F32)
    query = spread(mixed * HEAD_DIM**-0.5, True)
    gout_q_ref[...] = query.astype(BF16)
    q_t_ref[...] = (query + column_is(0, width)).astype(BF16).T
    mask = key_mask(lengths_ref[0], place * rows + row, k_ref.shape)
    keys_values(normed, mask, wkv_ref, vbias_ref, k_ref, v_ref)


def project_far_kernel(
    lengths_ref,
    own_ref,
    gain_ref,
    shift_ref,
    wkv_ref,
    vbias_ref,
    normed_in,
    k_in,
    v_in,
    normed_ref,
    k_ref,
    v_ref,
    got,
    send,
    recv,
):
    step = pl.program_id(0)
    seq = lax.axis_index("seq")
    core = lax.rem(seq, 2)
    width = normed_ref.shape[1]
    tile = normed_ref.shape[0]
    rows = own_ref.shape[0]
    per = rows // tile

    @pl.when(step == 0)
    def _():
        greet_core(seq)
        await_core()
        swap_tokens(seq, own_ref, got, send, recv).start()

    @pl.when(step == per)
    def _():
        swap_tokens(seq, own_ref, got, send, recv).wait()

    normed, row = normed_tile(step, per, own_ref, got, normed_ref, gain_ref, shift_ref)
    block = step // per
    place = seq + 2 - 4 * (seq // 2) + block * (1 - 2 * core)
    mask = key_mask(lengths_ref[0], place * rows + row, k_ref.shape)
    keys_values(normed, mask, wkv_ref, vbias_ref, k_ref, v_ref)


def as_row(ref):
    return ref[...].reshape(1, -1)


def whole(a):
    return pl.BlockSpec(a.shape, lambda *_: (0,) * len(a.shape))


def project_near(lengths, tokens, gain, shift, w_qkv, bias_query, bias_value):
    rows, width = tokens.shape
    tile = rows // 2
    shape = lambda *s: jax.ShapeDtypeStruct(s, BF16)
    tiled = pl.BlockSpec((tile, width), lambda i: (i, 0))
    image = shape(4 * rows, width)
    outs = [
        image,
        shape(width, width),
        jax.ShapeDtypeStruct((1, width // 2), F32),
        shape(width, width),
        shape(width // 2, width),
        shape(width, 2 * rows),
        image,
        image,
        image,
    ]
    return pl.pallas_call(
        project_near_kernel,
        grid=(4,),
        in_specs=[pl.BlockSpec(memory_space=pltpu.SMEM)]
        + [whole(a) for a in (tokens, gain, shift, w_qkv, bias_query, bias_value)],
        out_specs=[
            tiled,
            whole(outs[1]),
            whole(outs[2]),
            whole(outs[3]),
            whole(outs[4]),
            pl.BlockSpec((width, tile), lambda i: (0, i)),
            pl.BlockSpec((tile, width), lambda i: (i + 4, 0)),
            tiled,
            tiled,
        ],
        out_shape=outs,
        scratch_shapes=[
            pltpu.VMEM((width, width // 2), BF16),
            pltpu.VMEM((1, width // 2), F32),
            pltpu.VMEM((rows, width), BF16),
            pltpu.SemaphoreType.DMA,
            pltpu.SemaphoreType.DMA,
        ],
        compiler_params=pltpu.CompilerParams(
            vmem_limit_bytes=VMEM_LIMIT, collective_id=2, has_side_effects=True
        ),
        cost_estimate=pl.CostEstimate(
            flops=12 * rows * width * width, bytes_accessed=20 * MIB, transcendentals=0
        ),
        name="project_near",
    )(lengths, tokens, gain, shift, w_qkv, bias_query, bias_value)


def project_far(lengths, tokens, gain, shift, wkv, vbias, images):
    rows, width = tokens.shape
    tile = rows // 2
    tiled = pl.BlockSpec((tile, width), lambda i: (i + 4, 0))
    return pl.pallas_call(
        project_far_kernel,
        grid=(4,),
        in_specs=[pl.BlockSpec(memory_space=pltpu.SMEM)]
        + [whole(a) for a in (tokens, gain, shift, wkv, vbias)]
        + [pl.BlockSpec(memory_space=pl.ANY)] * 3,
        out_specs=[tiled] * 3,
        out_shape=[jax.ShapeDtypeStruct(a.shape, a.dtype) for a in images],
        input_output_aliases={6: 0, 7: 1, 8: 2},
        scratch_shapes=[
            pltpu.VMEM((rows, width), BF16),
            pltpu.SemaphoreType.DMA,
            pltpu.SemaphoreType.DMA,
        ],
        compiler_params=pltpu.CompilerParams(
            vmem_limit_bytes=VMEM_LIMIT, collective_id=3, has_side_effects=True
        ),
        cost_estimate=pl.CostEstimate(
            flops=8 * rows * width * width, bytes_accessed=16 * MIB, transcendentals=0
        ),
        name="project_far",
    )(lengths, tokens, gain, shift, wkv, vbias, *images)


PART = 72


def attend_near_kernel(q_t_ref, k_ref, v_ref, part_ref, top_ref):
    scores = dot_nn(k_ref[...], q_t_ref[...])
    top = jnp.max(scores, axis=0, keepdims=True)
    prob = jnp.exp2((scores - top) * LOG2E).astype(BF16)
    part_ref[...] = dot_tn(v_ref[...], prob)[:PART]
    top_ref[0] = top


def attend_far_kernel(q_t_ref, k_ref, v_ref, part_ref, near_top_ref, own_ref, other_ref, mass_ref):
    scores = dot_nn(k_ref[...], q_t_ref[...])
    near_top = near_top_ref[0]
    top = jnp.maximum(jnp.max(scores, axis=0, keepdims=True), near_top)
    prob = jnp.exp2((scores - top) * LOG2E).astype(BF16)
    summed = dot_tn(v_ref[...], prob)[:PART]
    summed = summed + part_ref[...] * jnp.exp2((near_top - top) * LOG2E)
    total = summed[HEAD_DIM : HEAD_DIM + 1]
    mass_ref[0] = top * LOG2E + jnp.log2(total)
    out = (summed[:HEAD_DIM] / total).astype(BF16)
    half = own_ref.shape[1]
    own_ref[...] = out[:, :half]
    other_ref[...] = out[:, half:]


def attend_cost(heads, rows, span):
    return pl.CostEstimate(
        flops=8 * heads * rows * span * LANES,
        bytes_accessed=(rows + 2 * span) * heads * LANES * 2,
        transcendentals=heads * rows * span,
    )


def attend_forward(kernel, name, queries_t, keys, values, *partial):
    width, rows = queries_t.shape
    span = keys.shape[0] // 2
    heads = width // LANES
    at = 1 if partial else 0
    part_spec = pl.BlockSpec((PART, rows), lambda h: (h, 0))
    row_spec = pl.BlockSpec((1, 1, rows), lambda h: (h, 0, 0))
    row_shape = jax.ShapeDtypeStruct((heads, 1, rows), F32)
    if partial:
        out_specs = [pl.BlockSpec((HEAD_DIM, rows // 2), lambda h: (h, 0))] * 2 + [row_spec]
        outs = [jax.ShapeDtypeStruct((heads * HEAD_DIM, rows // 2), BF16)] * 2 + [row_shape]
    else:
        out_specs = [part_spec, row_spec]
        outs = [jax.ShapeDtypeStruct((heads * PART, rows), F32), row_shape]
    return pl.pallas_call(
        kernel,
        grid=(heads,),
        in_specs=[
            pl.BlockSpec((LANES, rows), lambda h: (h, 0)),
            pl.BlockSpec((span, LANES), lambda h: (at, h)),
            pl.BlockSpec((span, LANES), lambda h: (at, h)),
        ]
        + [part_spec, row_spec][: len(partial)],
        out_specs=out_specs,
        out_shape=outs,
        compiler_params=pltpu.CompilerParams(vmem_limit_bytes=VMEM_LIMIT),
        cost_estimate=attend_cost(heads, rows, span),
        name=name,
    )(queries_t, keys, values, *partial)


def score_grads(q_t_ref, gout_t_ref, delta_ref, gout_q_ref, mass_ref, k_ref, v_ref):
    key_now = k_ref[...]
    scores = dot_nn(key_now, q_t_ref[...])
    prob = jnp.exp2(scores * LOG2E - mass_ref[0])
    gprob = dot_nn(v_ref[...], gout_t_ref[...])
    gscore = (prob * (gprob - delta_ref[0])).astype(BF16)
    gkv = dot_nn(jnp.concatenate([prob.astype(BF16), gscore], axis=1), gout_q_ref[...])
    return gkv.astype(BF16), dot_tn(key_now, gscore)[HEAD_DIM:]


def head_specs(rows, head_of):
    return [
        pl.BlockSpec((LANES, rows), lambda *n: (head_of(*n), 0)),
        pl.BlockSpec((LANES, rows), lambda *n: (head_of(*n), 0)),
        pl.BlockSpec((1, 1, rows), lambda *n: (head_of(*n), 0, 0)),
        pl.BlockSpec((2 * rows, LANES), lambda *n: (0, head_of(*n))),
        pl.BlockSpec((1, 1, rows), lambda *n: (head_of(*n), 0, 0)),
    ]


def attend_backward_kernel(q_t, gout_t, delta, gout_q, mass, k_ref, v_ref, gq_ref, gkv_ref, gq_sum):
    step = pl.program_id(1)
    gkv_ref[...], part = score_grads(q_t, gout_t, delta, gout_q, mass, k_ref, v_ref)

    @pl.when(step == 0)
    def _():
        gq_sum[...] = part

    @pl.when(step > 0)
    def _():
        gq_sum[...] += part

    @pl.when(step == pl.num_programs(1) - 1)
    def _():
        gq_ref[...] = (gq_sum[...] * HEAD_DIM**-0.5).astype(BF16)


def attend_backward(queries_t, gouts_t, delta, gout_q, mass, keys, values):
    width, rows = queries_t.shape
    span = keys.shape[0]
    heads = width // LANES
    tile = span // 4
    key_spec = pl.BlockSpec((tile, LANES), lambda h, j: (j, h))
    return pl.pallas_call(
        attend_backward_kernel,
        grid=(heads, span // tile),
        in_specs=head_specs(rows, lambda h, j: h) + [key_spec, key_spec],
        out_specs=[
            pl.BlockSpec((HEAD_DIM, rows), lambda h, j: (h, 0)),
            pl.BlockSpec((tile, LANES), lambda h, j: (j, h)),
        ],
        out_shape=[
            jax.ShapeDtypeStruct((heads * HEAD_DIM, rows), BF16),
            jax.ShapeDtypeStruct((span, width), BF16),
        ],
        scratch_shapes=[pltpu.VMEM((HEAD_DIM, rows), F32)],
        compiler_params=pltpu.CompilerParams(vmem_limit_bytes=VMEM_LIMIT),
        name="attend_backward",
    )(queries_t, gouts_t, delta, gout_q, mass, keys, values)


def erf_parts(u):
    size = jnp.abs(u)
    t = 1.0 / (1.0 + 0.2316418882 * size)
    bell = jnp.exp2(u * u * (-0.5 * LOG2E))
    poly = 0.5306027144 * t - 0.7265760135
    poly = poly * t + 0.7107068705
    poly = poly * t - 0.1422483683
    poly = poly * t + 0.1274147959
    tail = poly * t * bell
    return jnp.where(u < 0.0, tail, 1.0 - tail), bell * (2.0 * math.pi) ** -0.5


def core_order(matrix):
    width = matrix.shape[1] // 4
    return jnp.concatenate(
        [matrix[:, b * width : (b + 1) * width] for b in (0, 2, 1, 3)], axis=1
    )


def middle_kernel(
    lengths_ref,
    tok_ref,
    att_ref,
    other_in,
    dmask_ref,
    w_out_ref,
    bias_out_ref,
    gain_ref,
    shift_ref,
    w_up_in,
    bias_up_ref,
    w_down_in,
    bias_down_ref,
    patch_w_in,
    class_w_ref,
    class_ref,
    mask_ref,
    joined_ref,
    normed_ref,
    active_ref,
    ghid_ref,
    final_ref,
    gpatch_ref,
    gfeed_ref,
    gbranch_ref,
    gbranch_p_ref,
    gmid_ref,
    early_ref,
    classes_ref,
    slope,
    class_low,
    class_part_ref,
    gbias_down_ref,
    gbias_up_ref,
    gbias_out_ref,
    ggain_ref,
    gshift_ref,
    w_up_ref,
    w_down_ref,
    patch_w_ref,
    got_ref,
    load,
    send,
    recv,
):
    step = pl.program_id(0)
    seq = lax.axis_index("seq")
    moves = ((w_up_in, w_up_ref), (w_down_in, w_down_ref), (patch_w_in, patch_w_ref))
    loads = [pltpu.make_async_copy(a, b, load.at[i]) for i, (a, b) in enumerate(moves)]
    core = lax.rem(seq, 2)
    tile, width = tok_ref.shape
    third = width // 4
    scale = math.sqrt(width)
    chunks = w_up_ref.shape[1] // width

    @pl.when(step == 0)
    def _():
        greet_core(seq)
        for copy in loads:
            copy.start()
        await_core()
        swap_tokens(seq, other_in, got_ref, send, recv).start()
        classes = dot_nn(class_ref[...], class_w_ref[...])
        classes_ref[...] = classes
        class_low[...] = (
            classes * lax.rsqrt(jnp.sum(classes * classes, axis=-1, keepdims=True) + EPS_UNIT)
        ).astype(BF16)
        for ref in (class_part_ref, gbias_down_ref, gbias_up_ref, gbias_out_ref, ggain_ref, gshift_ref):
            ref[...] = jnp.zeros_like(ref)

    @pl.when(step == 0)
    def _():
        swap_tokens(seq, other_in, got_ref, send, recv).wait()

    here = pl.ds(pl.multiple_of(step * tile, tile), tile)
    for head in range(width // LANES):
        within, group = divmod(head, 2)
        at = 2 * group * third + within * HEAD_DIM
        own = slice(head * HEAD_DIM, (head + 1) * HEAD_DIM)
        joined_ref[pl.ds(at + core * third, HEAD_DIM), :] = att_ref[own, :]
        joined_ref[pl.ds(at + (1 - core) * third, HEAD_DIM), :] = got_ref[own, here]
    branch = dot_tn(joined_ref[...], w_out_ref[...]) + as_row(bias_out_ref)
    middle = tok_ref[...].astype(F32) + branch
    centred = middle - jnp.mean(middle, axis=-1, keepdims=True)
    inv = lax.rsqrt(jnp.mean(centred * centred, axis=-1, keepdims=True) + EPS_NORM)
    normal = centred * inv
    normed = (normal * as_row(gain_ref) + as_row(shift_ref)).astype(BF16)
    normed_ref[...] = normed
    bias_up = as_row(bias_up_ref)

    def ready(at):
        @pl.when(step == 0)
        def _():
            loads[at].wait()

    ready(0)
    final = middle + as_row(bias_down_ref)
    for chunk in range(chunks):
        cols = slice(chunk * width, (chunk + 1) * width)
        hidden = dot_nn(normed, w_up_ref[:, cols]) + bias_up[:, cols]
        below, density = erf_parts(hidden)
        active = (hidden * below).astype(BF16)
        active_ref[:, cols] = active
        slope[:, cols] = below + hidden * density
        if chunk == 0:
            ready(1)
        final = final + dot_nn(active, w_down_ref[cols, :])
    final_low = final.astype(BF16)
    final_ref[...] = final_low
    ready(2)
    patches = dot_nn(final_low, patch_w_ref[...])
    unit_scale = lax.rsqrt(jnp.sum(patches * patches, axis=-1, keepdims=True) + EPS_UNIT)
    unit = patches * unit_scale
    unit_low = unit.astype(BF16)
    first_row = seq * (tile * pl.num_programs(0)) + step * tile
    where_lane = lax.broadcasted_iota(jnp.int32, (1, tile), 1) + first_row
    valid = jnp.where(where_lane < lengths_ref[0], 1.0, 0.0)
    mask_ref[...] = (dot_nt(class_low[...], unit_low) * (scale * valid)).astype(BF16)
    gmask = (dmask_ref[...].astype(F32) * valid).astype(BF16)
    class_part_ref[...] += dot_nn(gmask, unit_low) * scale
    gunit = dot_tn(gmask, class_low[...]) * scale
    gpatch = (
        unit_scale * (gunit - unit * jnp.sum(gunit * unit, axis=-1, keepdims=True))
    ).astype(BF16)
    gpatch_ref[...] = core_order(gpatch)
    gfinal = dot_nt(gpatch, patch_w_ref[...])
    gfeed = gfinal.astype(BF16)
    gfeed_ref[...] = core_order(gfeed)
    gbias_down_ref[...] += jnp.sum(gfeed.astype(F32), axis=0, keepdims=True)
    gnormed = jnp.zeros((tile, width), F32)
    for chunk in range(chunks):
        cols = slice(chunk * width, (chunk + 1) * width)
        ghidden = (dot_nt(gfeed, w_down_ref[cols, :]) * slope[:, cols]).astype(BF16)
        ghid_ref[:, cols] = ghidden
        gbias_up_ref[:, cols] += jnp.sum(ghidden.astype(F32), axis=0, keepdims=True)
        gnormed = gnormed + dot_nt(ghidden, w_up_ref[:, cols])
    ggain_ref[...] += jnp.sum(gnormed * normal, axis=0, keepdims=True)
    gshift_ref[...] += jnp.sum(gnormed, axis=0, keepdims=True)
    turned = gnormed * as_row(gain_ref)
    gmid = gfinal + inv * (
        turned
        - jnp.mean(turned, axis=-1, keepdims=True)
        - normal * jnp.mean(turned * normal, axis=-1, keepdims=True)
    )
    gmid_ref[...] = gmid
    gbranch = gmid.astype(BF16)
    gbranch_ref[...] = gbranch
    gbranch_p_ref[...] = core_order(gbranch)
    gbias_out_ref[...] += jnp.sum(gbranch.astype(F32), axis=0, keepdims=True)

    @pl.when(step == pl.num_programs(0) - 1)
    def _():
        class_rows = class_part_ref.shape[0]
        at = early_ref.shape[0] - 16
        early_ref[...] = jnp.zeros_like(early_ref)
        early_ref[:class_rows, :] = class_part_ref[...].astype(BF16)
        parts = [gbias_down_ref[...], gbias_out_ref[...], ggain_ref[...], gshift_ref[...]]
        parts += [gbias_up_ref[:, i * width : (i + 1) * width] for i in range(chunks)]
        parts += [jnp.zeros_like(gbias_down_ref)] * (16 - len(parts))
        early_ref[at:, :] = jnp.concatenate(parts, axis=0).astype(BF16)


def middle(lengths, tokens, att_own, att_other, d_masks, params):
    rows, width = tokens.shape
    tile = rows // 2
    classes = d_masks.shape[0]
    hidden = params[4].shape[1]
    full = lambda a: pl.BlockSpec(a.shape, lambda i: (0,) * len(a.shape))
    tiled = lambda n: pl.BlockSpec((tile, n), lambda i: (i, 0))
    turned = lambda n: pl.BlockSpec((n, tile), lambda i: (0, i))
    shape = jax.ShapeDtypeStruct
    low = lambda n: shape((rows, n), BF16)
    early_rows = (classes + 15) // 16 * 16 + 16
    sums = [shape((early_rows, width), BF16), shape((classes, width), F32)]
    return pl.pallas_call(
        middle_kernel,
        grid_spec=pl.GridSpec(
            grid=(2,),
            in_specs=[
                pl.BlockSpec(memory_space=pltpu.SMEM),
                tiled(width),
                turned(width // 2),
                pl.BlockSpec(memory_space=pl.ANY),
                turned(classes),
            ]
            + [
                pl.BlockSpec(memory_space=pl.ANY)
                if at in (4, 6, 8)
                else pl.BlockSpec(
                    a.shape, lambda i, n=a.ndim: (0,) * n, pipeline_mode=pl.Buffered(1)
                )
                for at, a in enumerate(params)
            ],
            out_specs=[
                turned(classes),
                turned(width),
                tiled(width),
                tiled(hidden),
                tiled(hidden),
                tiled(width),
                tiled(width),
                tiled(width),
                tiled(width),
                tiled(width),
                tiled(width),
            ]
            + [full(a) for a in sums],
            scratch_shapes=[
                pltpu.VMEM((tile, hidden), F32),
                pltpu.VMEM((classes, width), BF16),
                pltpu.VMEM((classes, width), F32),
                pltpu.VMEM((1, width), F32),
                pltpu.VMEM((1, hidden), F32),
                pltpu.VMEM((1, width), F32),
                pltpu.VMEM((1, width), F32),
                pltpu.VMEM((1, width), F32),
                pltpu.VMEM(params[4].shape, BF16),
                pltpu.VMEM(params[6].shape, BF16),
                pltpu.VMEM(params[8].shape, BF16),
                pltpu.VMEM((width // 2, rows), BF16),
                pltpu.SemaphoreType.DMA((3,)),
                pltpu.SemaphoreType.DMA,
                pltpu.SemaphoreType.DMA,
            ],
        ),
        out_shape=[
            shape((classes, rows), BF16),
            shape((width, rows), BF16),
            low(width),
            low(hidden),
            low(hidden),
            low(width),
            low(width),
            low(width),
            low(width),
            low(width),
            shape((rows, width), F32),
        ]
        + sums,
        compiler_params=pltpu.CompilerParams(
            vmem_limit_bytes=VMEM_LIMIT, collective_id=4, has_side_effects=True
        ),
        cost_estimate=pl.CostEstimate(
            flops=4 * rows * width * (2 * hidden + 2 * width),
            bytes_accessed=40 * MIB,
            transcendentals=2 * rows * hidden,
        ),
        name="middle",
    )(lengths, tokens, att_own, att_other, d_masks, *params)


def weights_kernel(
    normed_in,
    ghid_in,
    active_in,
    gfeed_in,
    joined_in,
    gbranch_in,
    gbranch_p_in,
    final_in,
    gpatch_in,
    w_out_in,
    att_own_in,
    att_other_in,
    early_in,
    gout_q_in,
    up_out,
    down_out,
    pair_out,
    early_out,
    gout_q_out,
    gout_t_out,
    delta_out,
    normed,
    ghid,
    active,
    gfeed,
    joined,
    gbranch,
    gbranch_p,
    final,
    gpatch,
    w_out,
    att_own,
    att_other,
    early,
    w_pad,
    up_part,
    down_part,
    pair_part,
    up_got,
    down_got,
    pair_got,
    branch_got,
    gout,
    gout_t,
    delta,
    early_got,
    pair_sum,
    pair_far,
    send,
    recv,
    load,
    store,
):
    seq = lax.axis_index("seq")
    grp = lax.axis_index("grp")
    core = lax.rem(seq, 2)
    x = seq // 2
    y = lax.rem(grp, 2)
    z = lax.rem(grp // 2, 2)
    rows, width = normed.shape
    half = width // 2
    heads = width // LANES
    third = width // 4
    tiles = active.shape[1] // width
    peer = {"seq": seq + 1 - 2 * core}

    peer_x = {"seq": seq + 2 - 4 * x}
    peer_y = {"grp": grp + 1 - 2 * y}
    peer_z = {"grp": grp + 2 - 4 * z}
    peers = (peer, peer_x, peer_y, peer_z)

    barrier = pltpu.get_barrier_semaphore()
    for other in peers:
        pl.semaphore_signal(barrier, inc=1, device_id=other, device_id_type=MESH)

    ins = (
        (joined_in, joined),
        (gbranch_p_in, gbranch_p),
        (final_in, final),
        (gpatch_in, gpatch),
        (gfeed_in, gfeed),
        (active_in, active),
        (normed_in, normed),
        (ghid_in, ghid),
        (w_out_in, w_out),
        (gbranch_in, gbranch),
        (att_own_in, att_own),
        (att_other_in, att_other),
        (early_in, early),
    )
    loads = [pltpu.make_async_copy(a, b, load.at[i]) for i, (a, b) in enumerate(ins)]
    for copy in loads:
        copy.start()
    pl.semaphore_wait(barrier, len(peers))

    def far(at, src, dst, to=peer):
        return pltpu.make_async_remote_copy(
            src_ref=src,
            dst_ref=dst,
            send_sem=send.at[at],
            recv_sem=recv.at[at],
            device_id=to,
            device_id_type=MESH,
        )

    def far_early(i):
        return far(4 + tiles + i, early, early_got.at[i], (peer, peer_y, peer_x)[i])

    def early_step(i):
        far_early(i).wait()
        early[...] = early[...] + early_got[i]

    def far_z():
        return far(7 + tiles, pair_sum.at[:, 1 - z], pair_far, peer_z)

    def far_branch():
        return far(0, gbranch_in, branch_got)

    def far_pair():
        return far(1, pair_part.at[1 - core], pair_got)

    def far_down(i):
        return far(2 + i, down_part.at[1 - core, i], down_got.at[i])

    def far_up(i):
        return far(2 + tiles + i, up_part.at[1 - core, i], up_got.at[i])

    def lanes(index, size):
        return pl.ds(pl.multiple_of(index * size, size), size)

    stores = []

    def gouts():
        loads[8].wait()
        loads[9].wait()
        w_pad[...] = jnp.zeros_like(w_pad)
        for head in range(heads):
            within, group = divmod(head, 2)
            at = 2 * group * third + within * HEAD_DIM
            w_pad[head * LANES : head * LANES + HEAD_DIM, :] = w_out[
                pl.ds(pl.multiple_of(at + core * third, HEAD_DIM), HEAD_DIM), :
            ]
        loads[10].wait()
        loads[11].wait()
        for at, (rows_in, att) in enumerate(((gbranch, att_own), (branch_got, att_other))):
            if at == 1:
                far_branch().wait()
            spot = slice(at * rows, (at + 1) * rows)
            gout[spot, :] = dot_nt(rows_in[...], w_pad[...]).astype(BF16)
            turned = gout[spot, :].T
            gout_t[:, spot] = turned
            for head in range(heads):
                low = turned[head * LANES : head * LANES + HEAD_DIM].astype(F32)
                own = att[head * HEAD_DIM : (head + 1) * HEAD_DIM, :].astype(F32)
                delta[head, :, spot] = jnp.sum(low * own, axis=0, keepdims=True)
        stores.extend([
            pltpu.make_async_copy(gout, gout_q_out.at[pl.ds(0, 2 * rows)], store.at[0]),
            pltpu.make_async_copy(gout_t, gout_t_out, store.at[4]),
            pltpu.make_async_copy(delta, delta_out, store.at[5]),
        ])
        for copy in stores:
            copy.start()

    far_branch().start()
    for i in range(4):
        loads[i].wait()
    first = dot_nn(joined[...], gbranch_p[...]).astype(BF16)
    second = dot_tn(final[...], gpatch[...]).astype(BF16)
    for i in range(2):
        pair_part[i, :, :half] = first[:, i * half : (i + 1) * half]
        pair_part[i, :, half:] = second[:, i * half : (i + 1) * half]
    far_pair().start()
    loads[12].wait()
    far_early(0).start()
    gouts()
    early_step(0)
    far_early(1).start()
    far_pair().wait()
    pair_sum[...] = (pair_part[core] + pair_got[...]).reshape(pair_sum.shape)
    far_z().start()
    loads[4].wait()
    loads[5].wait()

    def down_tile(i, carry):
        part = dot_tn(active[:, lanes(i, width)], gfeed[...]).astype(BF16)
        down_part[0, i] = part[:, :half]
        down_part[1, i] = part[:, half:]
        far_down(i).start()
        return carry

    lax.fori_loop(0, tiles, down_tile, 0)
    early_step(1)
    far_early(2).start()
    loads[6].wait()
    loads[7].wait()

    def up_of(which, i):
        block = 2 * (x + i - 2 * i * x) + which
        up_part[which, i] = dot_tn(normed[...], ghid[:, lanes(block, width)]).astype(BF16)

    for i in range(2):
        up_of(1 - core, i)
        far_up(i).start()
    for i in range(2):
        up_of(core, i)

    def keep(at, part, out):
        copy = pltpu.make_async_copy(part, out, store.at[at])
        copy.start()
        stores.append(copy)

    def keep_down(i, carry):
        far_down(i).wait()
        down_part[core, i] = down_part[core, i] + down_got[i]
        return carry

    lax.fori_loop(0, tiles, keep_down, 0)
    keep(2, down_part.at[core], down_out)
    for i in range(2):
        far_up(i).wait()
        up_part[core, i] = up_part[core, i] + up_got[i]
    keep(3, up_part.at[core], up_out)
    far_z().wait()
    for i in range(2):
        pair_sum[i, z] = pair_sum[i, z] + pair_far[i]
    keep(1, pair_sum.at[:, z], pair_out)
    early_step(2)
    keep(6, early, early_out)
    for copy in stores:
        copy.wait()


def weights(gout_q, *operands):
    rows, width = operands[0].shape
    hidden = operands[2].shape[1]
    tiles = hidden // width
    half = width // 2
    heads = width // LANES
    low = lambda *s: pltpu.VMEM(s, BF16)
    hbm = pl.BlockSpec(memory_space=pl.ANY)
    sets = [low(2, 2, width, width), low(2, tiles, width, half), low(2, width, width)]
    sets += [low(2, width, width), low(tiles, width, half), low(width, width)]
    shape = lambda *s: jax.ShapeDtypeStruct(s, BF16)
    early = operands[-1].shape
    each = width // 8
    outs = [
        shape(2, width, width),
        shape(tiles, width, half),
        shape(2, 2, each, width),
        shape(*early),
        shape(*gout_q.shape),
        shape(width, 2 * rows),
        jax.ShapeDtypeStruct((heads, 1, 2 * rows), F32),
    ]
    return pl.pallas_call(
        weights_kernel,
        in_specs=[hbm] * (len(operands) + 1),
        out_specs=[hbm] * len(outs),
        out_shape=outs,
        input_output_aliases={len(operands): 4},
        scratch_shapes=[low(*a.shape) for a in operands]
        + [low(width, width)]
        + sets
        + [
            low(rows, width),
            low(2 * rows, width),
            low(width, 2 * rows),
            pltpu.VMEM((heads, 1, 2 * rows), F32),
            low(3, *early),
            low(2, 2, 2, each, width),
            low(2, 2, each, width),
            pltpu.SemaphoreType.DMA((8 + tiles,)),
            pltpu.SemaphoreType.DMA((8 + tiles,)),
            pltpu.SemaphoreType.DMA((len(operands),)),
            pltpu.SemaphoreType.DMA((7,)),
        ],
        compiler_params=pltpu.CompilerParams(
            vmem_limit_bytes=VMEM_LIMIT, collective_id=1, has_side_effects=True
        ),
        cost_estimate=pl.CostEstimate(
            flops=4 * rows * width * (hidden + 2 * width),
            bytes_accessed=30 * MIB,
            transcendentals=0,
        ),
        name="weights",
    )(*operands, gout_q)


def weights_plain(
    gout_q,
    normed,
    ghid,
    active,
    gfeed,
    joined,
    gbranch,
    gbranch_p,
    final,
    gpatch,
    w_out,
    att_own,
    att_other,
    early,
):
    rows, width = normed.shape
    half = width // 2
    heads = width // LANES
    third = width // 4
    seq = lax.axis_index("seq")
    core = seq & 1

    def both_cores(matrix):
        mine = lax.dynamic_index_in_dim(matrix, core, 0, keepdims=False)
        other = lax.dynamic_index_in_dim(matrix, 1 - core, 0, keepdims=False)
        return (mine + swap(other, "seq", 1).astype(F32)).astype(BF16)

    up = dot_tn(normed, ghid).reshape(width, 2, 2, -1).transpose(2, 1, 0, 3)
    up = jnp.where(seq < 2, up, up[:, ::-1])
    down = dot_tn(active, gfeed).reshape(active.shape[1], 2, half).transpose(1, 0, 2)
    first = dot_nn(joined, gbranch_p).reshape(width, 2, half)
    second = dot_tn(final, gpatch).reshape(width, 2, half)
    pair = jnp.concatenate([first, second], axis=2).transpose(1, 0, 2)
    w_heads = w_out.reshape(2, 2, heads // 2, HEAD_DIM, width)
    w_heads = lax.dynamic_index_in_dim(w_heads, core, 1, keepdims=False)
    w_heads = w_heads.swapaxes(0, 1).reshape(heads, HEAD_DIM, width)
    w_pad = jnp.concatenate([w_heads, jnp.zeros_like(w_heads)], axis=1).reshape(width, width)
    branch = jnp.concatenate([gbranch, swap(gbranch, "seq", 1)])
    gout = dot_nt(branch, w_pad).astype(BF16)
    gout_t = gout.T
    att = jnp.concatenate([att_own, att_other], axis=1).reshape(heads, HEAD_DIM, 2 * rows)
    low = gout_t.reshape(heads, 2, HEAD_DIM, 2 * rows)[:, 0]
    delta = jnp.sum(low.astype(F32) * att.astype(F32), axis=1, keepdims=True)
    gout_q = jnp.concatenate([gout, gout_q[2 * rows :]])
    return (
        both_cores(up),
        both_cores(down),
        both_cores(pair),
        lax.psum(early.astype(F32), ("grp", "seq")),
        gout_q,
        gout_t,
        delta,
    )


EXCHANGES = tuple(
    chain + way
    for chain, ways in (
        ("U", "XYZW"),
        ("D", "YZWX"),
        ("C", "WYX"),
        ("V", "ZW"),
        ("G", "CXN"),
        ("L", "CXYZWD"),
        ("Q0", "YZWXCR"),
        ("Q1", "YZWXCR"),
        ("Q2", "YZWDyzwdXCR"),
    )
    for way in ways
)


def backward_kernel(
    q_t,
    gout_t,
    delta,
    gout_q,
    mass,
    k_ref,
    v_ref,
    up_in,
    down_in,
    pair_in,
    early_in,
    normed_in,
    tokens_in,
    gmid_in,
    gain_ref,
    wpair_ref,
    wqt_ref,
    up_out,
    down_out,
    pair_out,
    early_out,
    qkv_out,
    swap_out,
    late_out,
    gtok_out,
    gq_all,
    gq_low,
    gkv_all,
    far_dw,
    normed,
    tokens,
    gmid,
    gn_far,
    gn_send,
    gn_own,
    gkv_sum,
    au,
    ad,
    ac,
    wq,
    aq,
    bq,
    fin,
    piece,
    ru0,
    ru1,
    ru2,
    ru3,
    rd0,
    rd1,
    rd2,
    rd3,
    rc1,
    rc2,
    rc3,
    rv,
    rwy,
    rwz,
    rww,
    rqy,
    rqz,
    sqy,
    sqz,
    rqx,
    rqp,
    rg,
    rl,
    send,
    recv,
    local,
):
    step = pl.program_id(0)
    seq = lax.axis_index("seq")
    grp = lax.axis_index("grp")
    core = lax.rem(seq, 2)
    x = seq // 2
    y = lax.rem(grp, 2)
    z = lax.rem(grp // 2, 2)
    w = grp // 4
    peers = {
        "C": {"seq": seq + 1 - 2 * core},
        "X": {"seq": seq + 2 - 4 * x},
        "Y": {"grp": grp + 1 - 2 * y},
        "Z": {"grp": grp + 2 - 4 * z},
        "W": {"grp": grp + 4 - 8 * w},
        "D": {"grp": grp + 4 - 8 * w + 2 - 4 * z},
        "R": {"seq": seq + 2 - 4 * x + 1 - 2 * core},
    }
    tile = k_ref.shape[0]
    rows, heads = q_t.shape[1], gkv_all.shape[1] // LANES
    half = rows // 2
    width = wpair_ref.shape[1]
    tiles = half * 2 // tile
    per_phase = heads * tiles
    now = lax.rem(step, per_phase)
    head, block = now // tiles, lax.rem(now, tiles)

    def far(name, src, dst, way=None):
        at = EXCHANGES.index(name)
        return pltpu.make_async_remote_copy(
            src_ref=src,
            dst_ref=dst,
            send_sem=send.at[at],
            recv_sem=recv.at[at],
            device_id=peers[way or name[-1].upper()],
            device_id_type=MESH,
        )

    def near(at, src, dst):
        return pltpu.make_async_copy(src, dst, local.at[at])

    def add(dst, src, count):
        if count is None:
            dst[...] = dst[...] + src[...]
            return
        for i in range(count):
            dst[i] = dst[i] + src[i]

    def exchange(name):
        if name == "UX":
            return far(name, up_in.at[1], ru0)
        if name == "UY":
            return far(name, au.at[:, :, 1 - y], ru1)
        if name == "UZ":
            return far(name, au.at[:, 1 - z, y], ru2)
        if name == "UW":
            return far(name, au.at[1 - w, z, y], ru3)
        if name == "DY":
            return far(name, down_in.at[:, :, 1 - y], rd0)
        if name == "DZ":
            return far(name, ad.at[:, 1 - z], rd1)
        if name == "DW":
            return far(name, ad.at[1 - w, z], rd2)
        if name == "DX":
            return far(name, ad.at[w, z], rd3)
        if name == "CW":
            return far(name, pair_in.at[1 - w], rc1)
        if name == "CY":
            return far(name, ac.at[w, 1 - y], rc2)
        if name == "CX":
            return far(name, ac.at[w, y], rc3)
        if name[0] == "V":
            return far(name, early_out, rv.at["ZW".index(name[1])])
        if name == "GC":
            return far(name, gn_far.at[1], rg.at[0])
        if name == "GX":
            return far(name, gn_far.at[0], rg.at[1])
        if name == "GN":
            return far(name, gn_send, rg.at[2], "C")
        if name[0] == "L":
            return far(name, late_out, rl.at["CXYZWD".index(name[1])])
        b, way = int(name[1]), name[2]
        spots = {"Z": (w, 1 - z), "W": (1 - w, z), "D": (1 - w, 1 - z)}
        if way == "X":
            return far(name, fin.at[b], rqx.at[b])
        if way in "CR":
            return far(name, piece.at[b, "CR".index(way)], rqp.at[b, "CR".index(way)])
        if b < 2:
            if way == "Y":
                return far(name, wq.at[b, :, :, 1 - y], rwy.at[b])
            if way == "Z":
                return far(name, wq.at[b, :, 1 - z, y], rwz.at[b])
            return far(name, wq.at[b, 1 - w, z, y], rww.at[b])
        if way == "Y":
            return far(name, aq.at[:, :, 1 - y], rqy)
        if way in spots:
            return far(name, aq.at[*spots[way], y], rqz.at["ZWD".index(way)])
        if way == "y":
            return far(name, bq.at[w, z, 1 - y], sqy)
        return far(name, bq.at[*spots[way.upper()]], sqz.at["zwd".index(way)])

    def arrive(name):
        exchange(name).wait()
        if name == "UX":
            near(0, up_in.at[0], au).wait()
            for i in range(2):
                for j in range(2):
                    add(au.at[i, j], ru0.at[i, j], 2)
        elif name == "UY":
            for i in range(2):
                for j in range(2):
                    add(au.at[i, j, y], ru1.at[i, j], None)
        elif name == "UZ":
            for i in range(2):
                add(au.at[i, z, y], ru2.at[i], None)
        elif name == "UW":
            up_out[...] = au[w, z, y].astype(F32) + ru3[...].astype(F32)
        elif name == "DY":
            near(1, down_in.at[:, :, y], ad).wait()
            for i in range(2):
                add(ad.at[i], rd0.at[i], 2)
        elif name == "DZ":
            for i in range(2):
                add(ad.at[i, z], rd1.at[i], None)
        elif name == "DW":
            add(ad.at[w, z], rd2, None)
        elif name == "DX":
            down_out[...] = ad[w, z].astype(F32) + rd3[...].astype(F32)
        elif name == "CW":
            near(2, pair_in, ac).wait()
            add(ac.at[w], rc1, 2)
        elif name == "CY":
            add(ac.at[w, y], rc2, None)
        elif name == "CX":
            pair_out[...] = ac[w, y].astype(F32) + rc3[...].astype(F32)
        elif name[0] == "V":
            add(early_out, rv.at["ZW".index(name[1])], None)
        elif name == "GC":
            add(gn_far.at[0], rg.at[0], None)
        elif name[0] == "L":
            add(late_out, rl.at["CXYZWD".index(name[1])], None)
        elif name[0] != "Q":
            pass
        elif name[1] != "2":
            b = int(name[1])
            if name[2] == "Y":
                for i in range(2):
                    for j in range(2):
                        add(wq.at[b, i, j, y], rwy.at[b, i, j], None)
            elif name[2] == "Z":
                for i in range(2):
                    add(wq.at[b, i, z, y], rwz.at[b, i], None)
            elif name[2] == "W":
                add(wq.at[b, w, z, y], rww.at[b], None)
        elif name[2] == "Y":
            for i in range(2):
                for j in range(2):
                    add(aq.at[i, j, y], rqy.at[i, j], None)
        elif name[2] in "ZWD":
            add(aq.at[w, z, y], rqz.at["ZWD".index(name[2])], None)
        elif name[2] == "y":
            add(bq.at[w, z, y], sqy, None)
        elif name[2] in "zwd":
            add(bq.at[w, z], sqz.at["zwd".index(name[2])], 2)

    def start(*names):
        for name in names:
            exchange(name).start()

    def next_of(come, *then):
        for name in come.split():
            arrive(name)
        start(*then)

    def round_one():
        arrive("Q2Y")
        start("Q2Z", "Q2W", "Q2D")
        for way in "zwd":
            arrive("Q2" + way)
        start("Q2y")

    def pick(matrix, at, group):
        size = HEAD_DIM
        low = matrix[:, group * size : (group + 1) * size]
        high = matrix[:, (group + 3) * size : (group + 4) * size]
        return jnp.where(at == 0, low, high)

    def round_two(b):
        for way in "ZWDy" if b == 2 else "W":
            arrive("Q%d%s" % (b, way))
        if b == 2:
            whole = jnp.concatenate([aq[w, z, y], bq[w, z, y]], axis=1)
        else:
            whole = wq[b, w, z, y]
        fin[b] = whole
        for i, at in enumerate((x, 1 - x)):
            part = jnp.where(core == 0, pick(whole, at, 2), pick(whole, at, 0))
            piece[b, i] = jnp.concatenate([part, jnp.zeros_like(part)], axis=1)
        start("Q%dX" % b, "Q%dC" % b, "Q%dR" % b)

    def round_three(b):
        for way in "XCR":
            arrive("Q%d%s" % (b, way))
        qkv_out[b] = fin[b].astype(F32) + rqx[b].astype(F32)
        swap_out[b] = rqp[b, 0].astype(F32) + rqp[b, 1].astype(F32)

    def at_step(number, action):
        @pl.when(step == number)
        def _():
            action()

    def weights_of(b):
        lanes = slice(2 * b * LANES, 2 * (b + 1) * LANES)
        both = dot_tn(gkv_all[:, lanes], normed[...]) + far_dw[lanes, :]
        low_rows = gq_all[2 * b : 2 * b + 2].reshape(LANES, rows) * HEAD_DIM**-0.5
        low_rows = low_rows.astype(BF16)
        gq_low[b * LANES : (b + 1) * LANES, :] = low_rows
        query = dot_nn(low_rows, normed[...])
        size = HEAD_DIM
        stacked = jnp.concatenate(
            [
                query,
                both[size : 2 * size],
                both[3 * size :],
                both[:size],
                both[2 * size : 3 * size],
            ],
            axis=0,
        )
        turned = stacked.T.astype(BF16)
        if b < 2:
            wq[b] = turned.reshape(wq.shape[1:])
            start("Q%dY" % b)
        else:
            cut = aq.shape[-1]
            aq[...] = turned[:, :cut].reshape(aq.shape)
            bq[...] = turned[:, cut:].reshape(bq.shape)
            start("Q2Y", "Q2z", "Q2w", "Q2d")

    def first_step():
        barrier = pltpu.get_barrier_semaphore()
        for peer in peers.values():
            pl.semaphore_signal(barrier, inc=1, device_id=peer, device_id_type=MESH)
        pl.semaphore_wait(barrier, len(peers))
        near(0, up_in.at[0], au).start()
        near(1, down_in.at[:, :, y], ad).start()
        near(2, pair_in, ac).start()
        near(3, early_in, early_out).start()
        start("UX", "DY", "CW")
        near(4, normed_in.at[pl.ds(rows, rows)], normed).start()
        near(3, early_in, early_out).wait()

    def far_post():
        near(4, normed_in.at[pl.ds(rows, rows)], normed).wait()
        gkv_sum[...] = jnp.sum(gkv_all[...].astype(F32), axis=0, keepdims=True)
        for i in (1, 0):
            gn_far[i] = dot_nt(gkv_all[i * half : (i + 1) * half, :], wpair_ref[...]).astype(BF16)
            if i == 1:
                start("GC")
        far_dw[...] = dot_tn(gkv_all[...], normed[...])
        near(5, normed_in.at[pl.ds(0, rows)], normed).start()

    at_step(0, first_step)
    at_step(5, lambda: next_of("CW", "CY"))
    at_step(5, lambda: start("VZ"))
    at_step(7, lambda: next_of("VZ", "VW"))
    at_step(8, lambda: next_of("CY", "CX"))
    at_step(9, lambda: next_of("UX", "UY"))
    at_step(9, lambda: next_of("DY", "DZ"))
    at_step(11, lambda: arrive("CX"))
    at_step(12, far_post)
    at_step(13, lambda: next_of("GC", "GX"))
    at_step(13, lambda: arrive("VW"))
    at_step(14, lambda: next_of("UY", "UZ"))
    at_step(14, lambda: next_of("DZ", "DW"))
    at_step(16, lambda: near(5, normed_in.at[pl.ds(0, rows)], normed).wait())
    at_step(16, lambda: weights_of(0))
    at_step(17, lambda: next_of("UZ", "UW"))
    at_step(19, lambda: next_of("Q0Y", "Q0Z"))
    at_step(19, lambda: next_of("DW", "DX"))
    at_step(20, lambda: weights_of(1))
    at_step(20, lambda: arrive("UW"))
    at_step(21, lambda: next_of("Q0Z", "Q0W"))
    at_step(20, lambda: near(6, tokens_in, tokens).start())
    at_step(20, lambda: near(7, gmid_in, gmid).start())
    at_step(23, lambda: round_two(0))
    at_step(23, lambda: next_of("Q1Y", "Q1Z"))

    gkv, part = score_grads(q_t, gout_t, delta, gout_q, mass, k_ref, v_ref)
    lanes = pl.ds(pl.multiple_of(head * LANES, LANES), LANES)
    gkv_all[pl.ds(pl.multiple_of(block * tile, tile), tile), lanes] = gkv

    @pl.when(step < per_phase)
    def _():
        @pl.when(block == 0)
        def _():
            gq_all[head] = part

        @pl.when(block != 0)
        def _():
            gq_all[head] += part

    @pl.when(step >= per_phase)
    def _():
        gq_all[head] += part

    @pl.when(step == 2 * per_phase - 1)
    def _():
        weights_of(2)

        def gn_of(at):
            spot = slice(at * half, (at + 1) * half)
            return dot_nt(gkv_all[spot, :], wpair_ref[...]) + dot_tn(gq_low[:, spot], wqt_ref[...])

        gn_send[...] = gn_of(1).astype(BF16)
        start("GN")
        gn_own[...] = gn_of(0)
        gkv_now = gkv_sum[...] + jnp.sum(gkv_all[...].astype(F32), axis=0, keepdims=True)
        ones = jnp.ones((8, rows), BF16)
        gq_now = dot_nt(ones, gq_low[...])[:1]
        gq_now = jnp.concatenate([gq_now, jnp.zeros_like(gq_now)], axis=1)
        next_of("Q1Z", "Q1W")
        arrive("GN")
        exchange("GX").wait()
        near(6, tokens_in, tokens).wait()
        rows_now = tokens[...].astype(F32)
        centred = rows_now - jnp.mean(rows_now, axis=-1, keepdims=True)
        inv = lax.rsqrt(jnp.mean(centred * centred, axis=-1, keepdims=True) + EPS_NORM)
        normal = centred * inv
        gn = gn_own[...] + rg[1].astype(F32) + rg[2].astype(F32)
        zero = jnp.zeros((1, width), F32)
        mine = core == 0
        late_out[...] = jnp.concatenate(
            [
                jnp.sum(gn * normal, axis=0, keepdims=True),
                jnp.sum(gn, axis=0, keepdims=True),
                zero,
                zero,
                jnp.where(mine, gq_now, zero),
                jnp.where(mine, zero, gq_now),
                jnp.where(mine, gkv_now, zero),
                jnp.where(mine, zero, gkv_now),
            ],
            axis=0,
        )
        start("LC")
        round_two(1)
        next_of("LC", "LX")
        round_one()
        near(7, gmid_in, gmid).wait()
        turned = gn * as_row(gain_ref)
        gtok_out[...] = (
            gmid[...]
            + inv
            * (
                turned
                - jnp.mean(turned, axis=-1, keepdims=True)
                - normal * jnp.mean(turned * normal, axis=-1, keepdims=True)
            )
        ).astype(BF16)
        next_of("LX", "LY")
        round_three(0)
        round_three(1)
        arrive("DX")
        round_two(2)
        next_of("LY", "LZ", "LW", "LD")
        round_three(2)
        for name in ("LZ", "LW", "LD"):
            exchange(name).wait()
        for at in range(3, 6):
            late_out[...] = late_out[...] + rl[at]


def backward(head_arrays, keys, values, sums, early, normed, tokens, gmid, gain, wpair, wqt):
    width, rows = head_arrays[0].shape
    heads = width // LANES
    half = rows // 2
    tile = half
    up, down, pair = sums
    each = up.shape[4]
    down_each, down_width = down.shape[3:]
    grid = 4 * heads
    head_of = lambda n: lax.rem(n, 2 * heads) // 2
    key_spec = pl.BlockSpec(
        (tile, LANES), lambda n: ((1 - n // (2 * heads)) * 2 + lax.rem(n, 2), head_of(n))
    )
    hbm = pl.BlockSpec(memory_space=pl.ANY)
    vmem = pl.BlockSpec(memory_space=pltpu.VMEM)
    low = lambda *s: pltpu.VMEM(s, BF16)
    full = lambda *s: pltpu.VMEM(s, F32)
    qkv_width = width // 2
    wide = qkv_width - LANES
    outs = [
        jax.ShapeDtypeStruct((each, width), F32),
        jax.ShapeDtypeStruct((down_each, down_width), F32),
        jax.ShapeDtypeStruct((each, width), F32),
        jax.ShapeDtypeStruct(early.shape, BF16),
        jax.ShapeDtypeStruct((3, each, qkv_width), F32),
        jax.ShapeDtypeStruct((3, each, LANES), F32),
        jax.ShapeDtypeStruct((8, width), F32),
        jax.ShapeDtypeStruct((half, width), BF16),
    ]
    return pl.pallas_call(
        backward_kernel,
        grid=(grid,),
        in_specs=head_specs(rows, head_of) + [key_spec, key_spec] + [hbm] * 7
        + [vmem] * 3,
        out_specs=[vmem] * len(outs),
        out_shape=outs,
        scratch_shapes=[
            full(heads, HEAD_DIM, rows),
            low(heads * HEAD_DIM, rows),
            low(rows, width),
            full(width, width),
            low(rows, width),
            low(half, width),
            full(half, width),
            low(2, half, width),
            low(half, width),
            full(half, width),
            full(1, width),
            low(2, 2, 2, each, width),
            low(2, 2, down_each, down_width),
            low(2, 2, each, width),
            low(2, 2, 2, 2, each, qkv_width),
            low(2, 2, 2, each, wide),
            low(2, 2, 2, each, LANES),
            low(3, each, qkv_width),
            low(3, 2, each, LANES),
            low(2, 2, 2, each, width),
            low(2, 2, each, width),
            low(2, each, width),
            low(each, width),
            low(2, 2, down_each, down_width),
            low(2, down_each, down_width),
            low(down_each, down_width),
            low(down_each, down_width),
            low(2, each, width),
            low(each, width),
            low(each, width),
            low(2, *early.shape),
            low(2, 2, 2, each, qkv_width),
            low(2, 2, each, qkv_width),
            low(2, each, qkv_width),
            low(2, 2, each, wide),
            low(3, each, wide),
            low(each, LANES),
            low(3, 2, each, LANES),
            low(3, each, qkv_width),
            low(3, 2, each, LANES),
            low(3, half, width),
            full(6, 8, width),
            pltpu.SemaphoreType.DMA((len(EXCHANGES),)),
            pltpu.SemaphoreType.DMA((len(EXCHANGES),)),
            pltpu.SemaphoreType.DMA((8,)),
        ],
        compiler_params=pltpu.CompilerParams(
            vmem_limit_bytes=VMEM_LIMIT, collective_id=0, has_side_effects=True
        ),
        cost_estimate=pl.CostEstimate(
            flops=40 * heads * rows * rows * LANES,
            bytes_accessed=40 * MIB,
            transcendentals=2 * heads * rows * rows,
        ),
        name="backward",
    )(*head_arrays, keys, values, up, down, pair, early, normed, tokens, gmid, gain, wpair, wqt)


def finish_kernel(
    up_ref,
    down_ref,
    pair_ref,
    early_ref,
    qkv_ref,
    swap_ref,
    late_ref,
    gtok_ref,
    classes_ref,
    class_ref,
    class_w_ref,
    up_out,
    down_out,
    wout_out,
    patch_out,
    qkv_out,
    class_w_out,
    class_out,
    gtok_out,
    gbias_up_out,
    *rest,
):
    vector_outs, product = rest[:-1], rest[-1]
    seq, grp = lax.axis_index("seq"), lax.axis_index("grp")
    core, x = lax.rem(seq, 2), seq // 2
    gtok_out[...] = gtok_ref[...]
    width = up_ref.shape[1]
    third = width // 4
    each = up_ref.shape[0]
    size = HEAD_DIM
    up_out[...] = up_ref[...]
    down_out[...] = jnp.where(x == 0, down_ref[:, :third], down_ref[:, third:]).T
    wout_out[...] = jnp.where(x == 0, pair_ref[:, :third], pair_ref[:, third : 2 * third])
    patch_out[...] = jnp.where(x == 0, pair_ref[:, 2 * third : 3 * third], pair_ref[:, 3 * third :])

    def group(j):
        parts = []
        for b in range(3):
            low = qkv_ref[b, :, j * size : (j + 1) * size]
            high = qkv_ref[b, :, (j + 3) * size : (j + 4) * size]
            parts.append(jnp.where(x == 0, low, high))
        return jnp.concatenate(parts, axis=1)

    first, second, last = group(0), group(1), group(2)
    got = jnp.concatenate([swap_ref[b, :, :size] for b in range(3)], axis=1)
    qkv_out[...] = jnp.concatenate(
        [jnp.where(core == 0, first, second), got, jnp.where(core == 0, second, last)], axis=1
    )

    classes = classes_ref[...]
    count = classes.shape[0]
    scale = lax.rsqrt(jnp.sum(classes * classes, axis=-1, keepdims=True) + EPS_UNIT)
    unit = classes * scale
    gunit = early_ref[:count, :].astype(F32)
    gclass = (scale * (gunit - unit * jnp.sum(gunit * unit, axis=-1, keepdims=True))).astype(BF16)
    product[...] = dot_tn(class_ref[...], gclass)
    block = product[pl.ds(grp * each, each), :]
    mine = block[:, :third]
    for s in range(1, 4):
        mine = jnp.where(seq == s, block[:, s * third : (s + 1) * third], mine)
    class_w_out[...] = mine

    def own_lanes(matrix, each):
        total = matrix.shape[1]
        return pltpu.roll(matrix, lax.rem(total - grp * each, total), 1)[:, :each]

    class_out[...] = own_lanes(dot_nt(gclass, class_w_ref[...]), each)
    at = early_ref.shape[0] - 16
    vectors = early_ref[at:, :].astype(F32)
    late = late_ref[...]

    def all_heads(first, second):
        parts = []
        for g in range(2):
            for vector in (first, second):
                parts += [vector[i * 2 + g] for i in range(3)]
        return jnp.concatenate(parts, axis=1)

    def lanes_of(matrix, row, stride, count):
        return [matrix[row : row + 1, i * stride : i * stride + size] for i in range(count)]

    gquery = all_heads(lanes_of(late, 4, size, 6), lanes_of(late, 5, size, 6))
    gvalue = all_heads(lanes_of(late, 6, 2 * size, 6), lanes_of(late, 7, 2 * size, 6))
    packed = jnp.concatenate(
        [vectors[:4], late[:2], gquery, gvalue], axis=0
    )
    mine = own_lanes(packed, each)
    for i, ref in enumerate(vector_outs):
        ref[...] = mine[i]
    chunks = gbias_up_out.shape[0] // each
    flat = jnp.concatenate([vectors[4 + i : 5 + i] for i in range(chunks)], axis=1)
    flat = jnp.concatenate([flat] * 8, axis=0)
    gbias_up_out[...] = own_lanes(flat, chunks * each)[0]


def finish(*operands):
    up, down, pair, early, qkv, _, late, gtok, classes, class_emb, class_w = operands
    each, width = up.shape
    third = width // 4
    hidden_each = down.shape[0]
    shapes = [
        (each, width),
        (third, hidden_each),
        (each, third),
        (each, third),
        (each, 3 * third),
        (each, third),
        (classes.shape[0], each),
        gtok.shape,
        (hidden_each,),
    ] + [(each,)] * 8
    vmem = pl.BlockSpec(memory_space=pltpu.VMEM)
    return pl.pallas_call(
        finish_kernel,
        in_specs=[vmem] * len(operands),
        out_specs=[vmem] * len(shapes),
        out_shape=[jax.ShapeDtypeStruct(s, BF16 if s == gtok.shape else F32) for s in shapes],
        scratch_shapes=[pltpu.VMEM((width, width), F32)],
        compiler_params=pltpu.CompilerParams(vmem_limit_bytes=VMEM_LIMIT),
        name="finish",
    )(*operands)


def layer_norm(matrix_rows, gain_vec, shift_vec):
    row_mean = jnp.mean(matrix_rows, axis=-1, keepdims=True)
    centred = matrix_rows - row_mean
    row_var = jnp.mean(centred * centred, axis=-1, keepdims=True)
    return centred * lax.rsqrt(row_var + EPS_NORM) * gain_vec + shift_vec


def unit_rows(matrix_rows):
    return matrix_rows * lax.rsqrt(
        jnp.sum(matrix_rows * matrix_rows, axis=-1, keepdims=True) + EPS_UNIT
    )


def column_sum(matrix_low):
    return jnp.sum(matrix_low.astype(F32), axis=0)


def swap(value, axis, bit):
    size = lax.axis_size(axis)
    return lax.ppermute(value, axis, [(i, i ^ bit) for i in range(size)])


def add_low(first, second):
    return (first.astype(F32) + second.astype(F32)).astype(BF16)


def sum_rows(part):
    groups = lax.axis_size("grp")
    bits = groups.bit_length() - 1
    here = lax.axis_index("grp")
    each = part.shape[0] // groups
    width = part.shape[1]
    part = part.reshape((2,) * bits + (each, width))
    for name in range(bits):
        axis = bits - 1 - name
        mine = (here >> name) & 1
        send = lax.dynamic_index_in_dim(part, 1 - mine, axis, keepdims=True)
        keep = lax.dynamic_index_in_dim(part, mine, axis, keepdims=True)
        part = add_low(keep, swap(send, "grp", 1 << name))
    return part.reshape(each, width)


def sum_x(part, x_here):
    half = part.shape[1] // 2
    low, high = part[:, :half], part[:, half:]
    mine = jnp.where(x_here == 0, low, high)
    other = jnp.where(x_here == 0, high, low)
    return mine.astype(F32) + swap(other, "seq", 2).astype(F32)


def body(
    tokens_in,
    lengths,
    ln1_gain,
    ln1_bias,
    w_qkv,
    bias_query,
    bias_value,
    w_out,
    bias_out,
    ln2_gain,
    ln2_bias,
    w_up,
    bias_up,
    w_down,
    bias_down,
    proj_patch,
    proj_class,
    class_emb,
    d_masks,
):
    row_count, model_width = tokens_in.shape
    head_count = model_width // HEAD_DIM
    heads_here = head_count // 2
    third = model_width // 4
    seq_devices = lax.axis_size("seq")
    grp_devices = lax.axis_size("grp")
    seq_here = lax.axis_index("seq")
    grp_here = lax.axis_index("grp")
    core = seq_here & 1
    x_here = seq_here >> 1

    tokens_x = swap(tokens_in, "seq", 2)
    normed_image, w_kv, value_bias, w_pairs, w_query_t, queries_t, gout_q, keys, values = project_near(
        lengths, tokens_in, ln1_gain, ln1_bias, w_qkv, bias_query, bias_value
    )
    partial, near_top = attend_forward(attend_near_kernel, "attend_near", queries_t, keys, values)
    tokens_x, partial = lax.optimization_barrier((tokens_x, partial))
    normed_image, keys, values = project_far(
        lengths,
        tokens_x,
        ln1_gain,
        ln1_bias,
        w_kv,
        value_bias,
        (normed_image, keys, values),
    )
    att_own, att_other, mass = attend_forward(
        attend_far_kernel, "attend_far", queries_t, keys, values, partial, near_top
    )
    (
        mask_out,
        joined,
        normed_two,
        active,
        grad_hidden,
        final_low,
        grad_patches,
        grad_feed,
        grad_branch,
        grad_branch_p,
        grad_middle,
        early,
        classes,
    ) = middle(
        lengths,
        tokens_in,
        att_own,
        att_other,
        d_masks.T,
        (
            w_out,
            bias_out,
            ln2_gain,
            ln2_bias,
            w_up,
            bias_up,
            w_down,
            bias_down,
            proj_patch,
            proj_class,
            class_emb,
        ),
    )
    fused = grp_devices == 8 and model_width % (16 * grp_devices) == 0
    up_sum, down_sum, pair_sum, early, gout_q, gouts_t, delta = (weights if fused else weights_plain)(
        gout_q,
        normed_two,
        grad_hidden,
        active,
        grad_feed,
        joined,
        grad_branch,
        grad_branch_p,
        final_low,
        grad_patches,
        w_out,
        att_own,
        att_other,
        early,
    )
    head_arrays = (queries_t, gouts_t, delta, gout_q, mass)
    down_sum = down_sum.reshape(bias_up.shape[0], model_width // 2)
    rows_each = model_width // grp_devices
    ff_each = bias_up.shape[0] // grp_devices
    cols_each = model_width // seq_devices

    if fused:
        sums = (
            up_sum.reshape(2, 2, 2, 2, rows_each, -1),
            down_sum.reshape(2, 2, 2, ff_each, -1),
            pair_sum,
        )
        raw = backward(
            head_arrays,
            keys,
            values,
            sums,
            early,
            normed_image,
            tokens_in,
            grad_middle,
            ln1_gain,
            w_pairs,
            w_query_t,
        )
        (
            out_w_up,
            out_w_down,
            out_w_out,
            out_proj_patch,
            out_w_qkv,
            grad_proj_class,
            grad_class_emb,
            grad_tokens,
            out_bias_up,
            *vectors,
        ) = finish(*raw, classes, class_emb, proj_class)
        return (
            mask_out.T,
            grad_tokens,
            vectors[4],
            vectors[5],
            out_w_qkv,
            vectors[6],
            vectors[7],
            out_w_out,
            vectors[1],
            vectors[2],
            vectors[3],
            out_w_up,
            out_bias_up,
            out_w_down.T,
            vectors[0],
            out_proj_patch,
            grad_proj_class,
            grad_class_emb,
        )

    out_w_down = sum_x(sum_rows(down_sum), x_here)
    out_w_up = sum_rows(add_low(up_sum[0], swap(up_sum[1], "seq", 2))).astype(F32)
    pair_rows = sum_rows(pair_sum)
    out_w_out = sum_x(pair_rows[:, : 2 * third], x_here)
    out_proj_patch = sum_x(pair_rows[:, 2 * third :], x_here)
    class_total = early[: class_emb.shape[0]]
    vectors = early[-16:]
    gq_t, gkv = attend_backward(*head_arrays, keys, values)

    gq = gq_t.T
    gn_far = dot_nt(gkv[2 * row_count :], w_pairs)
    gn_near = dot_nt(gkv[: 2 * row_count], w_pairs) + dot_nn(gq, w_query_t)
    far_got = swap(gn_far[row_count:].astype(BF16), "seq", 1)
    far_sum = (gn_far[:row_count] + far_got.astype(F32)).astype(BF16)
    near_got = swap(gn_near[row_count:].astype(BF16), "seq", 1)
    x_got = swap(far_sum, "seq", 2)
    grad_normed_one = gn_near[:row_count] + near_got.astype(F32) + x_got.astype(F32)
    norm_one_back = jax.vjp(layer_norm, tokens_in.astype(F32), ln1_gain, ln1_bias)[1]
    grad_tokens_norm, grad_ln1_gain, grad_ln1_bias = norm_one_back(grad_normed_one)
    grad_tokens = (grad_middle + grad_tokens_norm).astype(BF16)

    dw_q = dot_tn(normed_image[: 2 * row_count], gq).reshape(model_width, 3, 2, HEAD_DIM)
    dw_kv = dot_tn(normed_image, gkv).reshape(model_width, 3, 2, 2, HEAD_DIM)
    three = lambda matrix: matrix.reshape(model_width, third)
    part_zero = [three(dw_q[:, :, 0]), three(dw_q[:, :, 1]), three(dw_kv[:, :, 0, 1])]
    part_one = [three(dw_kv[:, :, 1, 1]), three(dw_kv[:, :, 0, 0]), three(dw_kv[:, :, 1, 0])]
    part_zero = jnp.concatenate(part_zero, axis=1).astype(BF16)
    part_one = jnp.concatenate(part_one, axis=1).astype(BF16)
    qkv_mine = jnp.where(x_here == 0, part_zero, part_one)
    qkv_other = jnp.where(x_here == 0, part_one, part_zero)
    qkv_rows = sum_rows(add_low(qkv_mine, swap(qkv_other, "seq", 2))).astype(F32)
    pieces = [qkv_rows[:, i * third : (i + 1) * third] for i in range(3)]
    piece_got = swap(jnp.where(core == 0, pieces[2], pieces[0]), "seq", 1)
    out_w_qkv = jnp.concatenate(
        [
            jnp.where(core == 0, pieces[0], pieces[1]),
            piece_got,
            jnp.where(core == 0, pieces[1], pieces[2]),
        ],
        axis=1,
    )

    def put_back(vector):
        halves = vector.reshape(3, 2, HEAD_DIM).swapaxes(0, 1).reshape(2, 1, third)
        zero = jnp.zeros_like(halves)
        both = jnp.where(
            core == 0,
            jnp.concatenate([halves, zero], axis=1),
            jnp.concatenate([zero, halves], axis=1),
        )
        return both.reshape(model_width)

    grad_bias_query = put_back(column_sum(gq))
    gkv_sums = column_sum(gkv).reshape(heads_here, 2, HEAD_DIM)
    grad_bias_value = put_back(gkv_sums[:, 0].reshape(heads_here * HEAD_DIM))
    late = jnp.stack([grad_ln1_gain, grad_ln1_bias, grad_bias_query, grad_bias_value], axis=1)
    late = jnp.concatenate([late, jnp.zeros((model_width, LANES - 4), F32)], axis=1).astype(BF16)
    late = add_low(late, swap(late, "seq", 1))
    late = sum_rows(add_low(late, swap(late, "seq", 2))).astype(F32)

    class_back = jax.vjp(unit_rows, classes)[1]
    grad_classes = class_back(class_total)[0].astype(BF16)

    def vector_rows(index):
        return lax.dynamic_slice_in_dim(vectors[index], grp_here * rows_each, rows_each, 0)

    out_bias_up = lax.dynamic_slice_in_dim(
        vectors[4 : 4 + bias_up.shape[0] // model_width].reshape(-1), grp_here * ff_each, ff_each, 0
    )
    emb_cols = lax.dynamic_slice_in_dim(class_emb, grp_here * rows_each, rows_each, 1)
    class_cols = lax.dynamic_slice_in_dim(grad_classes, seq_here * cols_each, cols_each, 1)
    grad_proj_class = dot_tn(emb_cols, class_cols)
    proj_rows = lax.dynamic_slice_in_dim(proj_class, grp_here * rows_each, rows_each, 0)
    grad_class_emb = dot_nt(grad_classes, proj_rows)
    return (
        mask_out.T,
        grad_tokens,
        late[:, 0],
        late[:, 1],
        out_w_qkv,
        late[:, 2],
        late[:, 3],
        out_w_out,
        vector_rows(1),
        vector_rows(2),
        vector_rows(3),
        out_w_up,
        out_bias_up,
        out_w_down,
        vector_rows(0),
        out_proj_patch,
        grad_proj_class,
        grad_class_emb,
    )


def solution(mesh):
    rows = P(("grp", "seq"), None)
    both = P("grp", "seq")
    return jax.shard_map(
        body,
        mesh=mesh,
        in_specs=(rows, P("grp")) + (P(),) * 16 + (rows,),
        out_specs=(
            rows,
            rows,
            P("grp"),
            P("grp"),
            both,
            P("grp"),
            P("grp"),
            both,
            P("grp"),
            P("grp"),
            P("grp"),
            both,
            P("grp"),
            both,
            P("grp"),
            both,
            both,
            P(None, "grp"),
        ),
        check_vma=False,
    )
```

```python
import functools
import math

import jax
import jax.numpy as jnp
from jax import lax
from jax.experimental import pallas as pl
from jax.experimental.pallas import tpu as pltpu
from jax.sharding import PartitionSpec as P

HEAD_DIM = 64
LANES = 128
EPS_NORM = 1e-06
EPS_UNIT = 1e-06
NEG_FILL = -1e30
LOG2E = math.log2(math.e)
F32 = jnp.float32
BF16 = jnp.bfloat16
MIB = 1 << 20
VMEM_LIMIT = 63 * MIB
MESH = pl.DeviceIdType.MESH


def dot_nn(a, b):
    return lax.dot_general(a, b, (((1,), (0,)), ((), ())), preferred_element_type=F32)


def dot_nt(a, b):
    return lax.dot_general(a, b, (((1,), (1,)), ((), ())), preferred_element_type=F32)


def dot_tn(a, b):
    return lax.dot_general(a, b, (((0,), (0,)), ((), ())), preferred_element_type=F32)


def swap_tokens(seq, src, dst, send, recv):
    return pltpu.make_async_remote_copy(
        src_ref=src,
        dst_ref=dst,
        send_sem=send,
        recv_sem=recv,
        device_id={"seq": seq + 1 - 2 * lax.rem(seq, 2)},
        device_id_type=MESH,
    )


def greet_core(seq):
    peer = {"seq": seq + 1 - 2 * lax.rem(seq, 2)}
    pl.semaphore_signal(
        pltpu.get_barrier_semaphore(), inc=1, device_id=peer, device_id_type=MESH
    )


def await_core():
    pl.semaphore_wait(pltpu.get_barrier_semaphore(), 1)


def normed_tile(step, per, own_ref, got, out_ref, gain_ref, shift_ref):
    tile = out_ref.shape[0]
    row = lax.rem(step, per) * tile

    @pl.when(step < per)
    def _():
        out_ref[...] = own_ref[pl.ds(pl.multiple_of(row, tile), tile), :]

    @pl.when(step >= per)
    def _():
        out_ref[...] = got[pl.ds(pl.multiple_of(row, tile), tile), :]

    rows = out_ref[...].astype(F32)
    centred = rows - jnp.mean(rows, axis=-1, keepdims=True)
    var = jnp.mean(centred * centred, axis=-1, keepdims=True)
    normed = centred * lax.rsqrt(var + EPS_NORM) * as_row(gain_ref) + as_row(shift_ref)
    normed = normed.astype(BF16)
    out_ref[...] = normed
    return normed, row


def spread(matrix, upper):
    zero = jnp.zeros((matrix.shape[0], HEAD_DIM), matrix.dtype)
    parts = []
    for at in range(0, matrix.shape[1], HEAD_DIM):
        piece = matrix[:, at : at + HEAD_DIM]
        parts += [zero, piece] if upper else [piece, zero]
    return jnp.concatenate(parts, axis=1)


def column_is(column, width):
    at = lax.broadcasted_iota(jnp.int32, (1, width), 1)
    return jnp.where(lax.rem(at, LANES) == column, 1.0, 0.0)


def key_mask(length, first_row, shape):
    where_row = lax.broadcasted_iota(jnp.int32, (shape[0], 1), 0) + first_row
    masked = jnp.where(where_row < length, 0.0, NEG_FILL)
    return masked * column_is(0, shape[1])


def keys_values(normed, mask, wkv_ref, vbias_ref, k_ref, v_ref):
    width = k_ref.shape[1]
    both = dot_nn(normed, wkv_ref[...])
    k_ref[...] = (spread(both[:, : width // 2], True) + mask).astype(BF16)
    value = spread(both[:, width // 2 :] + vbias_ref[...], False)
    v_ref[...] = (value + column_is(HEAD_DIM, width)).astype(BF16)


def project_near_kernel(
    lengths_ref,
    own_ref,
    gain_ref,
    shift_ref,
    w_ref,
    bias_query_ref,
    bias_value_ref,
    normed_ref,
    wkv_ref,
    vbias_ref,
    wpair_ref,
    wqt_ref,
    q_t_ref,
    gout_q_ref,
    k_ref,
    v_ref,
    wq,
    qbias,
    got,
    send,
    recv,
):
    step = pl.program_id(0)
    seq = lax.axis_index("seq")
    core = lax.rem(seq, 2)
    width = normed_ref.shape[1]
    tile = normed_ref.shape[0]
    rows = own_ref.shape[0]
    per = rows // tile

    @pl.when(step == 0)
    def _():
        greet_core(seq)
        bias_query, bias_value = as_row(bias_query_ref), as_row(bias_value_ref)
        for which in range(2):

            @pl.when(core == which)
            def _():
                rows_q, rows_v, queries, keys, values, pairs = [], [], [], [], [], []
                for head in range(width // LANES):
                    within, group = divmod(head, 2)
                    at = (2 * group + which) * (width // 4) + within * HEAD_DIM
                    spot = slice(at, at + HEAD_DIM)
                    queries.append(w_ref[:, spot])
                    keys.append(w_ref[:, width + at : width + at + HEAD_DIM])
                    values.append(w_ref[:, 2 * width + at : 2 * width + at + HEAD_DIM])
                    pairs += [values[-1], keys[-1]]
                    rows_q.append(bias_query[:, spot])
                    rows_v.append(bias_value[:, spot])
                together = jnp.concatenate(queries, axis=1)
                wq[...] = together
                wqt_ref[...] = together.T
                wkv_ref[...] = jnp.concatenate(keys + values, axis=1)
                wpair_ref[...] = jnp.concatenate(pairs, axis=1)
                qbias[...] = jnp.concatenate(rows_q, axis=1)
                vbias_ref[...] = jnp.concatenate(rows_v, axis=1)

        await_core()
        swap_tokens(seq, own_ref, got, send, recv).start()

    @pl.when(step == per)
    def _():
        swap_tokens(seq, own_ref, got, send, recv).wait()

    normed, row = normed_tile(step, per, own_ref, got, normed_ref, gain_ref, shift_ref)
    block = step // per
    place = seq + block * (1 - 2 * core)
    mixed = (dot_nn(normed, wq[...]) + qbias[...]).astype(BF16).astype(F32)
    query = spread(mixed * HEAD_DIM**-0.5, True)
    gout_q_ref[...] = query.astype(BF16)
    q_t_ref[...] = (query + column_is(0, width)).astype(BF16).T
    mask = key_mask(lengths_ref[0], place * rows + row, k_ref.shape)
    keys_values(normed, mask, wkv_ref, vbias_ref, k_ref, v_ref)


def project_far_kernel(
    lengths_ref,
    own_ref,
    gain_ref,
    shift_ref,
    wkv_ref,
    vbias_ref,
    normed_in,
    k_in,
    v_in,
    normed_ref,
    k_ref,
    v_ref,
    got,
    send,
    recv,
):
    step = pl.program_id(0)
    seq = lax.axis_index("seq")
    core = lax.rem(seq, 2)
    width = normed_ref.shape[1]
    tile = normed_ref.shape[0]
    rows = own_ref.shape[0]
    per = rows // tile

    @pl.when(step == 0)
    def _():
        greet_core(seq)
        await_core()
        swap_tokens(seq, own_ref, got, send, recv).start()

    @pl.when(step == per)
    def _():
        swap_tokens(seq, own_ref, got, send, recv).wait()

    normed, row = normed_tile(step, per, own_ref, got, normed_ref, gain_ref, shift_ref)
    block = step // per
    place = seq + 2 - 4 * (seq // 2) + block * (1 - 2 * core)
    mask = key_mask(lengths_ref[0], place * rows + row, k_ref.shape)
    keys_values(normed, mask, wkv_ref, vbias_ref, k_ref, v_ref)


def as_row(ref):
    return ref[...].reshape(1, -1)


def whole(a):
    return pl.BlockSpec(a.shape, lambda *_: (0,) * len(a.shape))


def project_near(lengths, tokens, gain, shift, w_qkv, bias_query, bias_value):
    rows, width = tokens.shape
    tile = rows // 2
    shape = lambda *s: jax.ShapeDtypeStruct(s, BF16)
    tiled = pl.BlockSpec((tile, width), lambda i: (i, 0))
    image = shape(4 * rows, width)
    outs = [
        image,
        shape(width, width),
        jax.ShapeDtypeStruct((1, width // 2), F32),
        shape(width, width),
        shape(width // 2, width),
        shape(width, 2 * rows),
        image,
        image,
        image,
    ]
    return pl.pallas_call(
        project_near_kernel,
        grid=(4,),
        in_specs=[pl.BlockSpec(memory_space=pltpu.SMEM)]
        + [whole(a) for a in (tokens, gain, shift, w_qkv, bias_query, bias_value)],
        out_specs=[
            tiled,
            whole(outs[1]),
            whole(outs[2]),
            whole(outs[3]),
            whole(outs[4]),
            pl.BlockSpec((width, tile), lambda i: (0, i)),
            pl.BlockSpec((tile, width), lambda i: (i + 4, 0)),
            tiled,
            tiled,
        ],
        out_shape=outs,
        scratch_shapes=[
            pltpu.VMEM((width, width // 2), BF16),
            pltpu.VMEM((1, width // 2), F32),
            pltpu.VMEM((rows, width), BF16),
            pltpu.SemaphoreType.DMA,
            pltpu.SemaphoreType.DMA,
        ],
        compiler_params=pltpu.CompilerParams(
            vmem_limit_bytes=VMEM_LIMIT, collective_id=2, has_side_effects=True
        ),
        cost_estimate=pl.CostEstimate(
            flops=12 * rows * width * width, bytes_accessed=20 * MIB, transcendentals=0
        ),
        name="project_near",
    )(lengths, tokens, gain, shift, w_qkv, bias_query, bias_value)


def project_far(lengths, tokens, gain, shift, wkv, vbias, images):
    rows, width = tokens.shape
    tile = rows // 2
    tiled = pl.BlockSpec((tile, width), lambda i: (i + 4, 0))
    return pl.pallas_call(
        project_far_kernel,
        grid=(4,),
        in_specs=[pl.BlockSpec(memory_space=pltpu.SMEM)]
        + [whole(a) for a in (tokens, gain, shift, wkv, vbias)]
        + [pl.BlockSpec(memory_space=pl.ANY)] * 3,
        out_specs=[tiled] * 3,
        out_shape=[jax.ShapeDtypeStruct(a.shape, a.dtype) for a in images],
        input_output_aliases={6: 0, 7: 1, 8: 2},
        scratch_shapes=[
            pltpu.VMEM((rows, width), BF16),
            pltpu.SemaphoreType.DMA,
            pltpu.SemaphoreType.DMA,
        ],
        compiler_params=pltpu.CompilerParams(
            vmem_limit_bytes=VMEM_LIMIT, collective_id=3, has_side_effects=True
        ),
        cost_estimate=pl.CostEstimate(
            flops=8 * rows * width * width, bytes_accessed=16 * MIB, transcendentals=0
        ),
        name="project_far",
    )(lengths, tokens, gain, shift, wkv, vbias, *images)


PART = 72


def attend_near_kernel(q_t_ref, k_ref, v_ref, part_ref, top_ref):
    scores = dot_nn(k_ref[...], q_t_ref[...])
    top = jnp.max(scores, axis=0, keepdims=True)
    prob = jnp.exp2((scores - top) * LOG2E).astype(BF16)
    part_ref[...] = dot_tn(v_ref[...], prob)[:PART]
    top_ref[0] = top


def attend_far_kernel(q_t_ref, k_ref, v_ref, part_ref, near_top_ref, own_ref, other_ref, mass_ref):
    scores = dot_nn(k_ref[...], q_t_ref[...])
    near_top = near_top_ref[0]
    top = jnp.maximum(jnp.max(scores, axis=0, keepdims=True), near_top)
    prob = jnp.exp2((scores - top) * LOG2E).astype(BF16)
    summed = dot_tn(v_ref[...], prob)[:PART]
    summed = summed + part_ref[...] * jnp.exp2((near_top - top) * LOG2E)
    total = summed[HEAD_DIM : HEAD_DIM + 1]
    mass_ref[0] = top * LOG2E + jnp.log2(total)
    out = (summed[:HEAD_DIM] / total).astype(BF16)
    half = own_ref.shape[1]
    own_ref[...] = out[:, :half]
    other_ref[...] = out[:, half:]


def attend_cost(heads, rows, span):
    return pl.CostEstimate(
        flops=8 * heads * rows * span * LANES,
        bytes_accessed=(rows + 2 * span) * heads * LANES * 2,
        transcendentals=heads * rows * span,
    )


def attend_forward(kernel, name, queries_t, keys, values, *partial):
    width, rows = queries_t.shape
    span = keys.shape[0] // 2
    heads = width // LANES
    at = 1 if partial else 0
    part_spec = pl.BlockSpec((PART, rows), lambda h: (h, 0))
    row_spec = pl.BlockSpec((1, 1, rows), lambda h: (h, 0, 0))
    row_shape = jax.ShapeDtypeStruct((heads, 1, rows), F32)
    if partial:
        out_specs = [pl.BlockSpec((HEAD_DIM, rows // 2), lambda h: (h, 0))] * 2 + [row_spec]
        outs = [jax.ShapeDtypeStruct((heads * HEAD_DIM, rows // 2), BF16)] * 2 + [row_shape]
    else:
        out_specs = [part_spec, row_spec]
        outs = [jax.ShapeDtypeStruct((heads * PART, rows), F32), row_shape]
    return pl.pallas_call(
        kernel,
        grid=(heads,),
        in_specs=[
            pl.BlockSpec((LANES, rows), lambda h: (h, 0)),
            pl.BlockSpec((span, LANES), lambda h: (at, h)),
            pl.BlockSpec((span, LANES), lambda h: (at, h)),
        ]
        + [part_spec, row_spec][: len(partial)],
        out_specs=out_specs,
        out_shape=outs,
        compiler_params=pltpu.CompilerParams(vmem_limit_bytes=VMEM_LIMIT),
        cost_estimate=attend_cost(heads, rows, span),
        name=name,
    )(queries_t, keys, values, *partial)


def score_grads(q_t_ref, gout_t_ref, delta_ref, gout_q_ref, mass_ref, k_ref, v_ref):
    key_now = k_ref[...]
    scores = dot_nn(key_now, q_t_ref[...])
    prob = jnp.exp2(scores * LOG2E - mass_ref[0])
    gprob = dot_nn(v_ref[...], gout_t_ref[...])
    gscore = (prob * (gprob - delta_ref[0])).astype(BF16)
    gkv = dot_nn(jnp.concatenate([prob.astype(BF16), gscore], axis=1), gout_q_ref[...])
    return gkv.astype(BF16), dot_tn(key_now, gscore)[HEAD_DIM:]


def head_specs(rows, head_of):
    return [
        pl.BlockSpec((LANES, rows), lambda *n: (head_of(*n), 0)),
        pl.BlockSpec((LANES, rows), lambda *n: (head_of(*n), 0)),
        pl.BlockSpec((1, 1, rows), lambda *n: (head_of(*n), 0, 0)),
        pl.BlockSpec((2 * rows, LANES), lambda *n: (0, head_of(*n))),
        pl.BlockSpec((1, 1, rows), lambda *n: (head_of(*n), 0, 0)),
    ]


def attend_backward_kernel(q_t, gout_t, delta, gout_q, mass, k_ref, v_ref, gq_ref, gkv_ref, gq_sum):
    step = pl.program_id(1)
    gkv_ref[...], part = score_grads(q_t, gout_t, delta, gout_q, mass, k_ref, v_ref)

    @pl.when(step == 0)
    def _():
        gq_sum[...] = part

    @pl.when(step > 0)
    def _():
        gq_sum[...] += part

    @pl.when(step == pl.num_programs(1) - 1)
    def _():
        gq_ref[...] = (gq_sum[...] * HEAD_DIM**-0.5).astype(BF16)


def attend_backward(queries_t, gouts_t, delta, gout_q, mass, keys, values):
    width, rows = queries_t.shape
    span = keys.shape[0]
    heads = width // LANES
    tile = span // 4
    key_spec = pl.BlockSpec((tile, LANES), lambda h, j: (j, h))
    return pl.pallas_call(
        attend_backward_kernel,
        grid=(heads, span // tile),
        in_specs=head_specs(rows, lambda h, j: h) + [key_spec, key_spec],
        out_specs=[
            pl.BlockSpec((HEAD_DIM, rows), lambda h, j: (h, 0)),
            pl.BlockSpec((tile, LANES), lambda h, j: (j, h)),
        ],
        out_shape=[
            jax.ShapeDtypeStruct((heads * HEAD_DIM, rows), BF16),
            jax.ShapeDtypeStruct((span, width), BF16),
        ],
        scratch_shapes=[pltpu.VMEM((HEAD_DIM, rows), F32)],
        compiler_params=pltpu.CompilerParams(vmem_limit_bytes=VMEM_LIMIT),
        name="attend_backward",
    )(queries_t, gouts_t, delta, gout_q, mass, keys, values)


def erf_parts(u):
    size = jnp.abs(u)
    t = 1.0 / (1.0 + 0.2316418882 * size)
    bell = jnp.exp2(u * u * (-0.5 * LOG2E))
    poly = 0.5306027144 * t - 0.7265760135
    poly = poly * t + 0.7107068705
    poly = poly * t - 0.1422483683
    poly = poly * t + 0.1274147959
    tail = poly * t * bell
    return jnp.where(u < 0.0, tail, 1.0 - tail), bell * (2.0 * math.pi) ** -0.5


def core_order(matrix):
    width = matrix.shape[1] // 4
    return jnp.concatenate(
        [matrix[:, b * width : (b + 1) * width] for b in (0, 2, 1, 3)], axis=1
    )


def middle_kernel(
    lengths_ref,
    tok_ref,
    att_ref,
    other_in,
    dmask_ref,
    w_out_ref,
    bias_out_ref,
    gain_ref,
    shift_ref,
    w_up_in,
    bias_up_ref,
    w_down_in,
    bias_down_ref,
    patch_w_in,
    class_w_ref,
    class_ref,
    mask_ref,
    joined_ref,
    normed_ref,
    active_ref,
    ghid_ref,
    final_ref,
    gpatch_ref,
    gfeed_ref,
    gbranch_ref,
    gbranch_p_ref,
    gmid_ref,
    early_ref,
    classes_ref,
    slope,
    class_low,
    class_part_ref,
    gbias_down_ref,
    gbias_up_ref,
    gbias_out_ref,
    ggain_ref,
    gshift_ref,
    w_up_ref,
    w_down_ref,
    patch_w_ref,
    got_ref,
    load,
    send,
    recv,
):
    step = pl.program_id(0)
    seq = lax.axis_index("seq")
    moves = ((w_up_in, w_up_ref), (w_down_in, w_down_ref), (patch_w_in, patch_w_ref))
    loads = [pltpu.make_async_copy(a, b, load.at[i]) for i, (a, b) in enumerate(moves)]
    core = lax.rem(seq, 2)
    tile, width = tok_ref.shape
    third = width // 4
    scale = math.sqrt(width)
    chunks = w_up_ref.shape[1] // width

    @pl.when(step == 0)
    def _():
        greet_core(seq)
        for copy in loads:
            copy.start()
        await_core()
        swap_tokens(seq, other_in, got_ref, send, recv).start()
        classes = dot_nn(class_ref[...], class_w_ref[...])
        classes_ref[...] = classes
        class_low[...] = (
            classes * lax.rsqrt(jnp.sum(classes * classes, axis=-1, keepdims=True) + EPS_UNIT)
        ).astype(BF16)
        for ref in (class_part_ref, gbias_down_ref, gbias_up_ref, gbias_out_ref, ggain_ref, gshift_ref):
            ref[...] = jnp.zeros_like(ref)

    @pl.when(step == 0)
    def _():
        swap_tokens(seq, other_in, got_ref, send, recv).wait()

    here = pl.ds(pl.multiple_of(step * tile, tile), tile)
    for head in range(width // LANES):
        within, group = divmod(head, 2)
        at = 2 * group * third + within * HEAD_DIM
        own = slice(head * HEAD_DIM, (head + 1) * HEAD_DIM)
        joined_ref[pl.ds(at + core * third, HEAD_DIM), :] = att_ref[own, :]
        joined_ref[pl.ds(at + (1 - core) * third, HEAD_DIM), :] = got_ref[own, here]
    branch = dot_tn(joined_ref[...], w_out_ref[...]) + as_row(bias_out_ref)
    middle = tok_ref[...].astype(F32) + branch
    centred = middle - jnp.mean(middle, axis=-1, keepdims=True)
    inv = lax.rsqrt(jnp.mean(centred * centred, axis=-1, keepdims=True) + EPS_NORM)
    normal = centred * inv
    normed = (normal * as_row(gain_ref) + as_row(shift_ref)).astype(BF16)
    normed_ref[...] = normed
    bias_up = as_row(bias_up_ref)

    def ready(at):
        @pl.when(step == 0)
        def _():
            loads[at].wait()

    ready(0)
    final = middle + as_row(bias_down_ref)
    for chunk in range(chunks):
        cols = slice(chunk * width, (chunk + 1) * width)
        hidden = dot_nn(normed, w_up_ref[:, cols]) + bias_up[:, cols]
        below, density = erf_parts(hidden)
        active = (hidden * below).astype(BF16)
        active_ref[:, cols] = active
        slope[:, cols] = below + hidden * density
        if chunk == 0:
            ready(1)
        final = final + dot_nn(active, w_down_ref[cols, :])
    final_low = final.astype(BF16)
    final_ref[...] = final_low
    ready(2)
    patches = dot_nn(final_low, patch_w_ref[...])
    unit_scale = lax.rsqrt(jnp.sum(patches * patches, axis=-1, keepdims=True) + EPS_UNIT)
    unit = patches * unit_scale
    unit_low = unit.astype(BF16)
    first_row = seq * (tile * pl.num_programs(0)) + step * tile
    where_lane = lax.broadcasted_iota(jnp.int32, (1, tile), 1) + first_row
    valid = jnp.where(where_lane < lengths_ref[0], 1.0, 0.0)
    mask_ref[...] = (dot_nt(class_low[...], unit_low) * (scale * valid)).astype(BF16)
    gmask = (dmask_ref[...].astype(F32) * valid).astype(BF16)
    class_part_ref[...] += dot_nn(gmask, unit_low) * scale
    gunit = dot_tn(gmask, class_low[...]) * scale
    gpatch = (
        unit_scale * (gunit - unit * jnp.sum(gunit * unit, axis=-1, keepdims=True))
    ).astype(BF16)
    gpatch_ref[...] = core_order(gpatch)
    gfinal = dot_nt(gpatch, patch_w_ref[...])
    gfeed = gfinal.astype(BF16)
    gfeed_ref[...] = core_order(gfeed)
    gbias_down_ref[...] += jnp.sum(gfeed.astype(F32), axis=0, keepdims=True)
    gnormed = jnp.zeros((tile, width), F32)
    for chunk in range(chunks):
        cols = slice(chunk * width, (chunk + 1) * width)
        ghidden = (dot_nt(gfeed, w_down_ref[cols, :]) * slope[:, cols]).astype(BF16)
        ghid_ref[:, cols] = ghidden
        gbias_up_ref[:, cols] += jnp.sum(ghidden.astype(F32), axis=0, keepdims=True)
        gnormed = gnormed + dot_nt(ghidden, w_up_ref[:, cols])
    ggain_ref[...] += jnp.sum(gnormed * normal, axis=0, keepdims=True)
    gshift_ref[...] += jnp.sum(gnormed, axis=0, keepdims=True)
    turned = gnormed * as_row(gain_ref)
    gmid = gfinal + inv * (
        turned
        - jnp.mean(turned, axis=-1, keepdims=True)
        - normal * jnp.mean(turned * normal, axis=-1, keepdims=True)
    )
    gmid_ref[...] = gmid
    gbranch = gmid.astype(BF16)
    gbranch_ref[...] = gbranch
    gbranch_p_ref[...] = core_order(gbranch)
    gbias_out_ref[...] += jnp.sum(gbranch.astype(F32), axis=0, keepdims=True)

    @pl.when(step == pl.num_programs(0) - 1)
    def _():
        class_rows = class_part_ref.shape[0]
        at = early_ref.shape[0] - 16
        early_ref[...] = jnp.zeros_like(early_ref)
        early_ref[:class_rows, :] = class_part_ref[...].astype(BF16)
        parts = [gbias_down_ref[...], gbias_out_ref[...], ggain_ref[...], gshift_ref[...]]
        parts += [gbias_up_ref[:, i * width : (i + 1) * width] for i in range(chunks)]
        parts += [jnp.zeros_like(gbias_down_ref)] * (16 - len(parts))
        early_ref[at:, :] = jnp.concatenate(parts, axis=0).astype(BF16)


def middle(lengths, tokens, att_own, att_other, d_masks, params):
    rows, width = tokens.shape
    tile = rows // 2
    classes = d_masks.shape[0]
    hidden = params[4].shape[1]
    full = lambda a: pl.BlockSpec(a.shape, lambda i: (0,) * len(a.shape))
    tiled = lambda n: pl.BlockSpec((tile, n), lambda i: (i, 0))
    turned = lambda n: pl.BlockSpec((n, tile), lambda i: (0, i))
    shape = jax.ShapeDtypeStruct
    low = lambda n: shape((rows, n), BF16)
    early_rows = (classes + 15) // 16 * 16 + 16
    sums = [shape((early_rows, width), BF16), shape((classes, width), F32)]
    return pl.pallas_call(
        middle_kernel,
        grid_spec=pl.GridSpec(
            grid=(2,),
            in_specs=[
                pl.BlockSpec(memory_space=pltpu.SMEM),
                tiled(width),
                turned(width // 2),
                pl.BlockSpec(memory_space=pl.ANY),
                turned(classes),
            ]
            + [
                pl.BlockSpec(memory_space=pl.ANY)
                if at in (4, 6, 8)
                else pl.BlockSpec(
                    a.shape, lambda i, n=a.ndim: (0,) * n, pipeline_mode=pl.Buffered(1)
                )
                for at, a in enumerate(params)
            ],
            out_specs=[
                turned(classes),
                turned(width),
                tiled(width),
                tiled(hidden),
                tiled(hidden),
                tiled(width),
                tiled(width),
                tiled(width),
                tiled(width),
                tiled(width),
                tiled(width),
            ]
            + [full(a) for a in sums],
            scratch_shapes=[
                pltpu.VMEM((tile, hidden), F32),
                pltpu.VMEM((classes, width), BF16),
                pltpu.VMEM((classes, width), F32),
                pltpu.VMEM((1, width), F32),
                pltpu.VMEM((1, hidden), F32),
                pltpu.VMEM((1, width), F32),
                pltpu.VMEM((1, width), F32),
                pltpu.VMEM((1, width), F32),
                pltpu.VMEM(params[4].shape, BF16),
                pltpu.VMEM(params[6].shape, BF16),
                pltpu.VMEM(params[8].shape, BF16),
                pltpu.VMEM((width // 2, rows), BF16),
                pltpu.SemaphoreType.DMA((3,)),
                pltpu.SemaphoreType.DMA,
                pltpu.SemaphoreType.DMA,
            ],
        ),
        out_shape=[
            shape((classes, rows), BF16),
            shape((width, rows), BF16),
            low(width),
            low(hidden),
            low(hidden),
            low(width),
            low(width),
            low(width),
            low(width),
            low(width),
            shape((rows, width), F32),
        ]
        + sums,
        compiler_params=pltpu.CompilerParams(
            vmem_limit_bytes=VMEM_LIMIT, collective_id=4, has_side_effects=True
        ),
        cost_estimate=pl.CostEstimate(
            flops=4 * rows * width * (2 * hidden + 2 * width),
            bytes_accessed=40 * MIB,
            transcendentals=2 * rows * hidden,
        ),
        name="middle",
    )(lengths, tokens, att_own, att_other, d_masks, *params)


def weights_kernel(
    normed_in,
    ghid_in,
    active_in,
    gfeed_in,
    joined_in,
    gbranch_in,
    gbranch_p_in,
    final_in,
    gpatch_in,
    w_out_in,
    att_own_in,
    att_other_in,
    early_in,
    gout_q_in,
    up_out,
    down_out,
    pair_out,
    early_out,
    gout_q_out,
    gout_t_out,
    delta_out,
    normed,
    ghid,
    active,
    gfeed,
    joined,
    gbranch,
    gbranch_p,
    final,
    gpatch,
    w_out,
    att_own,
    att_other,
    early,
    w_pad,
    up_part,
    down_part,
    pair_part,
    up_got,
    down_got,
    pair_got,
    branch_got,
    gout,
    gout_t,
    delta,
    early_got,
    pair_sum,
    pair_far,
    send,
    recv,
    load,
    store,
):
    seq = lax.axis_index("seq")
    grp = lax.axis_index("grp")
    core = lax.rem(seq, 2)
    x = seq // 2
    y = lax.rem(grp, 2)
    z = lax.rem(grp // 2, 2)
    rows, width = normed.shape
    half = width // 2
    heads = width // LANES
    third = width // 4
    tiles = active.shape[1] // width
    peer = {"seq": seq + 1 - 2 * core}

    peer_x = {"seq": seq + 2 - 4 * x}
    peer_y = {"grp": grp + 1 - 2 * y}
    peer_z = {"grp": grp + 2 - 4 * z}
    peers = (peer, peer_x, peer_y, peer_z)

    barrier = pltpu.get_barrier_semaphore()
    for other in peers:
        pl.semaphore_signal(barrier, inc=1, device_id=other, device_id_type=MESH)

    ins = (
        (joined_in, joined),
        (gbranch_p_in, gbranch_p),
        (final_in, final),
        (gpatch_in, gpatch),
        (gfeed_in, gfeed),
        (active_in, active),
        (normed_in, normed),
        (ghid_in, ghid),
        (w_out_in, w_out),
        (gbranch_in, gbranch),
        (att_own_in, att_own),
        (att_other_in, att_other),
        (early_in, early),
    )
    loads = [pltpu.make_async_copy(a, b, load.at[i]) for i, (a, b) in enumerate(ins)]
    for copy in loads:
        copy.start()
    pl.semaphore_wait(barrier, len(peers))

    def far(at, src, dst, to=peer):
        return pltpu.make_async_remote_copy(
            src_ref=src,
            dst_ref=dst,
            send_sem=send.at[at],
            recv_sem=recv.at[at],
            device_id=to,
            device_id_type=MESH,
        )

    def far_early(i):
        return far(4 + tiles + i, early, early_got.at[i], (peer, peer_y, peer_x)[i])

    def early_step(i):
        far_early(i).wait()
        early[...] = early[...] + early_got[i]

    def far_z():
        return far(7 + tiles, pair_sum.at[:, 1 - z], pair_far, peer_z)

    def far_branch():
        return far(0, gbranch_in, branch_got)

    def far_pair():
        return far(1, pair_part.at[1 - core], pair_got)

    def far_down(i):
        return far(2 + i, down_part.at[1 - core, i], down_got.at[i])

    def far_up(i):
        return far(2 + tiles + i, up_part.at[1 - core, i], up_got.at[i])

    def lanes(index, size):
        return pl.ds(pl.multiple_of(index * size, size), size)

    stores = []

    def gouts():
        loads[8].wait()
        loads[9].wait()
        w_pad[...] = jnp.zeros_like(w_pad)
        for head in range(heads):
            within, group = divmod(head, 2)
            at = 2 * group * third + within * HEAD_DIM
            w_pad[head * LANES : head * LANES + HEAD_DIM, :] = w_out[
                pl.ds(pl.multiple_of(at + core * third, HEAD_DIM), HEAD_DIM), :
            ]
        loads[10].wait()
        loads[11].wait()
        for at, (rows_in, att) in enumerate(((gbranch, att_own), (branch_got, att_other))):
            if at == 1:
                far_branch().wait()
            spot = slice(at * rows, (at + 1) * rows)
            gout[spot, :] = dot_nt(rows_in[...], w_pad[...]).astype(BF16)
            turned = gout[spot, :].T
            gout_t[:, spot] = turned
            for head in range(heads):
                low = turned[head * LANES : head * LANES + HEAD_DIM].astype(F32)
                own = att[head * HEAD_DIM : (head + 1) * HEAD_DIM, :].astype(F32)
                delta[head, :, spot] = jnp.sum(low * own, axis=0, keepdims=True)
        stores.extend([
            pltpu.make_async_copy(gout, gout_q_out.at[pl.ds(0, 2 * rows)], store.at[0]),
            pltpu.make_async_copy(gout_t, gout_t_out, store.at[4]),
            pltpu.make_async_copy(delta, delta_out, store.at[5]),
        ])
        for copy in stores:
            copy.start()

    far_branch().start()
    for i in range(4):
        loads[i].wait()
    first = dot_nn(joined[...], gbranch_p[...]).astype(BF16)
    second = dot_tn(final[...], gpatch[...]).astype(BF16)
    for i in range(2):
        pair_part[i, :, :half] = first[:, i * half : (i + 1) * half]
        pair_part[i, :, half:] = second[:, i * half : (i + 1) * half]
    far_pair().start()
    loads[12].wait()
    far_early(0).start()
    gouts()
    early_step(0)
    far_early(1).start()
    far_pair().wait()
    pair_sum[...] = (pair_part[core] + pair_got[...]).reshape(pair_sum.shape)
    far_z().start()
    loads[4].wait()
    loads[5].wait()

    def down_tile(i, carry):
        part = dot_tn(active[:, lanes(i, width)], gfeed[...]).astype(BF16)
        down_part[0, i] = part[:, :half]
        down_part[1, i] = part[:, half:]
        far_down(i).start()
        return carry

    lax.fori_loop(0, tiles, down_tile, 0)
    early_step(1)
    far_early(2).start()
    loads[6].wait()
    loads[7].wait()

    def up_of(which, i):
        block = 2 * (x + i - 2 * i * x) + which
        up_part[which, i] = dot_tn(normed[...], ghid[:, lanes(block, width)]).astype(BF16)

    for i in range(2):
        up_of(1 - core, i)
        far_up(i).start()
    for i in range(2):
        up_of(core, i)

    def keep(at, part, out):
        copy = pltpu.make_async_copy(part, out, store.at[at])
        copy.start()
        stores.append(copy)

    def keep_down(i, carry):
        far_down(i).wait()
        down_part[core, i] = down_part[core, i] + down_got[i]
        return carry

    lax.fori_loop(0, tiles, keep_down, 0)
    keep(2, down_part.at[core], down_out)
    for i in range(2):
        far_up(i).wait()
        up_part[core, i] = up_part[core, i] + up_got[i]
    keep(3, up_part.at[core], up_out)
    far_z().wait()
    for i in range(2):
        pair_sum[i, z] = pair_sum[i, z] + pair_far[i]
    keep(1, pair_sum.at[:, z], pair_out)
    early_step(2)
    keep(6, early, early_out)
    for copy in stores:
        copy.wait()


def weights(gout_q, *operands):
    rows, width = operands[0].shape
    hidden = operands[2].shape[1]
    tiles = hidden // width
    half = width // 2
    heads = width // LANES
    low = lambda *s: pltpu.VMEM(s, BF16)
    hbm = pl.BlockSpec(memory_space=pl.ANY)
    sets = [low(2, 2, width, width), low(2, tiles, width, half), low(2, width, width)]
    sets += [low(2, width, width), low(tiles, width, half), low(width, width)]
    shape = lambda *s: jax.ShapeDtypeStruct(s, BF16)
    early = operands[-1].shape
    each = width // 8
    outs = [
        shape(2, width, width),
        shape(tiles, width, half),
        shape(2, 2, each, width),
        shape(*early),
        shape(*gout_q.shape),
        shape(width, 2 * rows),
        jax.ShapeDtypeStruct((heads, 1, 2 * rows), F32),
    ]
    return pl.pallas_call(
        weights_kernel,
        in_specs=[hbm] * (len(operands) + 1),
        out_specs=[hbm] * len(outs),
        out_shape=outs,
        input_output_aliases={len(operands): 4},
        scratch_shapes=[low(*a.shape) for a in operands]
        + [low(width, width)]
        + sets
        + [
            low(rows, width),
            low(2 * rows, width),
            low(width, 2 * rows),
            pltpu.VMEM((heads, 1, 2 * rows), F32),
            low(3, *early),
            low(2, 2, 2, each, width),
            low(2, 2, each, width),
            pltpu.SemaphoreType.DMA((8 + tiles,)),
            pltpu.SemaphoreType.DMA((8 + tiles,)),
            pltpu.SemaphoreType.DMA((len(operands),)),
            pltpu.SemaphoreType.DMA((7,)),
        ],
        compiler_params=pltpu.CompilerParams(
            vmem_limit_bytes=VMEM_LIMIT, collective_id=1, has_side_effects=True
        ),
        cost_estimate=pl.CostEstimate(
            flops=4 * rows * width * (hidden + 2 * width),
            bytes_accessed=30 * MIB,
            transcendentals=0,
        ),
        name="weights",
    )(*operands, gout_q)


def weights_plain(
    gout_q,
    normed,
    ghid,
    active,
    gfeed,
    joined,
    gbranch,
    gbranch_p,
    final,
    gpatch,
    w_out,
    att_own,
    att_other,
    early,
):
    rows, width = normed.shape
    half = width // 2
    heads = width // LANES
    third = width // 4
    seq = lax.axis_index("seq")
    core = seq & 1

    def both_cores(matrix):
        mine = lax.dynamic_index_in_dim(matrix, core, 0, keepdims=False)
        other = lax.dynamic_index_in_dim(matrix, 1 - core, 0, keepdims=False)
        return (mine + swap(other, "seq", 1).astype(F32)).astype(BF16)

    up = dot_tn(normed, ghid).reshape(width, 2, 2, -1).transpose(2, 1, 0, 3)
    up = jnp.where(seq < 2, up, up[:, ::-1])
    down = dot_tn(active, gfeed).reshape(active.shape[1], 2, half).transpose(1, 0, 2)
    first = dot_nn(joined, gbranch_p).reshape(width, 2, half)
    second = dot_tn(final, gpatch).reshape(width, 2, half)
    pair = jnp.concatenate([first, second], axis=2).transpose(1, 0, 2)
    w_heads = w_out.reshape(2, 2, heads // 2, HEAD_DIM, width)
    w_heads = lax.dynamic_index_in_dim(w_heads, core, 1, keepdims=False)
    w_heads = w_heads.swapaxes(0, 1).reshape(heads, HEAD_DIM, width)
    w_pad = jnp.concatenate([w_heads, jnp.zeros_like(w_heads)], axis=1).reshape(width, width)
    branch = jnp.concatenate([gbranch, swap(gbranch, "seq", 1)])
    gout = dot_nt(branch, w_pad).astype(BF16)
    gout_t = gout.T
    att = jnp.concatenate([att_own, att_other], axis=1).reshape(heads, HEAD_DIM, 2 * rows)
    low = gout_t.reshape(heads, 2, HEAD_DIM, 2 * rows)[:, 0]
    delta = jnp.sum(low.astype(F32) * att.astype(F32), axis=1, keepdims=True)
    gout_q = jnp.concatenate([gout, gout_q[2 * rows :]])
    return (
        both_cores(up),
        both_cores(down),
        both_cores(pair),
        lax.psum(early.astype(F32), ("grp", "seq")),
        gout_q,
        gout_t,
        delta,
    )


EXCHANGES = tuple(
    chain + way
    for chain, ways in (
        ("U", "XYZW"),
        ("D", "YZWX"),
        ("C", "WYX"),
        ("V", "ZW"),
        ("G", "CXN"),
        ("L", "CXYZWD"),
        ("Q0", "YZWXCR"),
        ("Q1", "YZWXCR"),
        ("Q2", "YZWDyzwdXCR"),
    )
    for way in ways
)


def backward_kernel(
    q_t,
    gout_t,
    delta,
    gout_q,
    mass,
    k_ref,
    v_ref,
    up_in,
    down_in,
    pair_in,
    early_in,
    normed_in,
    tokens_in,
    gmid_in,
    gain_ref,
    wpair_ref,
    wqt_ref,
    up_out,
    down_out,
    pair_out,
    early_out,
    qkv_out,
    swap_out,
    late_out,
    gtok_out,
    gq_all,
    gq_low,
    gkv_all,
    far_dw,
    normed,
    tokens,
    gmid,
    gn_far,
    gn_send,
    gn_own,
    gkv_sum,
    au,
    ad,
    ac,
    wq,
    aq,
    bq,
    fin,
    piece,
    ru0,
    ru1,
    ru2,
    ru3,
    rd0,
    rd1,
    rd2,
    rd3,
    rc1,
    rc2,
    rc3,
    rv,
    rwy,
    rwz,
    rww,
    rqy,
    rqz,
    sqy,
    sqz,
    rqx,
    rqp,
    rg,
    rl,
    send,
    recv,
    local,
):
    step = pl.program_id(0)
    seq = lax.axis_index("seq")
    grp = lax.axis_index("grp")
    core = lax.rem(seq, 2)
    x = seq // 2
    y = lax.rem(grp, 2)
    z = lax.rem(grp // 2, 2)
    w = grp // 4
    peers = {
        "C": {"seq": seq + 1 - 2 * core},
        "X": {"seq": seq + 2 - 4 * x},
        "Y": {"grp": grp + 1 - 2 * y},
        "Z": {"grp": grp + 2 - 4 * z},
        "W": {"grp": grp + 4 - 8 * w},
        "D": {"grp": grp + 4 - 8 * w + 2 - 4 * z},
        "R": {"seq": seq + 2 - 4 * x + 1 - 2 * core},
    }
    tile = k_ref.shape[0]
    rows, heads = q_t.shape[1], gkv_all.shape[1] // LANES
    half = rows // 2
    width = wpair_ref.shape[1]
    tiles = half * 2 // tile
    per_phase = heads * tiles
    now = lax.rem(step, per_phase)
    head, block = now // tiles, lax.rem(now, tiles)

    def far(name, src, dst, way=None):
        at = EXCHANGES.index(name)
        return pltpu.make_async_remote_copy(
            src_ref=src,
            dst_ref=dst,
            send_sem=send.at[at],
            recv_sem=recv.at[at],
            device_id=peers[way or name[-1].upper()],
            device_id_type=MESH,
        )

    def near(at, src, dst):
        return pltpu.make_async_copy(src, dst, local.at[at])

    def add(dst, src, count):
        if count is None:
            dst[...] = dst[...] + src[...]
            return
        for i in range(count):
            dst[i] = dst[i] + src[i]

    def exchange(name):
        if name == "UX":
            return far(name, up_in.at[1], ru0)
        if name == "UY":
            return far(name, au.at[:, :, 1 - y], ru1)
        if name == "UZ":
            return far(name, au.at[:, 1 - z, y], ru2)
        if name == "UW":
            return far(name, au.at[1 - w, z, y], ru3)
        if name == "DY":
            return far(name, down_in.at[:, :, 1 - y], rd0)
        if name == "DZ":
            return far(name, ad.at[:, 1 - z], rd1)
        if name == "DW":
            return far(name, ad.at[1 - w, z], rd2)
        if name == "DX":
            return far(name, ad.at[w, z], rd3)
        if name == "CW":
            return far(name, pair_in.at[1 - w], rc1)
        if name == "CY":
            return far(name, ac.at[w, 1 - y], rc2)
        if name == "CX":
            return far(name, ac.at[w, y], rc3)
        if name[0] == "V":
            return far(name, early_out, rv.at["ZW".index(name[1])])
        if name == "GC":
            return far(name, gn_far.at[1], rg.at[0])
        if name == "GX":
            return far(name, gn_far.at[0], rg.at[1])
        if name == "GN":
            return far(name, gn_send, rg.at[2], "C")
        if name[0] == "L":
            return far(name, late_out, rl.at["CXYZWD".index(name[1])])
        b, way = int(name[1]), name[2]
        spots = {"Z": (w, 1 - z), "W": (1 - w, z), "D": (1 - w, 1 - z)}
        if way == "X":
            return far(name, fin.at[b], rqx.at[b])
        if way in "CR":
            return far(name, piece.at[b, "CR".index(way)], rqp.at[b, "CR".index(way)])
        if b < 2:
            if way == "Y":
                return far(name, wq.at[b, :, :, 1 - y], rwy.at[b])
            if way == "Z":
                return far(name, wq.at[b, :, 1 - z, y], rwz.at[b])
            return far(name, wq.at[b, 1 - w, z, y], rww.at[b])
        if way == "Y":
            return far(name, aq.at[:, :, 1 - y], rqy)
        if way in spots:
            return far(name, aq.at[*spots[way], y], rqz.at["ZWD".index(way)])
        if way == "y":
            return far(name, bq.at[w, z, 1 - y], sqy)
        return far(name, bq.at[*spots[way.upper()]], sqz.at["zwd".index(way)])

    def arrive(name):
        exchange(name).wait()
        if name == "UX":
            near(0, up_in.at[0], au).wait()
            for i in range(2):
                for j in range(2):
                    add(au.at[i, j], ru0.at[i, j], 2)
        elif name == "UY":
            for i in range(2):
                for j in range(2):
                    add(au.at[i, j, y], ru1.at[i, j], None)
        elif name == "UZ":
            for i in range(2):
                add(au.at[i, z, y], ru2.at[i], None)
        elif name == "UW":
            up_out[...] = au[w, z, y].astype(F32) + ru3[...].astype(F32)
        elif name == "DY":
            near(1, down_in.at[:, :, y], ad).wait()
            for i in range(2):
                add(ad.at[i], rd0.at[i], 2)
        elif name == "DZ":
            for i in range(2):
                add(ad.at[i, z], rd1.at[i], None)
        elif name == "DW":
            add(ad.at[w, z], rd2, None)
        elif name == "DX":
            down_out[...] = ad[w, z].astype(F32) + rd3[...].astype(F32)
        elif name == "CW":
            near(2, pair_in, ac).wait()
            add(ac.at[w], rc1, 2)
        elif name == "CY":
            add(ac.at[w, y], rc2, None)
        elif name == "CX":
            pair_out[...] = ac[w, y].astype(F32) + rc3[...].astype(F32)
        elif name[0] == "V":
            add(early_out, rv.at["ZW".index(name[1])], None)
        elif name == "GC":
            add(gn_far.at[0], rg.at[0], None)
        elif name[0] == "L":
            add(late_out, rl.at["CXYZWD".index(name[1])], None)
        elif name[0] != "Q":
            pass
        elif name[1] != "2":
            b = int(name[1])
            if name[2] == "Y":
                for i in range(2):
                    for j in range(2):
                        add(wq.at[b, i, j, y], rwy.at[b, i, j], None)
            elif name[2] == "Z":
                for i in range(2):
                    add(wq.at[b, i, z, y], rwz.at[b, i], None)
            elif name[2] == "W":
                add(wq.at[b, w, z, y], rww.at[b], None)
        elif name[2] == "Y":
            for i in range(2):
                for j in range(2):
                    add(aq.at[i, j, y], rqy.at[i, j], None)
        elif name[2] in "ZWD":
            add(aq.at[w, z, y], rqz.at["ZWD".index(name[2])], None)
        elif name[2] == "y":
            add(bq.at[w, z, y], sqy, None)
        elif name[2] in "zwd":
            add(bq.at[w, z], sqz.at["zwd".index(name[2])], 2)

    def start(*names):
        for name in names:
            exchange(name).start()

    def next_of(come, *then):
        for name in come.split():
            arrive(name)
        start(*then)

    def round_one():
        arrive("Q2Y")
        start("Q2Z", "Q2W", "Q2D")
        for way in "zwd":
            arrive("Q2" + way)
        start("Q2y")

    def pick(matrix, at, group):
        size = HEAD_DIM
        low = matrix[:, group * size : (group + 1) * size]
        high = matrix[:, (group + 3) * size : (group + 4) * size]
        return jnp.where(at == 0, low, high)

    def round_two(b):
        for way in "ZWDy" if b == 2 else "W":
            arrive("Q%d%s" % (b, way))
        if b == 2:
            whole = jnp.concatenate([aq[w, z, y], bq[w, z, y]], axis=1)
        else:
            whole = wq[b, w, z, y]
        fin[b] = whole
        for i, at in enumerate((x, 1 - x)):
            part = jnp.where(core == 0, pick(whole, at, 2), pick(whole, at, 0))
            piece[b, i] = jnp.concatenate([part, jnp.zeros_like(part)], axis=1)
        start("Q%dX" % b, "Q%dC" % b, "Q%dR" % b)

    def round_three(b):
        for way in "XCR":
            arrive("Q%d%s" % (b, way))
        qkv_out[b] = fin[b].astype(F32) + rqx[b].astype(F32)
        swap_out[b] = rqp[b, 0].astype(F32) + rqp[b, 1].astype(F32)

    def at_step(number, action):
        @pl.when(step == number)
        def _():
            action()

    def weights_of(b):
        lanes = slice(2 * b * LANES, 2 * (b + 1) * LANES)
        both = dot_tn(gkv_all[:, lanes], normed[...]) + far_dw[lanes, :]
        low_rows = gq_all[2 * b : 2 * b + 2].reshape(LANES, rows) * HEAD_DIM**-0.5
        low_rows = low_rows.astype(BF16)
        gq_low[b * LANES : (b + 1) * LANES, :] = low_rows
        query = dot_nn(low_rows, normed[...])
        size = HEAD_DIM
        stacked = jnp.concatenate(
            [
                query,
                both[size : 2 * size],
                both[3 * size :],
                both[:size],
                both[2 * size : 3 * size],
            ],
            axis=0,
        )
        turned = stacked.T.astype(BF16)
        if b < 2:
            wq[b] = turned.reshape(wq.shape[1:])
            start("Q%dY" % b)
        else:
            cut = aq.shape[-1]
            aq[...] = turned[:, :cut].reshape(aq.shape)
            bq[...] = turned[:, cut:].reshape(bq.shape)
            start("Q2Y", "Q2z", "Q2w", "Q2d")

    def first_step():
        barrier = pltpu.get_barrier_semaphore()
        for peer in peers.values():
            pl.semaphore_signal(barrier, inc=1, device_id=peer, device_id_type=MESH)
        pl.semaphore_wait(barrier, len(peers))
        near(0, up_in.at[0], au).start()
        near(1, down_in.at[:, :, y], ad).start()
        near(2, pair_in, ac).start()
        near(3, early_in, early_out).start()
        start("UX", "DY", "CW")
        near(4, normed_in.at[pl.ds(rows, rows)], normed).start()
        near(3, early_in, early_out).wait()

    def far_post():
        near(4, normed_in.at[pl.ds(rows, rows)], normed).wait()
        gkv_sum[...] = jnp.sum(gkv_all[...].astype(F32), axis=0, keepdims=True)
        for i in (1, 0):
            gn_far[i] = dot_nt(gkv_all[i * half : (i + 1) * half, :], wpair_ref[...]).astype(BF16)
            if i == 1:
                start("GC")
        far_dw[...] = dot_tn(gkv_all[...], normed[...])
        near(5, normed_in.at[pl.ds(0, rows)], normed).start()

    at_step(0, first_step)
    at_step(5, lambda: next_of("CW", "CY"))
    at_step(5, lambda: start("VZ"))
    at_step(7, lambda: next_of("VZ", "VW"))
    at_step(8, lambda: next_of("CY", "CX"))
    at_step(9, lambda: next_of("UX", "UY"))
    at_step(9, lambda: next_of("DY", "DZ"))
    at_step(12, far_post)
    at_step(13, lambda: next_of("GC", "GX"))
    at_step(14, lambda: next_of("UY", "UZ"))
    at_step(14, lambda: next_of("DZ", "DW"))
    at_step(16, lambda: near(5, normed_in.at[pl.ds(0, rows)], normed).wait())
    at_step(16, lambda: weights_of(0))
    at_step(17, lambda: next_of("UZ", "UW"))
    at_step(19, lambda: next_of("Q0Y", "Q0Z"))
    at_step(19, lambda: next_of("DW", "DX"))
    at_step(20, lambda: weights_of(1))
    at_step(21, lambda: next_of("Q0Z", "Q0W"))
    at_step(20, lambda: near(6, tokens_in, tokens).start())
    at_step(20, lambda: near(7, gmid_in, gmid).start())
    at_step(23, lambda: round_two(0))
    at_step(23, lambda: next_of("Q1Y", "Q1Z"))

    gkv, part = score_grads(q_t, gout_t, delta, gout_q, mass, k_ref, v_ref)
    lanes = pl.ds(pl.multiple_of(head * LANES, LANES), LANES)
    gkv_all[pl.ds(pl.multiple_of(block * tile, tile), tile), lanes] = gkv

    @pl.when(step < per_phase)
    def _():
        @pl.when(block == 0)
        def _():
            gq_all[head] = part

        @pl.when(block != 0)
        def _():
            gq_all[head] += part

    @pl.when(step >= per_phase)
    def _():
        gq_all[head] += part

    @pl.when(step == 2 * per_phase - 1)
    def _():
        weights_of(2)

        def gn_of(at):
            spot = slice(at * half, (at + 1) * half)
            return dot_nt(gkv_all[spot, :], wpair_ref[...]) + dot_tn(gq_low[:, spot], wqt_ref[...])

        gn_send[...] = gn_of(1).astype(BF16)
        start("GN")
        gn_own[...] = gn_of(0)
        gkv_now = gkv_sum[...] + jnp.sum(gkv_all[...].astype(F32), axis=0, keepdims=True)
        ones = jnp.ones((8, rows), BF16)
        gq_now = dot_nt(ones, gq_low[...])[:1]
        gq_now = jnp.concatenate([gq_now, jnp.zeros_like(gq_now)], axis=1)
        next_of("Q1Z", "Q1W")
        arrive("GN")
        exchange("GX").wait()
        near(6, tokens_in, tokens).wait()
        rows_now = tokens[...].astype(F32)
        centred = rows_now - jnp.mean(rows_now, axis=-1, keepdims=True)
        inv = lax.rsqrt(jnp.mean(centred * centred, axis=-1, keepdims=True) + EPS_NORM)
        normal = centred * inv
        gn = gn_own[...] + rg[1].astype(F32) + rg[2].astype(F32)
        zero = jnp.zeros((1, width), F32)
        mine = core == 0
        late_out[...] = jnp.concatenate(
            [
                jnp.sum(gn * normal, axis=0, keepdims=True),
                jnp.sum(gn, axis=0, keepdims=True),
                zero,
                zero,
                jnp.where(mine, gq_now, zero),
                jnp.where(mine, zero, gq_now),
                jnp.where(mine, gkv_now, zero),
                jnp.where(mine, zero, gkv_now),
            ],
            axis=0,
        )
        start("LC")
        round_two(1)
        next_of("LC", "LX")
        round_one()
        near(7, gmid_in, gmid).wait()
        turned = gn * as_row(gain_ref)
        gtok_out[...] = (
            gmid[...]
            + inv
            * (
                turned
                - jnp.mean(turned, axis=-1, keepdims=True)
                - normal * jnp.mean(turned * normal, axis=-1, keepdims=True)
            )
        ).astype(BF16)
        next_of("LX", "LY")
        round_three(0)
        round_three(1)
        arrive("UW")
        arrive("CX")
        arrive("VW")
        arrive("DX")
        round_two(2)
        next_of("LY", "LZ", "LW", "LD")
        round_three(2)
        for name in ("LZ", "LW", "LD"):
            exchange(name).wait()
        for at in range(3, 6):
            late_out[...] = late_out[...] + rl[at]


def backward(head_arrays, keys, values, sums, early, normed, tokens, gmid, gain, wpair, wqt):
    width, rows = head_arrays[0].shape
    heads = width // LANES
    half = rows // 2
    tile = half
    up, down, pair = sums
    each = up.shape[4]
    down_each, down_width = down.shape[3:]
    grid = 4 * heads
    head_of = lambda n: lax.rem(n, 2 * heads) // 2
    key_spec = pl.BlockSpec(
        (tile, LANES), lambda n: ((1 - n // (2 * heads)) * 2 + lax.rem(n, 2), head_of(n))
    )
    hbm = pl.BlockSpec(memory_space=pl.ANY)
    vmem = pl.BlockSpec(memory_space=pltpu.VMEM)
    low = lambda *s: pltpu.VMEM(s, BF16)
    full = lambda *s: pltpu.VMEM(s, F32)
    qkv_width = width // 2
    wide = qkv_width - LANES
    outs = [
        jax.ShapeDtypeStruct((each, width), F32),
        jax.ShapeDtypeStruct((down_each, down_width), F32),
        jax.ShapeDtypeStruct((each, width), F32),
        jax.ShapeDtypeStruct(early.shape, BF16),
        jax.ShapeDtypeStruct((3, each, qkv_width), F32),
        jax.ShapeDtypeStruct((3, each, LANES), F32),
        jax.ShapeDtypeStruct((8, width), F32),
        jax.ShapeDtypeStruct((half, width), BF16),
    ]
    return pl.pallas_call(
        backward_kernel,
        grid=(grid,),
        in_specs=head_specs(rows, head_of) + [key_spec, key_spec] + [hbm] * 7
        + [vmem] * 3,
        out_specs=[vmem] * len(outs),
        out_shape=outs,
        scratch_shapes=[
            full(heads, HEAD_DIM, rows),
            low(heads * HEAD_DIM, rows),
            low(rows, width),
            full(width, width),
            low(rows, width),
            low(half, width),
            full(half, width),
            low(2, half, width),
            low(half, width),
            full(half, width),
            full(1, width),
            low(2, 2, 2, each, width),
            low(2, 2, down_each, down_width),
            low(2, 2, each, width),
            low(2, 2, 2, 2, each, qkv_width),
            low(2, 2, 2, each, wide),
            low(2, 2, 2, each, LANES),
            low(3, each, qkv_width),
            low(3, 2, each, LANES),
            low(2, 2, 2, each, width),
            low(2, 2, each, width),
            low(2, each, width),
            low(each, width),
            low(2, 2, down_each, down_width),
            low(2, down_each, down_width),
            low(down_each, down_width),
            low(down_each, down_width),
            low(2, each, width),
            low(each, width),
            low(each, width),
            low(2, *early.shape),
            low(2, 2, 2, each, qkv_width),
            low(2, 2, each, qkv_width),
            low(2, each, qkv_width),
            low(2, 2, each, wide),
            low(3, each, wide),
            low(each, LANES),
            low(3, 2, each, LANES),
            low(3, each, qkv_width),
            low(3, 2, each, LANES),
            low(3, half, width),
            full(6, 8, width),
            pltpu.SemaphoreType.DMA((len(EXCHANGES),)),
            pltpu.SemaphoreType.DMA((len(EXCHANGES),)),
            pltpu.SemaphoreType.DMA((8,)),
        ],
        compiler_params=pltpu.CompilerParams(
            vmem_limit_bytes=VMEM_LIMIT, collective_id=0, has_side_effects=True
        ),
        cost_estimate=pl.CostEstimate(
            flops=40 * heads * rows * rows * LANES,
            bytes_accessed=40 * MIB,
            transcendentals=2 * heads * rows * rows,
        ),
        name="backward",
    )(*head_arrays, keys, values, up, down, pair, early, normed, tokens, gmid, gain, wpair, wqt)


def finish_kernel(
    up_ref,
    down_ref,
    pair_ref,
    early_ref,
    qkv_ref,
    swap_ref,
    late_ref,
    gtok_ref,
    classes_ref,
    class_ref,
    class_w_ref,
    up_out,
    down_out,
    wout_out,
    patch_out,
    qkv_out,
    class_w_out,
    class_out,
    gtok_out,
    gbias_up_out,
    *rest,
):
    vector_outs, product = rest[:-1], rest[-1]
    seq, grp = lax.axis_index("seq"), lax.axis_index("grp")
    core, x = lax.rem(seq, 2), seq // 2
    gtok_out[...] = gtok_ref[...]
    width = up_ref.shape[1]
    third = width // 4
    each = up_ref.shape[0]
    size = HEAD_DIM
    up_out[...] = up_ref[...]
    down_out[...] = jnp.where(x == 0, down_ref[:, :third], down_ref[:, third:]).T
    wout_out[...] = jnp.where(x == 0, pair_ref[:, :third], pair_ref[:, third : 2 * third])
    patch_out[...] = jnp.where(x == 0, pair_ref[:, 2 * third : 3 * third], pair_ref[:, 3 * third :])

    def group(j):
        parts = []
        for b in range(3):
            low = qkv_ref[b, :, j * size : (j + 1) * size]
            high = qkv_ref[b, :, (j + 3) * size : (j + 4) * size]
            parts.append(jnp.where(x == 0, low, high))
        return jnp.concatenate(parts, axis=1)

    first, second, last = group(0), group(1), group(2)
    got = jnp.concatenate([swap_ref[b, :, :size] for b in range(3)], axis=1)
    qkv_out[...] = jnp.concatenate(
        [jnp.where(core == 0, first, second), got, jnp.where(core == 0, second, last)], axis=1
    )

    classes = classes_ref[...]
    count = classes.shape[0]
    scale = lax.rsqrt(jnp.sum(classes * classes, axis=-1, keepdims=True) + EPS_UNIT)
    unit = classes * scale
    gunit = early_ref[:count, :].astype(F32)
    gclass = (scale * (gunit - unit * jnp.sum(gunit * unit, axis=-1, keepdims=True))).astype(BF16)
    product[...] = dot_tn(class_ref[...], gclass)
    block = product[pl.ds(grp * each, each), :]
    mine = block[:, :third]
    for s in range(1, 4):
        mine = jnp.where(seq == s, block[:, s * third : (s + 1) * third], mine)
    class_w_out[...] = mine

    def own_lanes(matrix, each):
        total = matrix.shape[1]
        return pltpu.roll(matrix, lax.rem(total - grp * each, total), 1)[:, :each]

    class_out[...] = own_lanes(dot_nt(gclass, class_w_ref[...]), each)
    at = early_ref.shape[0] - 16
    vectors = early_ref[at:, :].astype(F32)
    late = late_ref[...]

    def all_heads(first, second):
        parts = []
        for g in range(2):
            for vector in (first, second):
                parts += [vector[i * 2 + g] for i in range(3)]
        return jnp.concatenate(parts, axis=1)

    def lanes_of(matrix, row, stride, count):
        return [matrix[row : row + 1, i * stride : i * stride + size] for i in range(count)]

    gquery = all_heads(lanes_of(late, 4, size, 6), lanes_of(late, 5, size, 6))
    gvalue = all_heads(lanes_of(late, 6, 2 * size, 6), lanes_of(late, 7, 2 * size, 6))
    packed = jnp.concatenate(
        [vectors[:4], late[:2], gquery, gvalue], axis=0
    )
    mine = own_lanes(packed, each)
    for i, ref in enumerate(vector_outs):
        ref[...] = mine[i]
    chunks = gbias_up_out.shape[0] // each
    flat = jnp.concatenate([vectors[4 + i : 5 + i] for i in range(chunks)], axis=1)
    flat = jnp.concatenate([flat] * 8, axis=0)
    gbias_up_out[...] = own_lanes(flat, chunks * each)[0]


def finish(*operands):
    up, down, pair, early, qkv, _, late, gtok, classes, class_emb, class_w = operands
    each, width = up.shape
    third = width // 4
    hidden_each = down.shape[0]
    shapes = [
        (each, width),
        (third, hidden_each),
        (each, third),
        (each, third),
        (each, 3 * third),
        (each, third),
        (classes.shape[0], each),
        gtok.shape,
        (hidden_each,),
    ] + [(each,)] * 8
    vmem = pl.BlockSpec(memory_space=pltpu.VMEM)
    return pl.pallas_call(
        finish_kernel,
        in_specs=[vmem] * len(operands),
        out_specs=[vmem] * len(shapes),
        out_shape=[jax.ShapeDtypeStruct(s, BF16 if s == gtok.shape else F32) for s in shapes],
        scratch_shapes=[pltpu.VMEM((width, width), F32)],
        compiler_params=pltpu.CompilerParams(vmem_limit_bytes=VMEM_LIMIT),
        name="finish",
    )(*operands)


def layer_norm(matrix_rows, gain_vec, shift_vec):
    row_mean = jnp.mean(matrix_rows, axis=-1, keepdims=True)
    centred = matrix_rows - row_mean
    row_var = jnp.mean(centred * centred, axis=-1, keepdims=True)
    return centred * lax.rsqrt(row_var + EPS_NORM) * gain_vec + shift_vec


def unit_rows(matrix_rows):
    return matrix_rows * lax.rsqrt(
        jnp.sum(matrix_rows * matrix_rows, axis=-1, keepdims=True) + EPS_UNIT
    )


def column_sum(matrix_low):
    return jnp.sum(matrix_low.astype(F32), axis=0)


def swap(value, axis, bit):
    size = lax.axis_size(axis)
    return lax.ppermute(value, axis, [(i, i ^ bit) for i in range(size)])


def add_low(first, second):
    return (first.astype(F32) + second.astype(F32)).astype(BF16)


def sum_rows(part):
    groups = lax.axis_size("grp")
    bits = groups.bit_length() - 1
    here = lax.axis_index("grp")
    each = part.shape[0] // groups
    width = part.shape[1]
    part = part.reshape((2,) * bits + (each, width))
    for name in range(bits):
        axis = bits - 1 - name
        mine = (here >> name) & 1
        send = lax.dynamic_index_in_dim(part, 1 - mine, axis, keepdims=True)
        keep = lax.dynamic_index_in_dim(part, mine, axis, keepdims=True)
        part = add_low(keep, swap(send, "grp", 1 << name))
    return part.reshape(each, width)


def sum_x(part, x_here):
    half = part.shape[1] // 2
    low, high = part[:, :half], part[:, half:]
    mine = jnp.where(x_here == 0, low, high)
    other = jnp.where(x_here == 0, high, low)
    return mine.astype(F32) + swap(other, "seq", 2).astype(F32)


def body(
    tokens_in,
    lengths,
    ln1_gain,
    ln1_bias,
    w_qkv,
    bias_query,
    bias_value,
    w_out,
    bias_out,
    ln2_gain,
    ln2_bias,
    w_up,
    bias_up,
    w_down,
    bias_down,
    proj_patch,
    proj_class,
    class_emb,
    d_masks,
):
    row_count, model_width = tokens_in.shape
    head_count = model_width // HEAD_DIM
    heads_here = head_count // 2
    third = model_width // 4
    seq_devices = lax.axis_size("seq")
    grp_devices = lax.axis_size("grp")
    seq_here = lax.axis_index("seq")
    grp_here = lax.axis_index("grp")
    core = seq_here & 1
    x_here = seq_here >> 1

    tokens_x = swap(tokens_in, "seq", 2)
    normed_image, w_kv, value_bias, w_pairs, w_query_t, queries_t, gout_q, keys, values = project_near(
        lengths, tokens_in, ln1_gain, ln1_bias, w_qkv, bias_query, bias_value
    )
    partial, near_top = attend_forward(attend_near_kernel, "attend_near", queries_t, keys, values)
    tokens_x, partial = lax.optimization_barrier((tokens_x, partial))
    normed_image, keys, values = project_far(
        lengths,
        tokens_x,
        ln1_gain,
        ln1_bias,
        w_kv,
        value_bias,
        (normed_image, keys, values),
    )
    att_own, att_other, mass = attend_forward(
        attend_far_kernel, "attend_far", queries_t, keys, values, partial, near_top
    )
    (
        mask_out,
        joined,
        normed_two,
        active,
        grad_hidden,
        final_low,
        grad_patches,
        grad_feed,
        grad_branch,
        grad_branch_p,
        grad_middle,
        early,
        classes,
    ) = middle(
        lengths,
        tokens_in,
        att_own,
        att_other,
        d_masks.T,
        (
            w_out,
            bias_out,
            ln2_gain,
            ln2_bias,
            w_up,
            bias_up,
            w_down,
            bias_down,
            proj_patch,
            proj_class,
            class_emb,
        ),
    )
    fused = grp_devices == 8 and model_width % (16 * grp_devices) == 0
    up_sum, down_sum, pair_sum, early, gout_q, gouts_t, delta = (weights if fused else weights_plain)(
        gout_q,
        normed_two,
        grad_hidden,
        active,
        grad_feed,
        joined,
        grad_branch,
        grad_branch_p,
        final_low,
        grad_patches,
        w_out,
        att_own,
        att_other,
        early,
    )
    head_arrays = (queries_t, gouts_t, delta, gout_q, mass)
    down_sum = down_sum.reshape(bias_up.shape[0], model_width // 2)
    rows_each = model_width // grp_devices
    ff_each = bias_up.shape[0] // grp_devices
    cols_each = model_width // seq_devices

    if fused:
        sums = (
            up_sum.reshape(2, 2, 2, 2, rows_each, -1),
            down_sum.reshape(2, 2, 2, ff_each, -1),
            pair_sum,
        )
        raw = backward(
            head_arrays,
            keys,
            values,
            sums,
            early,
            normed_image,
            tokens_in,
            grad_middle,
            ln1_gain,
            w_pairs,
            w_query_t,
        )
        (
            out_w_up,
            out_w_down,
            out_w_out,
            out_proj_patch,
            out_w_qkv,
            grad_proj_class,
            grad_class_emb,
            grad_tokens,
            out_bias_up,
            *vectors,
        ) = finish(*raw, classes, class_emb, proj_class)
        return (
            mask_out.T,
            grad_tokens,
            vectors[4],
            vectors[5],
            out_w_qkv,
            vectors[6],
            vectors[7],
            out_w_out,
            vectors[1],
            vectors[2],
            vectors[3],
            out_w_up,
            out_bias_up,
            out_w_down.T,
            vectors[0],
            out_proj_patch,
            grad_proj_class,
            grad_class_emb,
        )

    out_w_down = sum_x(sum_rows(down_sum), x_here)
    out_w_up = sum_rows(add_low(up_sum[0], swap(up_sum[1], "seq", 2))).astype(F32)
    pair_rows = sum_rows(pair_sum)
    out_w_out = sum_x(pair_rows[:, : 2 * third], x_here)
    out_proj_patch = sum_x(pair_rows[:, 2 * third :], x_here)
    class_total = early[: class_emb.shape[0]]
    vectors = early[-16:]
    gq_t, gkv = attend_backward(*head_arrays, keys, values)

    gq = gq_t.T
    gn_far = dot_nt(gkv[2 * row_count :], w_pairs)
    gn_near = dot_nt(gkv[: 2 * row_count], w_pairs) + dot_nn(gq, w_query_t)
    far_got = swap(gn_far[row_count:].astype(BF16), "seq", 1)
    far_sum = (gn_far[:row_count] + far_got.astype(F32)).astype(BF16)
    near_got = swap(gn_near[row_count:].astype(BF16), "seq", 1)
    x_got = swap(far_sum, "seq", 2)
    grad_normed_one = gn_near[:row_count] + near_got.astype(F32) + x_got.astype(F32)
    norm_one_back = jax.vjp(layer_norm, tokens_in.astype(F32), ln1_gain, ln1_bias)[1]
    grad_tokens_norm, grad_ln1_gain, grad_ln1_bias = norm_one_back(grad_normed_one)
    grad_tokens = (grad_middle + grad_tokens_norm).astype(BF16)

    dw_q = dot_tn(normed_image[: 2 * row_count], gq).reshape(model_width, 3, 2, HEAD_DIM)
    dw_kv = dot_tn(normed_image, gkv).reshape(model_width, 3, 2, 2, HEAD_DIM)
    three = lambda matrix: matrix.reshape(model_width, third)
    part_zero = [three(dw_q[:, :, 0]), three(dw_q[:, :, 1]), three(dw_kv[:, :, 0, 1])]
    part_one = [three(dw_kv[:, :, 1, 1]), three(dw_kv[:, :, 0, 0]), three(dw_kv[:, :, 1, 0])]
    part_zero = jnp.concatenate(part_zero, axis=1).astype(BF16)
    part_one = jnp.concatenate(part_one, axis=1).astype(BF16)
    qkv_mine = jnp.where(x_here == 0, part_zero, part_one)
    qkv_other = jnp.where(x_here == 0, part_one, part_zero)
    qkv_rows = sum_rows(add_low(qkv_mine, swap(qkv_other, "seq", 2))).astype(F32)
    pieces = [qkv_rows[:, i * third : (i + 1) * third] for i in range(3)]
    piece_got = swap(jnp.where(core == 0, pieces[2], pieces[0]), "seq", 1)
    out_w_qkv = jnp.concatenate(
        [
            jnp.where(core == 0, pieces[0], pieces[1]),
            piece_got,
            jnp.where(core == 0, pieces[1], pieces[2]),
        ],
        axis=1,
    )

    def put_back(vector):
        halves = vector.reshape(3, 2, HEAD_DIM).swapaxes(0, 1).reshape(2, 1, third)
        zero = jnp.zeros_like(halves)
        both = jnp.where(
            core == 0,
            jnp.concatenate([halves, zero], axis=1),
            jnp.concatenate([zero, halves], axis=1),
        )
        return both.reshape(model_width)

    grad_bias_query = put_back(column_sum(gq))
    gkv_sums = column_sum(gkv).reshape(heads_here, 2, HEAD_DIM)
    grad_bias_value = put_back(gkv_sums[:, 0].reshape(heads_here * HEAD_DIM))
    late = jnp.stack([grad_ln1_gain, grad_ln1_bias, grad_bias_query, grad_bias_value], axis=1)
    late = jnp.concatenate([late, jnp.zeros((model_width, LANES - 4), F32)], axis=1).astype(BF16)
    late = add_low(late, swap(late, "seq", 1))
    late = sum_rows(add_low(late, swap(late, "seq", 2))).astype(F32)

    class_back = jax.vjp(unit_rows, classes)[1]
    grad_classes = class_back(class_total)[0].astype(BF16)

    def vector_rows(index):
        return lax.dynamic_slice_in_dim(vectors[index], grp_here * rows_each, rows_each, 0)

    out_bias_up = lax.dynamic_slice_in_dim(
        vectors[4 : 4 + bias_up.shape[0] // model_width].reshape(-1), grp_here * ff_each, ff_each, 0
    )
    emb_cols = lax.dynamic_slice_in_dim(class_emb, grp_here * rows_each, rows_each, 1)
    class_cols = lax.dynamic_slice_in_dim(grad_classes, seq_here * cols_each, cols_each, 1)
    grad_proj_class = dot_tn(emb_cols, class_cols)
    proj_rows = lax.dynamic_slice_in_dim(proj_class, grp_here * rows_each, rows_each, 0)
    grad_class_emb = dot_nt(grad_classes, proj_rows)
    return (
        mask_out.T,
        grad_tokens,
        late[:, 0],
        late[:, 1],
        out_w_qkv,
        late[:, 2],
        late[:, 3],
        out_w_out,
        vector_rows(1),
        vector_rows(2),
        vector_rows(3),
        out_w_up,
        out_bias_up,
        out_w_down,
        vector_rows(0),
        out_proj_patch,
        grad_proj_class,
        grad_class_emb,
    )


def solution(mesh):
    rows = P(("grp", "seq"), None)
    both = P("grp", "seq")
    return jax.shard_map(
        body,
        mesh=mesh,
        in_specs=(rows, P("grp")) + (P(),) * 16 + (rows,),
        out_specs=(
            rows,
            rows,
            P("grp"),
            P("grp"),
            both,
            P("grp"),
            P("grp"),
            both,
            P("grp"),
            P("grp"),
            P("grp"),
            both,
            P("grp"),
            both,
            P("grp"),
            both,
            both,
            P(None, "grp"),
        ),
        check_vma=False,
    )
```
